32 devices in a mesh: dp: 8 (over z, x), expert: 4 (over y, core).
Axes of the slice: x: 2, y: 2, z: 4, core: 2. Of those that a mesh axis runs over, the one named last changes fastest.
Arguments:
- tokens: bfloat16 [8192, 1536], P(('dp', 'expert')), may hold values from -6 to 6
- cotangent: bfloat16 [8192, 1536], P(('dp', 'expert')), may hold values from -6 to 6
- routes: int32 [8192, 8], P(('dp', 'expert')), may hold values from 0 to 19, all different within a row; in each aligned block of 256 rows (0 to 255, 256 to 511, ...) at most 153 rows name the same one
- segments: int32 [32, 256], P(('dp', 'expert')), may hold values from 0 to 1, never falling along the last dimension, each value on 1 to 192 neighbouring positions
- w_qkv: bfloat16 [1536, 2560], P(('dp', 'expert')), may hold values from -0.21875 to 0.21875
- w_out: bfloat16 [1536, 1536], P(('dp', 'expert')), may hold values from -0.4375 to 0.4375
- router: bfloat16 [1536, 20], P(('dp', 'expert')), may hold values from -0.078125 to 0.078125
- gain_attn: bfloat16 [1536], P(('dp', 'expert')), may hold values from 0.099609375 to 1.8984375
- gain_mlp: bfloat16 [1536], P(('dp', 'expert')), may hold values from 0.099609375 to 1.8984375
- expert_in: bfloat16 [20, 1536, 1024], P('expert'), may hold values from -0.15625 to 0.15625
- expert_out: bfloat16 [20, 512, 1536], P('expert'), may hold values from -1 to 1
Outputs:
- activations: bfloat16 [8192, 1536], P(('dp', 'expert'))
- d_tokens: float32 [8192, 1536], P(('dp', 'expert'))
- d_w_qkv: float32 [1536, 2560], P(('dp', 'expert'))
- d_w_out: float32 [1536, 1536], P(('dp', 'expert'))
- d_router: float32 [1536, 20], P(('dp', 'expert'))
- d_gain_attn: float32 [1536], P(('dp', 'expert'))
- d_gain_mlp: float32 [1536], P(('dp', 'expert'))
- d_expert_in: float32 [20, 1536, 1024], P('expert', 'dp')
- d_expert_out: float32 [20, 512, 1536], P('expert', 'dp')
The draws below stay inside these ranges and needn't reach their ends.
Inputs may be any that keep to these rules, and one draw needn't show every extreme that they name: `routes`: each row names 8 different experts. In the rows of one device (aligned blocks of 256 rows) no expert is named by more than 153 rows, a bound that some block reaches. `segments`: within a row the numbers never fall; each row holds two documents, each one run of a number of 64 to 192 positions.
All inputs are finite; a program needn't handle non-finite values.
Results may differ from the reference program's by a relative error of at most 0.017.
The reference program's roundings to bfloat16 on the way count: a program that leaves them out, or rounds other values in their place, can miss the bound.
Values may be sent and summed in bfloat16 or wider, within the bound.
No kernel may reach another device: no remote copies, remote signals or barrier semaphores. Data moves between devices by JAX's collectives and lax.ppermute only.
A program may use at most 320 MiB of HBM per device.

```python
import math
from functools import partial
import jax
import jax.numpy as jnp
import numpy as np
from jax import lax

D = 1536
H = 24
KV = 8
HD = 64
FE = 512
TOP = 8
TOK_DEV = 256
EXPERTS = 20
SEQS = 32
TOKENS = 8192
CAP = 153


def block_levels(own_key, dims, cuts, least, top_value):
    loudness, own = 1.0, jax.random.fold_in(own_key, 6)
    for dim, parts in cuts:
        draws = jnp.exp(jax.random.uniform(jax.random.fold_in(own, dim), (parts,), jnp.float32, least / len(cuts), top_value / len(cuts)))
        loudness = loudness * jnp.repeat(draws, dims[dim] // parts).reshape([-1 if axis == dim else 1 for axis in range(len(dims))])
    return loudness


def split_up(amount, total, bound, skew):
    loads = [(1 << 20) // math.isqrt(rank ** skew) + 1 for rank in range(2, amount + 1)]
    rest, counts = total - bound - (amount - 1), [1] * (amount - 1)
    while rest > 0:
        free = [i for i in range(amount - 1) if counts[i] < bound]
        whole, budget = sum([loads[i] for i in free]), rest
        for i in free:
            addition = min(bound - counts[i], max(1, budget * loads[i] // whole), rest)
            counts[i] = counts[i] + addition
            rest = rest - addition
    return np.array([bound] + counts)


def ragged_sizes(rng, amount, total, bound, slope):
    if amount == 2:
        one = jax.random.randint(rng, (), max(1, total - bound), min(bound, total - 1) + 1)
        return jnp.stack([one, total - one])
    sizes = jnp.asarray(split_up(amount, total, bound, slope), jnp.int32)
    twos = (amount - 1) // 2
    giver, sink = sizes[1:1 + 2 * twos:2], sizes[2:2 + 2 * twos:2]
    room = jnp.minimum(giver - 1, bound - sink)
    passed = jax.random.randint(jax.random.fold_in(rng, 1), (twos,), 0, 1 << 20) % (room + 1)
    sizes = sizes.at[1:1 + 2 * twos:2].set(giver - passed).at[2:2 + 2 * twos:2].set(sink + passed)
    return sizes[jax.random.permutation(jax.random.fold_in(rng, 2), amount)]


def shared_out(own_key, own, number, rows, number_of, top, bound, lean):
    sequence = jax.random.permutation(own_key, number_of)
    crowded, common = shares(number_of, rows * top, bound, lean, True), shares(number_of, rows * top, bound, lean, False)
    places = jnp.arange(number_of)

    def named(lengths, turn):
        used = int((lengths > 0).sum())
        fixed = max(1, used // 4)
        moved = fixed + (places - fixed + turn * (used - fixed)) % max(1, number_of - fixed)
        return jnp.zeros((number_of,), jnp.int32).at[sequence[jnp.where(places < fixed, places, moved)]].set(jnp.asarray(lengths, jnp.int32))

    lengths = jnp.where(number % 4 == 0, named(crowded, number // 4), named(common, number - number // 4 - 1))
    mixed = jax.random.permutation(jax.random.fold_in(own, 3), number_of)
    donor, sink = mixed[0:number_of // 2 * 2:2], mixed[1:number_of // 2 * 2:2]
    room = jnp.minimum(lengths[donor] - 1, bound - lengths[sink]) // 2
    room = jnp.where((donor == sequence[0]) | (sink == sequence[0]) | (lengths[sink] == 0), 0, jnp.maximum(room, 0))
    moved = jax.random.randint(jax.random.fold_in(own, 4), (number_of // 2,), 0, 1 << 20) % (room + 1)
    lengths = lengths.at[donor].add(-moved).at[sink].add(moved)
    items = jnp.searchsorted(jnp.cumsum(lengths), jnp.arange(rows * top), side="right").astype(jnp.int32)
    grid = items.reshape(top, rows).T
    grid = grid[jax.random.permutation(jax.random.fold_in(own, 1), rows)]
    turn = jax.random.randint(jax.random.fold_in(own, 2), (rows, 1), 0, top)
    return jnp.take_along_axis(grid, (jnp.arange(top)[None, :] + turn) % top, axis=1)


def shares(count, total, bound, slope, full):
    portions = [(1 << 20) // math.isqrt(rank ** slope) + 1 for rank in range(1, count + 1)]
    largest = bound if full else min(bound, max(-(-total // count), total * portions[0] // sum(portions)))
    least = 1 if total - largest >= count - 1 else 0
    holding, rest = [largest] + [least] * (count - 1), total - largest - least * (count - 1)
    while rest > 0:
        movable = [i for i in range(1, count) if holding[i] < largest] or [i for i in range(1, count) if holding[i] < bound]
        whole, remaining = sum([portions[i] for i in movable]), rest
        for i in movable:
            extra = min(bound - holding[i], max(1, remaining * portions[i] // whole), rest)
            holding[i] = holding[i] + extra
            rest = rest - extra
    return np.array(holding)


def centred(stream_key, shape, width, limit, shards=(), kind=jnp.bfloat16):
    level = block_levels(stream_key, shape, shards, -0.22, 0.18) if shards else 1.0
    drawn = jax.random.normal(stream_key, shape, jnp.float32) * width * level
    return jnp.minimum(jnp.maximum(drawn, -limit), limit).astype(kind)


def setup_inputs(seed: int = 0) -> dict:
    key_list = jax.random.split(jax.random.key(seed), 12)
    tokens = centred(key_list[0], (TOKENS, D), 1.0, 6.0, ((0, 32),))
    cotangent = centred(key_list[1], (TOKENS, D), 1.0, 6.0, ((0, 32),))
    routes_keys = jax.random.split(jax.random.fold_in(key_list[2], 1), TOKENS // TOK_DEV)
    routes_turns = jax.random.permutation(jax.random.fold_in(key_list[2], 3), TOKENS // TOK_DEV)
    routes = jax.vmap(lambda own, number: shared_out(jax.random.fold_in(key_list[2], 2), own, number, TOK_DEV, EXPERTS, TOP, CAP, 1))(routes_keys, routes_turns).reshape((TOKENS, TOP))
    segments = jax.vmap(lambda own: jnp.searchsorted(jnp.cumsum(ragged_sizes(own, 2, TOK_DEV, 3 * TOK_DEV // 4, 1)), jnp.arange(TOK_DEV), side="right"))(jax.random.split(key_list[3], SEQS)).reshape((SEQS, TOK_DEV)).astype(jnp.int32)
    w_qkv = centred(key_list[4], (D, (H + 2 * KV) * HD), (D // 2) ** -0.5, 0.21875, ((0, 32),))
    w_out = centred(key_list[5], (H * HD, D), (H * HD // 8) ** -0.5, 0.4375, ((0, 32),))
    router = centred(key_list[6], (D, EXPERTS), (4 * D) ** -0.5, 0.078125, ((0, 32),))
    gain_attn = jnp.clip(1.0 + 0.18 * jax.random.normal(key_list[7], (D,), jnp.float32), 0.099609375, 1.8984375).astype(jnp.bfloat16)
    gain_mlp = jnp.clip(1.0 + 0.18 * jax.random.normal(key_list[8], (D,), jnp.float32), 0.099609375, 1.8984375).astype(jnp.bfloat16)
    expert_in = centred(key_list[9], (EXPERTS, D, 2 * FE), D ** -0.5, 0.15625, ((0, 4),))
    expert_out = centred(key_list[10], (EXPERTS, FE, D), (FE // 16) ** -0.5, 1.0, ((0, 4),))
    return {"tokens": tokens, "cotangent": cotangent, "routes": routes, "segments": segments, "w_qkv": w_qkv, "w_out": w_out, "router": router, "gain_attn": gain_attn, "gain_mlp": gain_mlp, "expert_in": expert_in, "expert_out": expert_out}


EPSILON = 1e-06
THETA = 10000.0
NEGATIVE = -1e+30
HIGHEST = lax.Precision.HIGHEST

@jax.custom_vjp
def low(v):
    return lax.optimization_barrier(v.astype(jnp.bfloat16)).astype(jnp.float32)

@jax.custom_vjp
def low_back(v):
    return v

def low_keep(v):
    return (low(v), None)

def low_pass(kept, grad):
    return (grad,)

def back_keep(v):
    return (v, None)

def back_low(kept, grad):
    return (low(grad),)
low.defvjp(low_keep, low_pass)
low_back.defvjp(back_keep, back_low)

def rms_scale(values_in, gain_row):
    return values_in * lax.rsqrt(lax.optimization_barrier(jnp.mean(values_in * values_in, axis=-1, keepdims=True)) + EPSILON) * gain_row

def rope_tables(length, head_size):
    half_size = head_size // 2
    frequency = THETA ** (-(jnp.arange(half_size, dtype=jnp.float32) * 2.0) / head_size)
    angles = jnp.arange(length, dtype=jnp.float32)[:, None] * frequency[None, :]
    return (jnp.cos(angles)[:, None, :], jnp.sin(angles)[:, None, :])

def rotate(values_in, cos_table, sin_table):
    half_size = values_in.shape[-1] // 2
    first_half = values_in[..., :half_size]
    second_half = values_in[..., half_size:]
    return jnp.concatenate([first_half * cos_table - second_half * sin_table, second_half * cos_table + first_half * sin_table], axis=-1)

def slot_tables(routes_dev, experts_all, capacity):
    flat_routes = routes_dev.reshape(-1)
    choose = routes_dev.shape[1]
    onehot = (flat_routes[:, None] == jnp.arange(experts_all, dtype=jnp.int32)[None, :]).astype(jnp.int32)
    slot_rank = lax.optimization_barrier(jnp.sum((jnp.cumsum(onehot, axis=0) - onehot) * onehot, axis=1))
    slot_index = flat_routes * capacity + slot_rank
    token_of = jnp.arange(flat_routes.shape[0], dtype=jnp.int32) // choose
    slot_token = jnp.zeros((experts_all * capacity,), jnp.int32).at[slot_index].set(token_of)
    slot_used = jnp.zeros((experts_all * capacity,), jnp.int32).at[slot_index].set(1)
    return (slot_index.reshape(routes_dev.shape), slot_token, slot_used)

def layer_one(tokens_dev, segment_row, routes_dev, slot_index, slot_token, slot_used, w_qkv, w_out, router, gain_attn, gain_mlp, expert_in, expert_out):
    length = tokens_dev.shape[0]
    group_size = H // KV
    normed = low(rms_scale(tokens_dev, gain_attn))
    project = low_back(jnp.dot(normed, w_qkv, precision=HIGHEST))
    cos_table, sin_table = rope_tables(length, HD)
    queries = low(rotate(project[:, :H * HD].reshape(length, H, HD), cos_table, sin_table))
    queries = queries.reshape(length, KV, group_size, HD)
    key_rows = low(rotate(project[:, H * HD:(H + KV) * HD].reshape(length, KV, HD), cos_table, sin_table))
    values = low(project[:, (H + KV) * HD:].reshape(length, KV, HD))
    scores = low_back(jnp.einsum('tkgd,skd->kgts', queries, key_rows, precision=HIGHEST) * HD ** (-0.5))
    places = jnp.arange(length)
    allowed = (places[:, None] >= places[None, :]) & (segment_row[:, None] == segment_row[None, :])
    masked = jnp.where(allowed, scores, NEGATIVE)
    row_peak = lax.optimization_barrier(jnp.max(masked, axis=-1, keepdims=True))
    exponent = jnp.exp(masked - row_peak)
    probability = low(exponent / lax.optimization_barrier(jnp.sum(exponent, axis=-1, keepdims=True)))
    mixed_heads = jnp.einsum('kgts,skd->tkgd', probability, values, precision=HIGHEST).reshape(length, H * HD)
    mixed_heads = low(low_back(mixed_heads))
    branch = low_back(jnp.dot(mixed_heads, w_out, precision=HIGHEST))
    hidden_state = tokens_dev + branch
    normed_two = low(rms_scale(hidden_state, gain_mlp))
    logits = low_back(jnp.dot(normed_two, router, precision=HIGHEST))
    chosen = jnp.take_along_axis(logits, routes_dev, axis=1)
    top_logit = lax.optimization_barrier(jnp.max(chosen, axis=-1, keepdims=True))
    gate_exp = jnp.exp(chosen - top_logit)
    gate_values = low(low_back(gate_exp / lax.optimization_barrier(jnp.sum(gate_exp, axis=-1, keepdims=True))))
    slot_rows = jnp.where(slot_used[:, None] > 0, normed_two[slot_token], 0.0)
    slot_rows = low_back(slot_rows).reshape(EXPERTS, CAP, D)
    pre_act = low_back(jnp.einsum('ecd,edf->ecf', slot_rows, expert_in, precision=HIGHEST))
    gate_part = pre_act[..., :FE]
    activated = low(gate_part * jax.nn.sigmoid(gate_part) * pre_act[..., FE:])
    result_rows = low(low_back(jnp.einsum('ecf,efd->ecd', activated, expert_out, precision=HIGHEST)))
    picked = result_rows.reshape(EXPERTS * CAP, D)[slot_index]
    mixture = lax.optimization_barrier(jnp.sum(gate_values[:, :, None] * picked, axis=1))
    return hidden_state + mixture

def reference(tokens, cotangent, routes, segments, w_qkv, w_out, router, gain_attn, gain_mlp, expert_in, expert_out):
    seq_count = segments.shape[0]
    routes_dev = routes.reshape(seq_count, -1, TOP)
    slot_index, slot_token, slot_used = jax.vmap(partial(slot_tables, experts_all=EXPERTS, capacity=CAP))(routes_dev)
    tokens_dev = tokens.astype(jnp.float32).reshape(seq_count, -1, D)
    weights = tuple((item.astype(jnp.float32) for item in (w_qkv, w_out, router, gain_attn, gain_mlp, expert_in, expert_out)))

    def forward(inputs, *params):

        def single(pieces):
            return layer_one(*pieces, *params)
        return lax.map(jax.checkpoint(single), (inputs, segments, routes_dev, slot_index, slot_token, slot_used))
    outputs, pullback = jax.vjp(forward, tokens_dev, *weights)
    gradients = pullback(cotangent.astype(jnp.float32).reshape(outputs.shape))
    return (outputs.reshape(-1, D).astype(jnp.bfloat16), gradients[0].reshape(-1, D), gradients[1], gradients[2], gradients[3], gradients[4], gradients[5], gradients[6], gradients[7])
```

```python
import jax
import jax.numpy as jnp
from jax import lax
from jax.sharding import PartitionSpec as P

H = 24
KV = 8
HD = 64
FE = 512
TOP = 8

EPSILON = 1e-06
THETA = 10000.0
NEGATIVE = -1e30
AXES = ("dp", "expert")
CORE, WIDE = 1, 2
LANES = 128

F32 = jnp.float32
BF16 = jnp.bfloat16


def rope_tables(length, head_size):
    half_size = head_size // 2
    frequency = THETA ** (-(jnp.arange(half_size, dtype=jnp.float32) * 2.0) / head_size)
    angles = jnp.arange(length, dtype=jnp.float32)[:, None] * frequency[None, :]
    return (jnp.cos(angles)[:, None, :], jnp.sin(angles)[:, None, :])


def rotate(values_in, cos_table, sin_table):
    half_size = values_in.shape[-1] // 2
    first_half = values_in[..., :half_size]
    second_half = values_in[..., half_size:]
    return jnp.concatenate(
        [
            first_half * cos_table - second_half * sin_table,
            second_half * cos_table + first_half * sin_table,
        ],
        axis=-1,
    )


def norm_back(grad_normed, normed_plain, recip_row, gain_row):
    scaled = grad_normed * gain_row
    gain_grad = jnp.sum(grad_normed * normed_plain, axis=0)
    back_part = recip_row * (
        scaled - normed_plain * jnp.mean(scaled * normed_plain, axis=-1, keepdims=True)
    )
    return (back_part, gain_grad)


def dot(left, right, dims):
    return lax.dot_general(left, right, (dims, ((), ())), preferred_element_type=F32)


class Net:
    def __init__(self):
        self.nd = lax.axis_size("dp")
        self.ne = lax.axis_size("expert")
        self.p = lax.axis_index("dp")
        self.e = lax.axis_index("expert")
        self.r = self.place_of(self.p)
        order = list(range(0, self.nd, 2)) + list(range(1, self.nd, 2))[::-1]
        nd, ne = self.nd, self.ne
        self.ring = {
            way: [
                (order[i] * ne + e, order[(i + way) % nd] * ne + e)
                for i in range(nd)
                for e in range(ne)
            ]
            for way in (1, -1)
        }
        self.pair = {
            bit: [(p * ne + e, p * ne + (e ^ bit)) for p in range(nd) for e in range(ne)]
            for bit in (CORE, WIDE)
        }

    def place_of(self, p):
        return jnp.where(p % 2 == 0, p // 2, self.nd - 1 - p // 2)

    def dp_of(self, r):
        r = r % self.nd
        return jnp.where(r < self.nd // 2, 2 * r, 2 * (self.nd - 1 - r) + 1)

    def step(self, value, way):
        return lax.ppermute(value, AXES, self.ring[way])

    def swap(self, value, bit):
        return lax.ppermute(value, AXES, self.pair[bit])


def gather_weight(net, block):
    rows, columns = block.shape
    half = net.nd // 2
    own = jnp.stack([block, net.swap(block, WIDE)])
    parts = {0: own}
    ahead, back = own, own
    for s in range(1, half):
        ahead = net.step(ahead, 1)
        back = net.step(back, -1)
        parts[-s] = ahead
        parts[s] = back
    parts[half] = jnp.stack([net.step(ahead[0], 1), net.step(back[1], -1)])
    full = jnp.zeros((net.nd, net.ne, rows, columns), block.dtype)
    core, wide = net.e % 2, net.e // 2
    for offset, mine in parts.items():
        other = net.swap(mine, CORE)
        low = jnp.where(core == 0, mine, other)
        high = jnp.where(core == 0, other, mine)
        both = jnp.stack([low, high], axis=1)
        both = jnp.where(wide == 0, both, both[::-1]).reshape(net.ne, rows, columns)
        full = lax.dynamic_update_slice(full, both[None], (net.dp_of(net.r + offset), 0, 0, 0))
    return full.reshape(net.nd * net.ne * rows, columns)


def gather_rows(net, value):
    across = net.swap(value, WIDE)
    return jnp.concatenate([value, net.swap(value, CORE), across, net.swap(across, CORE)], axis=0)


def return_rows(net, partial):
    own, beside, across, corner = jnp.split(partial, 4, axis=0)
    sent = jnp.concatenate([beside, corner], axis=0).astype(BF16)
    came_beside, came_corner = jnp.split(net.swap(sent, CORE), 2, axis=0)
    onward = (across + came_corner.astype(F32)).astype(BF16)
    came = net.swap(onward, WIDE)
    return own + came_beside.astype(F32) + came.astype(F32)


def ring_sum(net, make, way):
    came = None
    for s in range(net.nd - 1):
        came = net.step(make(net.dp_of(net.r - way * (1 + s)), came).astype(BF16), way)
    return make(net.p, came)


def plus(value, came):
    return value if came is None else value + came.astype(F32)


def scatter_weight(net, left, right):
    depth = left.shape[1]
    rows = depth // (net.nd * net.ne)
    columns = right.shape[1]
    core, wide = net.e % 2, net.e // 2
    blocks = left.T.reshape(net.nd, net.ne // 2, 2, rows, left.shape[0])

    def product(which):
        some = lax.dynamic_index_in_dim(blocks, which, 2, keepdims=False)
        some = some.reshape(depth // 2, left.shape[0])
        return dot(some, right, ((1,), (0,)))

    came = net.swap(product(1 - core).astype(BF16), CORE)
    first = (product(core) + came.astype(F32)).reshape(net.nd, 2, rows, columns)
    sent = lax.dynamic_index_in_dim(first, 1 - wide, 1, keepdims=False).astype(BF16)
    kept = lax.dynamic_index_in_dim(first, wide, 1, keepdims=False)
    second = kept + net.swap(sent, WIDE).astype(F32)
    half = columns // 2

    def way_sum(way, low, high):
        def make(place, came):
            mine = lax.dynamic_index_in_dim(second[:, :, low:high], place, 0, keepdims=False)
            return plus(mine, came)

        return ring_sum(net, make, way)

    return jnp.concatenate([way_sum(1, 0, half), way_sum(-1, half, columns)], axis=1)


def on_device(
    tokens,
    cotangent,
    routes,
    segments,
    w_qkv,
    w_out,
    router,
    gain_attn,
    gain_mlp,
    expert_in,
    expert_out,
):
    net = Net()
    length, width = tokens.shape
    local_count = expert_in.shape[0]
    experts_all = local_count * net.ne
    group_size = H // KV
    score_scale = HD ** (-0.5)
    wide_qkv = w_qkv.shape[1]

    small = jnp.concatenate([router, gain_attn[:, None], gain_mlp[:, None]], axis=1)
    small = jnp.pad(small, ((0, 0), (0, LANES - small.shape[1])))
    first_full = gather_weight(net, jnp.concatenate([w_qkv, small], axis=1))
    out_full = gather_weight(net, w_out)
    qkv_full = first_full[:, :wide_qkv]
    router_full = first_full[:, wide_qkv : wide_qkv + experts_all]
    gains = first_full[:, wide_qkv + experts_all : wide_qkv + experts_all + 2].T.astype(F32)
    gain_one, gain_two = gains[0], gains[1]

    upstream_all = gather_rows(net, cotangent)
    grad_act_plain = jnp.einsum("td,efd->etf", upstream_all, expert_out, preferred_element_type=F32)

    inputs = tokens.astype(F32)
    recip_one = lax.rsqrt(jnp.mean(inputs * inputs, axis=-1, keepdims=True) + EPSILON)
    plain_one = inputs * recip_one
    normed = (plain_one * gain_one).astype(BF16)
    project = jnp.dot(normed, qkv_full, preferred_element_type=F32)
    cos_table, sin_table = rope_tables(length, HD)
    queries = rotate(project[:, : H * HD].reshape(length, H, HD), cos_table, sin_table).astype(BF16)
    queries = queries.reshape(length, KV, group_size, HD)
    key_rows = rotate(
        project[:, H * HD : (H + KV) * HD].reshape(length, KV, HD), cos_table, sin_table
    ).astype(BF16)
    values = project[:, (H + KV) * HD :].reshape(length, KV, HD).astype(BF16)
    segment_row = segments[0]
    places = jnp.arange(length)
    allowed = (places[:, None] >= places[None, :]) & (segment_row[:, None] == segment_row[None, :])

    raw_scores = (
        jnp.einsum("tkgd,skd->kgts", queries, key_rows, preferred_element_type=F32) * score_scale
    )
    masked = jnp.where(allowed, raw_scores, NEGATIVE)
    row_peak = jnp.max(masked, axis=-1, keepdims=True)
    exponent = jnp.exp(masked - row_peak)
    prob_float = exponent / jnp.sum(exponent, axis=-1, keepdims=True)
    probability = prob_float.astype(BF16)
    mixed_heads = jnp.einsum("kgts,skd->tkgd", probability, values, preferred_element_type=F32)
    mixed_heads = mixed_heads.reshape(length, H * HD).astype(BF16)
    hidden_state = inputs + jnp.dot(mixed_heads, out_full, preferred_element_type=F32)
    recip_two = lax.rsqrt(jnp.mean(hidden_state * hidden_state, axis=-1, keepdims=True) + EPSILON)
    plain_two = hidden_state * recip_two
    normed_two = (plain_two * gain_two).astype(BF16)
    logits = jnp.dot(normed_two, router_full, preferred_element_type=F32)
    expert_ids = jnp.arange(experts_all, dtype=jnp.int32)
    chosen = jnp.any(routes[:, :, None] == expert_ids[None, None, :], axis=1)
    picked = jnp.where(chosen, logits, NEGATIVE)
    gate_exp = jnp.where(chosen, jnp.exp(picked - jnp.max(picked, axis=-1, keepdims=True)), 0.0)
    gate_float = gate_exp / jnp.sum(gate_exp, axis=-1, keepdims=True)
    gate_values = gate_float.astype(BF16)

    sent = jnp.concatenate(
        [normed_two, jnp.pad(gate_values, ((0, 0), (0, LANES - experts_all)))], axis=1
    )
    arrived = gather_rows(net, sent)
    rows_all = arrived[:, :width]
    gates = lax.dynamic_slice_in_dim(
        arrived[:, width : width + experts_all], net.e * local_count, local_count, axis=1
    )
    gates = gates.T.astype(F32)[:, :, None]
    gate_part = jnp.einsum("td,edf->etf", rows_all, expert_in[..., :FE], preferred_element_type=F32)
    up_part = jnp.einsum("td,edf->etf", rows_all, expert_in[..., FE:], preferred_element_type=F32)
    sigmoid_gate = jax.nn.sigmoid(gate_part)
    silu_gate = gate_part * sigmoid_gate
    act_float = silu_gate * up_part
    activated = (act_float * gates).astype(BF16)
    gate_grads = jnp.sum(act_float * grad_act_plain, axis=-1).T
    grad_act = grad_act_plain * gates
    grad_pre = jnp.concatenate(
        [
            grad_act * up_part * sigmoid_gate * (1.0 + gate_part * (1.0 - sigmoid_gate)),
            grad_act * silu_gate,
        ],
        axis=-1,
    ).astype(BF16)

    rows_turned = rows_all.T
    act_turned = jnp.swapaxes(activated, 1, 2)
    slice_in = width // net.nd
    slice_out = FE // net.nd
    tokens_all = rows_all.shape[0]

    def in_share(low, high):
        def make(place, came):
            some = lax.dynamic_slice_in_dim(rows_turned, place * slice_in, slice_in, axis=0)
            return plus(
                jnp.einsum("dt,etf->edf", some, grad_pre[..., low:high], preferred_element_type=F32),
                came,
            )

        return make

    def out_share(low, high):
        def make(place, came):
            some = lax.dynamic_slice_in_dim(act_turned, place * slice_out, slice_out, axis=1)
            some = some.reshape(local_count * slice_out, tokens_all)
            return plus(
                dot(some, upstream_all[:, low:high], ((1,), (0,))),
                came,
            )

        return make

    d_expert_out = jnp.concatenate(
        [
            ring_sum(net, out_share(0, width // 2), 1),
            ring_sum(net, out_share(width // 2, width), -1),
        ],
        axis=-1,
    ).reshape(local_count, slice_out, width)
    d_expert_in = jnp.concatenate(
        [ring_sum(net, in_share(0, FE), 1), ring_sum(net, in_share(FE, 2 * FE), -1)], axis=-1
    )

    grad_rows = jnp.einsum("etf,edf->td", grad_pre, expert_in, preferred_element_type=F32)
    spread = jnp.zeros((tokens_all, LANES), F32)
    spread = lax.dynamic_update_slice(spread, gate_grads, (0, net.e * local_count))
    returned = return_rows(net, jnp.concatenate([grad_rows, spread], axis=1))
    mixture = return_rows(
        net, jnp.einsum("etf,efd->td", activated, expert_out, preferred_element_type=F32)
    )
    activations = (hidden_state + mixture).astype(BF16)

    upstream_grad = cotangent.astype(F32)
    grad_normed_two = returned[:, :width]
    gate_grads = returned[:, width : width + experts_all].astype(BF16).astype(F32)
    centered = gate_grads - jnp.sum(gate_float * gate_grads, axis=-1, keepdims=True)
    logit_grad = (gate_float * centered).astype(BF16)
    grad_normed_two = grad_normed_two + dot(logit_grad, router_full, ((1,), (1,)))
    back_two, d_gain_second = norm_back(grad_normed_two, plain_two, recip_two, gain_two)
    grad_hidden = upstream_grad + back_two
    grad_branch = grad_hidden.astype(BF16)
    grad_mixed = dot(grad_branch, out_full, ((1,), (1,))).astype(BF16)
    grad_mixed = grad_mixed.reshape(length, KV, group_size, HD)

    grad_values = jnp.einsum("kgts,tkgd->skd", probability, grad_mixed, preferred_element_type=F32)
    grad_probs = jnp.einsum("tkgd,skd->kgts", grad_mixed, values, preferred_element_type=F32)
    delta_row = jnp.sum(prob_float * grad_probs, axis=-1, keepdims=True)
    grad_scores = (prob_float * (grad_probs - delta_row)).astype(BF16)
    grad_queries = (
        jnp.einsum("kgts,skd->tkgd", grad_scores, key_rows, preferred_element_type=F32)
        * score_scale
    )
    grad_keys = (
        jnp.einsum("kgts,tkgd->skd", grad_scores, queries, preferred_element_type=F32) * score_scale
    )
    grad_queries = rotate(grad_queries.reshape(length, H, HD), cos_table, -sin_table)
    grad_keys = rotate(grad_keys, cos_table, -sin_table)
    grad_project = jnp.concatenate(
        [
            grad_queries.reshape(length, H * HD),
            grad_keys.reshape(length, KV * HD),
            grad_values.reshape(length, KV * HD),
        ],
        axis=1,
    ).astype(BF16)
    grad_normed = dot(grad_project, qkv_full, ((1,), (1,)))
    back_one, d_gain_first = norm_back(grad_normed, plain_one, recip_one, gain_one)
    grad_tokens = grad_hidden + back_one

    d_qkv = scatter_weight(net, normed, grad_project)
    d_out = scatter_weight(net, mixed_heads, grad_branch)
    d_small_local = jnp.concatenate(
        [dot(normed_two, logit_grad, ((0,), (0,))), d_gain_first[:, None], d_gain_second[:, None]],
        axis=1,
    )
    d_small = lax.psum_scatter(d_small_local, AXES, scatter_dimension=0, tiled=True)
    return (
        activations,
        grad_tokens,
        d_qkv,
        d_out,
        d_small[:, :experts_all],
        d_small[:, experts_all],
        d_small[:, experts_all + 1],
        d_expert_in,
        d_expert_out,
    )


def solution(mesh):
    rows = P(AXES, None)
    return jax.shard_map(
        on_device,
        mesh=mesh,
        in_specs=(rows,) * 7
        + (P(AXES), P(AXES), P("expert", None, None), P("expert", None, None)),
        out_specs=(rows,) * 5
        + (P(AXES), P(AXES), P("expert", "dp", None), P("expert", "dp", None)),
        check_vma=False,
    )
```

```python
import functools

import jax
import jax.numpy as jnp
from jax import lax
from jax.experimental import pallas as pl
from jax.experimental.pallas import tpu as pltpu
from jax.sharding import PartitionSpec as P

H = 24
KV = 8
HD = 64
FE = 512
TOP = 8

EPSILON = 1e-06
THETA = 10000.0
NEGATIVE = -1e30
AXES = ("dp", "expert")
CORE, WIDE = 1, 2
LANES = 128

F32 = jnp.float32
BF16 = jnp.bfloat16


def rope_tables(length):
    half_size = HD // 2
    frequency = THETA ** (-(jnp.arange(half_size, dtype=F32) * 2.0) / HD)
    angles = jnp.arange(length, dtype=F32)[:, None] * frequency[None, :]
    cos, sin = jnp.cos(angles), jnp.sin(angles)
    return (
        jnp.concatenate([cos] * (LANES // half_size), axis=1),
        jnp.concatenate([-sin, sin] * (LANES // HD), axis=1),
    )


def rotate_tile(tile, cos, sin):
    half_size = HD // 2
    lane = lax.broadcasted_iota(jnp.int32, tile.shape, 1)
    ahead = pltpu.roll(tile, LANES - half_size, 1)
    back = pltpu.roll(tile, half_size, 1)
    return tile * cos + jnp.where(lane % HD < half_size, ahead, back) * sin


def dot(left, right, dims=((1,), (0,))):
    return lax.dot_general(left, right, (dims, ((), ())), preferred_element_type=F32)


NT = ((1,), (1,))


def spread_row(row, lane, count):
    at = lax.broadcasted_iota(jnp.int32, (count, row.shape[1]), 0) == lane
    return jnp.where(at, jnp.broadcast_to(row, at.shape), 0.0).T


def call(kernel, out_shape, scratch=(), limit=40, name=None, specs=None, aliases=None):
    vmem = pl.BlockSpec(memory_space=pltpu.VMEM)
    return pl.pallas_call(
        kernel,
        out_shape=out_shape,
        in_specs=specs,
        out_specs=jax.tree.map(lambda _: vmem, out_shape),
        scratch_shapes=scratch,
        compiler_params=pltpu.CompilerParams(vmem_limit_bytes=limit * 2**20),
        cost_estimate=pl.CostEstimate(flops=1024, bytes_accessed=1024, transcendentals=0),
        name=name,
    )


VMEM_SPEC = pl.BlockSpec(memory_space=pltpu.VMEM)
ANY_SPEC = pl.BlockSpec(memory_space=pl.ANY)


def heads_of(array, group):
    size = H // KV
    first = group * size
    return jnp.concatenate(
        [array[:, h * HD : (h + 1) * HD] for h in range(first, first + size)], axis=0
    )


def group_softmax(queries, keys, bias):
    scores = dot(keys, queries, NT) * HD ** (-0.5)
    scores = jnp.where(bias > 0.0, scores, NEGATIVE)
    exponent = jnp.exp(scores - jnp.max(scores, axis=0, keepdims=True))
    return exponent * (1.0 / jnp.sum(exponent, axis=0, keepdims=True))


def attend_kernel(
    experts_all,
    tokens,
    bias,
    cos,
    sin,
    weight,
    normed,
    normed_turned,
    queries,
    key_rows,
    values,
    mixed,
    gains,
    project,
    held,
    sems,
):
    columns = weight.shape[1]
    wide = columns - LANES
    tile = held.shape[1] // sems.shape[0]
    copies = [
        pltpu.make_async_copy(
            weight.at[:, pl.ds(c * tile, tile)], held.at[:, pl.ds(c * tile, tile)], sems.at[c]
        )
        for c in range(sems.shape[0])
    ]
    for copy in copies[::-1]:
        copy.start()
    x = tokens[...].astype(F32)
    plain = x * lax.rsqrt(jnp.mean(x * x, axis=-1, keepdims=True) + EPSILON)
    copies[-1].wait()
    turned = held[:, wide:].astype(F32).T
    gains[...] = turned[experts_all // 8 * 8 : experts_all // 8 * 8 + 16]
    row = experts_all
    low = (plain * turned[row : row + 1]).astype(BF16)
    normed[...] = low
    normed_turned[...] = low.T
    for c in range(sems.shape[0] - 1, -1, -1):
        if c < sems.shape[0] - 1:
            copies[c].wait()
        at = slice(c * tile, (c + 1) * tile)
        project[:, at] = dot(low, held[:, at])
    c, s = cos[...], sin[...]
    for t in range(H * HD // LANES):
        at = slice(t * LANES, (t + 1) * LANES)
        queries[:, at] = rotate_tile(project[:, at], c, s).astype(BF16)
    for t in range(KV * HD // LANES):
        at = slice(t * LANES, (t + 1) * LANES)
        from_ = slice(H * HD + t * LANES, H * HD + (t + 1) * LANES)
        key_rows[:, at] = rotate_tile(project[:, from_], c, s).astype(BF16)
    values[...] = project[:, (H + KV) * HD : (H + 2 * KV) * HD].astype(BF16)
    size = H // KV
    length = tokens.shape[0]
    wide_bias = jnp.concatenate([bias[...]] * size, axis=1)
    for g in range(KV):
        at = slice(g * HD, (g + 1) * HD)
        probs = group_softmax(heads_of(queries, g), key_rows[:, at], wide_bias).astype(BF16)
        out = dot(values[:, at].T, probs)
        for j in range(size):
            h = g * size + j
            mixed[:, h * HD : (h + 1) * HD] = (
                out[:, j * length : (j + 1) * length].T.astype(BF16)
            )


def attend(experts_all, tokens, bias, cos, sin, weight):
    length, width = tokens.shape
    columns = weight.shape[1]
    shape = lambda *dims, kind=BF16: jax.ShapeDtypeStruct(dims, kind)
    out_shape = [
        shape(length, width),
        shape(width, length),
        shape(length, H * HD),
        shape(length, KV * HD),
        shape(length, KV * HD),
        shape(length, H * HD),
        shape(16, width, kind=F32),
    ]
    scratch = [
        pltpu.VMEM((length, columns), F32),
        pltpu.VMEM((width, columns), BF16),
        pltpu.SemaphoreType.DMA((7,)),
    ]
    return call(
        functools.partial(attend_kernel, experts_all),
        out_shape,
        scratch,
        limit=30,
        name="attend",
        specs=[VMEM_SPEC] * 4 + [ANY_SPEC],
    )(tokens, bias, cos, sin, weight)


def branch_kernel(
    gain_row,
    tokens,
    mixed,
    weight,
    small,
    gains,
    routes,
    hidden,
    sent,
    normed_turned,
    gate_float,
):
    width = tokens.shape[1]
    state = tokens[...].astype(F32) + dot(mixed[...], weight[...])
    hidden[...] = state
    recip = lax.rsqrt(jnp.mean(state * state, axis=-1, keepdims=True) + EPSILON)
    low = (state * recip * gains[gain_row : gain_row + 1, :]).astype(BF16)
    sent[:, :width] = low
    normed_turned[...] = low.T
    logits = dot(low, small[...])
    lanes = lax.broadcasted_iota(jnp.int32, logits.shape, 1)
    chosen = lanes < 0
    for j in range(routes.shape[1]):
        chosen = chosen | (lanes == routes[:, j : j + 1])
    picked = jnp.where(chosen, logits, NEGATIVE)
    exponent = jnp.where(chosen, jnp.exp(picked - jnp.max(picked, axis=-1, keepdims=True)), 0.0)
    gate = exponent / jnp.sum(exponent, axis=-1, keepdims=True)
    gate_float[...] = gate
    sent[:, width:] = gate.astype(BF16)


def branch(gain_row, tokens, mixed, weight, small, gains, routes):
    length, width = tokens.shape
    shape = lambda *dims, kind=BF16: jax.ShapeDtypeStruct(dims, kind)
    return call(
        functools.partial(branch_kernel, gain_row),
        [
            shape(length, width, kind=F32),
            shape(length, width + LANES),
            shape(width, length),
            shape(length, LANES, kind=F32),
        ],
        limit=20,
        name="branch",
        specs=[VMEM_SPEC] * 6,
    )(tokens, mixed, weight, small, gains, routes)


def owner_rows_kernel(extra_given, blocks, *refs):
    refs = refs[1:]
    left, weight = refs[:blocks], refs[blocks]
    extra = refs[blocks + 1 : 2 * blocks + 1] if extra_given else None
    out, total = refs[-2:]
    expert = pl.program_id(0)
    count = left[0].shape[1]
    width = total.shape[1]
    dims = NT if extra_given else ((1,), (0,))
    share = dot(jnp.concatenate([a[0] for a in left], axis=0), weight[0], dims)

    @pl.when(expert == 0)
    def _():
        total[...] = share

    @pl.when(expert > 0)
    def _():
        total[...] += share

    @pl.when(expert == pl.num_programs(0) - 1)
    def _():
        out[:, :width] = total[...].astype(BF16)
        if extra_given:
            for i in range(blocks):
                out[i * count : (i + 1) * count, width:] = extra[i][...].astype(BF16)


def owner_rows(devices, left, weight, extra=None):
    blocks = devices.shape[0]
    local, rows, inner = left.shape
    width = weight.shape[1] if extra is not None else weight.shape[2]
    columns = width if extra is None else width + LANES
    count = rows // 4
    out_shape = jax.ShapeDtypeStruct((blocks * count, columns), BF16)
    piece = lambda k: pl.BlockSpec((1, count, inner), lambda i, d: (i, d[k], 0))
    in_specs = [piece(k) for k in range(blocks)]
    in_specs.append(pl.BlockSpec((1,) + weight.shape[1:], lambda i, d: (i, 0, 0)))
    operands = [left] * blocks + [weight]
    if extra is not None:
        more = lambda k: pl.BlockSpec((count, LANES), lambda i, d: (d[k], 0))
        in_specs += [more(k) for k in range(blocks)]
        operands += [extra] * blocks
    return pl.pallas_call(
        functools.partial(owner_rows_kernel, extra is not None, blocks),
        out_shape=out_shape,
        grid_spec=pltpu.PrefetchScalarGridSpec(
            num_scalar_prefetch=1,
            grid=(local,),
            in_specs=in_specs,
            out_specs=pl.BlockSpec(out_shape.shape, lambda i, d: (0, 0)),
            scratch_shapes=[pltpu.VMEM((blocks * count, width), F32)],
        ),
        compiler_params=pltpu.CompilerParams(vmem_limit_bytes=30 * 2**20),
        cost_estimate=pl.CostEstimate(flops=1024, bytes_accessed=1024, transcendentals=0),
        name="owner_rows",
    )(devices.astype(jnp.int32), *operands)


def middle_kernel(
    experts_all,
    gain_row,
    kept,
    beside,
    came,
    cotangent,
    hidden,
    gate_float,
    normed_turned,
    gains,
    small,
    weight,
    grad_hidden,
    grad_branch,
    grad_mixed,
    extra,
):
    count, width = cotangent.shape
    total = kept[:count].astype(F32) + beside[:count].astype(F32) + came[...].astype(F32)
    gate = gate_float[...]
    gate_grad = total[:, width:].astype(BF16).astype(F32)
    centered = gate_grad - jnp.sum(gate * gate_grad, axis=-1, keepdims=True)
    logit_grad = (gate * centered).astype(BF16)
    grad_normed = total[:, :width] + dot(logit_grad, small[...], NT)
    state = hidden[...]
    recip = lax.rsqrt(jnp.mean(state * state, axis=-1, keepdims=True) + EPSILON)
    plain = state * recip
    scaled = grad_normed * gains[gain_row : gain_row + 1, :]
    gain_grad = jnp.sum(grad_normed * plain, axis=0, keepdims=True)
    back = recip * (scaled - plain * jnp.mean(scaled * plain, axis=-1, keepdims=True))
    grad = cotangent[...].astype(F32) + back
    grad_hidden[...] = grad
    low = grad.astype(BF16)
    grad_branch[...] = low
    grad_mixed[...] = dot(low, weight[...], NT).astype(BF16)
    extra[...] = dot(normed_turned[...], logit_grad) + spread_row(gain_grad, experts_all, LANES)


def attend_back_kernel(
    gain_row,
    tokens,
    queries,
    key_rows,
    values,
    grad_mixed,
    bias,
    cos,
    sin,
    gains,
    grad_hidden,
    weight,
    grad_project,
    grad_tokens,
    extra,
    project,
    held,
    sem,
):
    columns = grad_project.shape[1]
    copy = pltpu.make_async_copy(weight.at[:, pl.ds(0, columns)], held, sem)
    copy.start()
    size = H // KV
    length = tokens.shape[0]
    scale = HD ** (-0.5)
    wide_bias = jnp.concatenate([bias[...]] * size, axis=1)
    for g in range(KV):
        at = slice(g * HD, (g + 1) * HD)
        q, k, v = heads_of(queries, g), key_rows[:, at], values[:, at]
        upstream = heads_of(grad_mixed, g)
        weights = group_softmax(q, k, wide_bias)
        grad_values = dot(weights.astype(BF16), upstream)
        grad_probs = dot(v, upstream, NT)
        delta = jnp.sum(weights * grad_probs, axis=0, keepdims=True)
        grad_scores = (weights * (grad_probs - delta)).astype(BF16)
        grad_keys = dot(grad_scores, q) * scale
        grad_queries = dot(k.T, grad_scores) * scale
        for j in range(size):
            h = g * size + j
            project[:, h * HD : (h + 1) * HD] = grad_queries[:, j * length : (j + 1) * length].T
        project[:, (H + g) * HD : (H + g + 1) * HD] = grad_keys
        project[:, (H + KV + g) * HD : (H + KV + g + 1) * HD] = grad_values
    c, s = cos[...], -sin[...]
    turns = (H + KV) * HD // LANES
    for t in range(turns):
        at = slice(t * LANES, (t + 1) * LANES)
        grad_project[:, at] = rotate_tile(project[:, at], c, s).astype(BF16)
    rest = slice(turns * LANES, columns)
    grad_project[:, rest] = project[:, rest].astype(BF16)
    copy.wait()
    grad_normed = dot(grad_project[...], held[...], NT)
    x = tokens[...].astype(F32)
    recip = lax.rsqrt(jnp.mean(x * x, axis=-1, keepdims=True) + EPSILON)
    plain = x * recip
    scaled = grad_normed * gains[gain_row : gain_row + 1, :]
    gain_grad = jnp.sum(grad_normed * plain, axis=0, keepdims=True)
    back = recip * (scaled - plain * jnp.mean(scaled * plain, axis=-1, keepdims=True))
    grad_tokens[...] = grad_hidden[...] + back
    extra[...] = spread_row(gain_grad, 0, LANES)


def middle(experts_all, gain_row, *operands):
    count, width = operands[3].shape
    shape = lambda *dims, kind=BF16: jax.ShapeDtypeStruct(dims, kind)
    return call(
        functools.partial(middle_kernel, experts_all, gain_row),
        [
            shape(count, width, kind=F32),
            shape(count, width),
            shape(count, width),
            shape(width, LANES, kind=F32),
        ],
        limit=24,
        name="middle",
        specs=[VMEM_SPEC] * 10,
    )(*operands)


def attend_back(gain_row, *operands):
    length, width = operands[0].shape
    columns = (H + 2 * KV) * HD
    shape = lambda *dims, kind=BF16: jax.ShapeDtypeStruct(dims, kind)
    return call(
        functools.partial(attend_back_kernel, gain_row),
        [
            shape(length, columns),
            shape(length, width, kind=F32),
            shape(width, LANES, kind=F32),
        ],
        [
            pltpu.VMEM((length, columns), F32),
            pltpu.VMEM((width, columns), BF16),
            pltpu.SemaphoreType.DMA,
        ],
        limit=32,
        name="attend_back",
        specs=[VMEM_SPEC] * 10 + [ANY_SPEC],
    )(*operands)


def after(value, *earlier):
    return lax.optimization_barrier((value, earlier))[0]


class Net:
    def __init__(self):
        self.nd = lax.axis_size("dp")
        self.ne = lax.axis_size("expert")
        self.p = lax.axis_index("dp")
        self.e = lax.axis_index("expert")
        self.r = self.place_of(self.p)
        order = list(range(0, self.nd, 2)) + list(range(1, self.nd, 2))[::-1]
        nd, ne = self.nd, self.ne
        self.ring = {
            way: [
                (order[i] * ne + e, order[(i + way) % nd] * ne + e)
                for i in range(nd)
                for e in range(ne)
            ]
            for way in (1, -1)
        }
        self.devices = nd * ne

    def place_of(self, p):
        return jnp.where(p % 2 == 0, p // 2, self.nd - 1 - p // 2)

    def dp_of(self, r):
        r = r % self.nd
        return jnp.where(r < self.nd // 2, 2 * r, 2 * (self.nd - 1 - r) + 1)

    def step(self, value, way):
        return lax.ppermute(value, AXES, self.ring[way])

    def exchange(self, value, bit):
        pairs = [[d, d | 1 << bit] for d in range(self.devices) if not d >> bit & 1]
        return lax.all_to_all(value, AXES, 0, 0, axis_index_groups=pairs, tiled=True)

    def swap(self, value, bit):
        return lax.ppermute(value, AXES, [(d, d ^ bit) for d in range(self.devices)])


def gather_weights(net, first, second, beside):
    half = net.nd // 2
    other_first = net.swap(first, WIDE)
    other_second = net.swap(after(second, other_first), WIDE)
    own = [jnp.stack([first, other_first]), jnp.stack([second, other_second])]
    offsets = [(0,)] + [(-s, s) for s in range(1, half)] + [(half,)]
    parts = [[], []]
    ahead, back = list(own), list(own)
    sent = None
    for s in range(half + 1):
        for k in (0, 1):
            if k == 0 and s == half - 1:
                ahead[k], back[k] = after((ahead[k], back[k]), beside)
            elif sent is not None:
                ahead[k], back[k] = after((ahead[k], back[k]), sent)
            sent = (ahead[k], back[k])
            if s in (0, half):
                parts[k].append((ahead[k] if s == 0 else jnp.stack([ahead[k], back[k]]))[None])
            else:
                parts[k].append(jnp.stack([ahead[k], back[k]]))
            if s + 1 < half:
                ahead[k] = net.step(ahead[k], 1)
                back[k] = net.step(back[k], -1)
            elif s + 1 == half:
                ahead[k] = net.step(ahead[k][0], 1)
                back[k] = net.step(back[k][1], -1)
    core, wide = net.e % 2, net.e // 2

    def assemble(pieces):
        rows, columns = pieces[0][1].shape[-2:]
        full = jnp.zeros((net.nd, net.ne, rows, columns), BF16)
        for places, mine, other in pieces:
            low = jnp.where(core == 0, mine, other)
            high = jnp.where(core == 0, other, mine)
            both = jnp.stack([low, high], axis=2)
            both = jnp.where(wide == 0, both, both[:, ::-1]).reshape(-1, net.ne, rows, columns)
            for i, offset in enumerate(places):
                at = (net.dp_of(net.r + offset), 0, 0, 0)
                full = lax.dynamic_update_slice(full, both[i : i + 1], at)
        return full.reshape(net.nd * net.ne * rows, columns)

    first_full = assemble(
        [(offsets[i], mine, net.swap(mine, CORE)) for i, mine in enumerate(parts[0])]
    )
    mine = jnp.concatenate(parts[1])
    places = [o for group in offsets for o in group]
    second_full = assemble([(places, mine, net.swap(mine, CORE))])
    return first_full, second_full


def weight_product_kernel(left, extra, right, out):
    columns = right.shape[1]
    out[0, :, :columns] = dot(left[0], right[...]).astype(BF16)
    out[0, :, columns:] = extra[0].astype(BF16)


def weight_product(left, extra, right):
    parts, depth = left.shape[:2]
    columns = right.shape[1] + extra.shape[2]
    return pl.pallas_call(
        weight_product_kernel,
        out_shape=jax.ShapeDtypeStruct((parts, depth, columns), BF16),
        grid=(parts,),
        in_specs=[
            pl.BlockSpec((1,) + left.shape[1:], lambda i: (i, 0, 0)),
            pl.BlockSpec((1,) + extra.shape[1:], lambda i: (i, 0, 0)),
            pl.BlockSpec(right.shape, lambda i: (0, 0)),
        ],
        out_specs=pl.BlockSpec((1, depth, columns), lambda i: (i, 0, 0)),
        compiler_params=pltpu.CompilerParams(vmem_limit_bytes=20 * 2**20),
        cost_estimate=pl.CostEstimate(flops=1024, bytes_accessed=1024, transcendentals=0),
        name="weight_product",
    )(left, extra, right)


def parts_by(array, parts, rows):
    blocks = array.reshape(-1, parts, rows, array.shape[1])
    return jnp.swapaxes(blocks, 0, 1).reshape(parts, -1, array.shape[1])


def halve_kernel(mine, kept, came, out):
    for i in range(2):
        out[i, 0] = (kept[0, i].astype(F32) + came[0, i].astype(F32)).astype(BF16)


def halve(kept, came, rows):
    columns = kept.shape[1]
    kept, came = (a.reshape(-1, 2, rows, columns) for a in (kept, came))
    count = kept.shape[0]
    piece = pl.BlockSpec((1, 2, rows, columns), lambda i: (i, 0, 0, 0))
    return pl.pallas_call(
        functools.partial(halve_kernel, None),
        out_shape=jax.ShapeDtypeStruct((2, count, rows, columns), BF16),
        grid=(count,),
        in_specs=[piece, piece],
        out_specs=pl.BlockSpec((2, 1, rows, columns), lambda i: (0, i, 0, 0)),
        compiler_params=pltpu.CompilerParams(vmem_limit_bytes=12 * 2**20),
        cost_estimate=pl.CostEstimate(flops=1024, bytes_accessed=1024, transcendentals=0),
        name="halve",
    )(kept, came).reshape(2, count * rows, columns)


class BlockSum:
    def __init__(self, net, halves, bit, rows):
        self.net, self.halves, self.bit, self.rows = net, halves, bit, rows
        self.count = net.devices.bit_length() - 1
        self.number = net.p * net.ne + net.e

    def send(self, *earlier):
        mine = self.number // (1 << self.bit) % 2
        halves = after(self.halves, *earlier) if earlier else self.halves
        self.kept = lax.dynamic_index_in_dim(halves, mine, 0, keepdims=False)
        sent = lax.dynamic_index_in_dim(halves, 1 - mine, 0, keepdims=False)
        self.came = self.net.swap(sent, 1 << self.bit)
        self.bit += 1

    def add(self, *earlier):
        came = after(self.came, *earlier) if earlier else self.came
        if self.bit == self.count:
            return self.kept.astype(F32) + came.astype(F32)
        self.halves = halve(self.kept, came, self.rows)
        return self.halves


def in_kernel(places, rows_a, rows_b, grad_pre, *refs):
    came, out = (refs[:2], refs[2:]) if len(refs) > 2 else (None, refs)
    for i, rows in enumerate((rows_a, rows_b)):
        at = slice(i * FE, (i + 1) * FE)
        share = dot(rows[...], grad_pre[0, :, at])
        if came is not None:
            share += came[i][0].astype(F32)
        if len(out) == 2:
            out[i][0] = share.astype(BF16)
        else:
            out[0][0, :, at] = share


def in_share(places, turned_rows, grad_pre, came, last=False):
    local, tokens_all, wide = grad_pre.shape
    depth = turned_rows.shape[0] // lax.axis_size("dp")
    piece = pl.BlockSpec((1, depth, FE), lambda i, place: (i, 0, 0))
    in_specs = [
        pl.BlockSpec((depth, tokens_all), lambda i, place: (place[0], 0)),
        pl.BlockSpec((depth, tokens_all), lambda i, place: (place[1], 0)),
        pl.BlockSpec((1, tokens_all, wide), lambda i, place: (i, 0, 0)),
    ] + [piece] * len(came)
    if last:
        out_shape = [jax.ShapeDtypeStruct((local, depth, wide), F32)]
        out_specs = [pl.BlockSpec((1, depth, wide), lambda i, place: (i, 0, 0))]
    else:
        out_shape = [jax.ShapeDtypeStruct((local, depth, FE), BF16)] * 2
        out_specs = [piece] * 2
    return pl.pallas_call(
        in_kernel,
        out_shape=out_shape,
        grid_spec=pltpu.PrefetchScalarGridSpec(
            num_scalar_prefetch=1, grid=(local,), in_specs=in_specs, out_specs=out_specs
        ),
        compiler_params=pltpu.CompilerParams(vmem_limit_bytes=14 * 2**20),
        cost_estimate=pl.CostEstimate(
            flops=10**13, bytes_accessed=10**9, transcendentals=0
        ),
        name="in_share",
    )(places, turned_rows, turned_rows, grad_pre, *came)


def out_kernel(places, act_a, act_b, up_a, up_b, *refs):
    came, out = (refs[:2], refs[2:]) if len(refs) > 2 else (None, refs)
    local, depth, tokens_all = act_a.shape
    for i, (act, up) in enumerate(((act_a, up_a), (act_b, up_b))):
        share = jnp.dot(
            act[...].reshape(local * depth, tokens_all), up[...], preferred_element_type=F32
        )
        if came is not None:
            share += came[i][...].astype(F32)
        out[i][...] = share.astype(out[i].dtype)


def out_share(places, turned_act, upstream_all, came, last=False):
    local, hidden, tokens_all = turned_act.shape
    width = upstream_all.shape[1]
    depth = hidden // lax.axis_size("dp")
    tile = 2 * LANES
    count = width // (2 * tile)
    piece = pl.BlockSpec((local * depth, tile), lambda i, place: (0, i))
    in_specs = [
        pl.BlockSpec((local, depth, tokens_all), lambda i, place: (0, place[0], 0)),
        pl.BlockSpec((local, depth, tokens_all), lambda i, place: (0, place[1], 0)),
        pl.BlockSpec((tokens_all, tile), lambda i, place: (0, i)),
        pl.BlockSpec((tokens_all, tile), lambda i, place: (0, i + count)),
    ] + [piece] * len(came)
    kind = F32 if last else BF16
    return pl.pallas_call(
        out_kernel,
        out_shape=[jax.ShapeDtypeStruct((local * depth, width // 2), kind)] * 2,
        grid_spec=pltpu.PrefetchScalarGridSpec(
            num_scalar_prefetch=1, grid=(count,), in_specs=in_specs, out_specs=[piece] * 2
        ),
        compiler_params=pltpu.CompilerParams(vmem_limit_bytes=12 * 2**20),
        cost_estimate=pl.CostEstimate(
            flops=10**13, bytes_accessed=10**9, transcendentals=0
        ),
        name="out_share",
    )(places, turned_act, turned_act, upstream_all, upstream_all, *came)


def expert_kernel(
    scalars,
    rows_a,
    rows_b,
    grad_plain,
    weight,
    *refs,
):
    activated, turned_act, grad_pre, gate_grad, turned_rows = refs[-5:]
    expert = pl.program_id(0)
    width = weight.shape[1]
    count = rows_a.shape[0]
    lanes = lax.broadcasted_iota(jnp.int32, (count, LANES), 1)
    here = lanes == scalars[0] + expert
    starts = [pl.multiple_of(scalars[2] * count, count), pl.multiple_of((1 - scalars[2]) * count, count)]

    @pl.when(expert == 0)
    def _():
        gate_grad[...] = jnp.zeros_like(gate_grad)
        for start, rows in zip(starts, (rows_a, rows_b)):
            turned_rows[:, pl.ds(start, count)] = rows[:, :width].T

    for start, rows in zip(starts, (rows_a, rows_b)):
        at = pl.ds(start, count)
        gate = jnp.sum(
            jnp.where(here, rows[:, width:].astype(F32), 0.0), axis=1, keepdims=True
        )
        x = rows[:, :width]
        g = jnp.dot(x, weight[0, :, :FE], preferred_element_type=F32)
        u = jnp.dot(x, weight[0, :, FE:], preferred_element_type=F32)
        s = jax.nn.sigmoid(g)
        silu = g * s
        act = silu * u
        plain = grad_plain[0, at, :]
        gate_grad[at, :] += jnp.where(here, jnp.sum(act * plain, axis=1, keepdims=True), 0.0)
        low = (act * gate).astype(BF16)
        activated[0, at, :] = low
        turned_act[0, :, at] = low.T
        da = plain * gate
        grad_pre[0, at, :FE] = (da * u * s * (1.0 + g * (1.0 - s))).astype(BF16)
        grad_pre[0, at, FE:] = (da * silu).astype(BF16)


def expert_half(scalars, rows_a, rows_b, grad_plain, weight, earlier):
    count = 2 * rows_a.shape[0]
    local, width, wide = weight.shape
    total = 2 * count
    whole = lambda i, sc: (0, 0)
    out_shape = [
        jax.ShapeDtypeStruct((local, total, FE), BF16),
        jax.ShapeDtypeStruct((local, FE, total), BF16),
        jax.ShapeDtypeStruct((local, total, wide), BF16),
        jax.ShapeDtypeStruct((total, LANES), F32),
        jax.ShapeDtypeStruct((width, total), BF16),
    ]
    out_specs = [
        pl.BlockSpec((1, count, FE), lambda i, sc: (i, sc[1], 0)),
        pl.BlockSpec((1, FE, count), lambda i, sc: (i, 0, sc[1])),
        pl.BlockSpec((1, count, wide), lambda i, sc: (i, sc[1], 0)),
        pl.BlockSpec((count, LANES), lambda i, sc: (sc[1], 0)),
        pl.BlockSpec((width, count), lambda i, sc: (0, sc[1])),
    ]
    in_specs = [
        pl.BlockSpec(rows_a.shape, whole),
        pl.BlockSpec(rows_b.shape, whole),
        pl.BlockSpec((1, count, FE), lambda i, sc: (i, sc[1], 0)),
        pl.BlockSpec((1, width, wide), lambda i, sc: (i, 0, 0)),
    ] + [pl.BlockSpec(memory_space=pl.ANY)] * len(earlier)
    flops = 2 * local * count * width * wide
    return pl.pallas_call(
        expert_kernel,
        out_shape=out_shape,
        grid_spec=pltpu.PrefetchScalarGridSpec(
            num_scalar_prefetch=1, grid=(local,), in_specs=in_specs, out_specs=out_specs
        ),
        input_output_aliases={5 + k: k for k in range(len(earlier))},
        compiler_params=pltpu.CompilerParams(
            dimension_semantics=("arbitrary",), vmem_limit_bytes=50 * 2**20
        ),
        cost_estimate=pl.CostEstimate(flops=flops, bytes_accessed=30 * 2**20, transcendentals=0),
        name="expert_half",
    )(scalars, rows_a, rows_b, grad_plain, weight, *earlier)


def on_device(
    tokens,
    cotangent,
    routes,
    segments,
    w_qkv,
    w_out,
    router,
    gain_attn,
    gain_mlp,
    expert_in,
    expert_out,
):
    net = Net()
    length, width = tokens.shape
    local_count = expert_in.shape[0]
    experts_all = local_count * net.ne
    wide_qkv = w_qkv.shape[1]

    small = jnp.concatenate([router, gain_attn[:, None], gain_mlp[:, None]], axis=1)
    small = jnp.pad(small, ((0, 0), (0, LANES - small.shape[1])))
    first_block = jnp.concatenate([w_qkv, small], axis=1)
    upstream_all = lax.all_gather(cotangent, "expert", axis=0, tiled=True)
    grad_act_plain = jnp.einsum("td,efd->etf", upstream_all, expert_out, preferred_element_type=F32)
    first_full, out_full = gather_weights(net, first_block, w_out, grad_act_plain)
    small_full = first_full[:, wide_qkv:]
    gain_row = experts_all % 8

    cos, sin = rope_tables(length)
    places_row = jnp.arange(length)
    bias = (
        (places_row[:, None] <= places_row[None, :])
        & (segments[0][:, None] == segments[0][None, :])
    ).astype(F32)
    normed, normed_turned, queries, key_rows, values, mixed_heads, gains = attend(
        experts_all, tokens, bias, cos, sin, first_full
    )
    hidden_state, sent, normed_two_turned, gate_float = branch(
        gain_row + 1, tokens, mixed_heads, out_full, small_full, gains, routes
    )
    across_rows = net.swap(sent, WIDE)
    own_rows, beside_rows = sent, net.swap(sent, CORE)
    core, wide = net.e % 2, net.e // 2
    scalars = lambda half: jnp.stack([net.e * local_count, half, core]).astype(jnp.int32)
    early = expert_half(scalars(wide), own_rows, beside_rows, grad_act_plain, expert_in, ())
    across_rows = after(across_rows, early)
    corner_rows = net.swap(across_rows, CORE)
    activated, turned_act, grad_pre, gate_grads, turned_rows = expert_half(
        scalars(1 - wide), across_rows, corner_rows, grad_act_plain, expert_in, early
    )

    def places(s):
        return jnp.stack([net.dp_of(net.r - 1 - s), net.dp_of(net.r + 1 + s)]).astype(jnp.int32)

    def advance(shares):
        return [net.step(shares[0], 1), net.step(shares[1], -1)]

    came_in, came_out = (), ()

    def ring_in(s, *earlier):
        nonlocal came_in
        if earlier:
            came_in = after(came_in, *earlier)
        shares = in_share(places(s), turned_rows, grad_pre, came_in)
        came_in = advance(shares)
        return shares

    def ring_out(s, *earlier):
        nonlocal came_out
        if earlier:
            came_out = after(came_out, *earlier)
        shares = out_share(places(s), turned_act, upstream_all, came_out)
        came_out = advance(shares)
        return shares

    def devices(*bits):
        return jnp.stack([net.e ^ bit for bit in bits])

    sent_out = ring_out(0)
    sent_in = ring_in(0, sent_out)
    beside = owner_rows(devices(1, 3), after(grad_pre, sent_in), expert_in, gate_grads)
    sent_out = ring_out(1, beside)
    beside_came = net.swap(after(beside, sent_out), CORE)
    kept = owner_rows(devices(0, 2), after(grad_pre, sent_out), expert_in, gate_grads)
    sent_in = ring_in(1, kept)
    onward = after(kept, sent_in)[length:].astype(F32) + beside_came[length:].astype(F32)
    onward = onward.astype(BF16)
    came = net.swap(onward, WIDE)
    mix = owner_rows(jnp.arange(4), after(activated, onward), expert_out)
    sent_out = ring_out(2, mix)
    grad_hidden, grad_branch, grad_mixed, extra = middle(
        experts_all,
        gain_row + 1,
        kept,
        beside_came,
        after(came, sent_out),
        cotangent,
        hidden_state,
        gate_float,
        normed_two_turned,
        gains,
        small_full,
        out_full,
    )
    block = width // net.devices
    d_out_local = weight_product(
        parts_by(mixed_heads.T, net.ne, block), parts_by(extra, net.ne, block), grad_branch
    )
    sent_in = ring_in(2, d_out_local)
    d_out_some = lax.psum_scatter(
        after(d_out_local, sent_in).reshape(-1, d_out_local.shape[2]),
        "expert",
        scatter_dimension=0,
        tiled=True,
    )
    grad_project, grad_tokens, extra_first = attend_back(
        gain_row,
        tokens,
        queries,
        key_rows,
        values,
        after(grad_mixed, sent_in),
        bias,
        cos,
        sin,
        gains,
        grad_hidden,
        first_full,
    )
    sent_out = ring_out(3, grad_project)
    d_qkv_local = weight_product(
        parts_by(after(normed_turned, sent_out), 2, block), parts_by(extra_first, 2, block), grad_project
    )
    sent_in = ring_in(3, d_qkv_local)
    qkv_sum = BlockSum(net, d_qkv_local, 0, block)
    qkv_sum.send(sent_in)
    sent_out = ring_out(4, sent_in)
    qkv_sum.add(sent_out)
    qkv_sum.send()
    sent_in = ring_in(4, qkv_sum.halves)

    def over_dp(value):
        return lax.all_to_all(value, "dp", 0, 0, tiled=True)

    def total(value):
        return jnp.sum(value.reshape(net.nd, block, -1).astype(F32), axis=0)

    d_out_some = over_dp(after(d_out_some, sent_in))
    sent_out = ring_out(5, sent_in)
    sent_in = ring_in(5, sent_out)
    d_qkv_some = qkv_sum.kept.astype(F32) + after(qkv_sum.came, sent_in).astype(F32)
    d_qkv_some = over_dp(d_qkv_some.astype(BF16))
    mixture = lax.psum_scatter(
        after(mix, qkv_sum.came), "expert", scatter_dimension=0, tiled=True
    )
    sent_out = ring_out(6, sent_in)
    sent_in = ring_in(6, sent_out)
    d_out = total(after(d_out_some, sent_in))
    here = jnp.stack([net.p, net.p]).astype(jnp.int32)
    d_expert_out = jnp.concatenate(
        out_share(here, turned_act, upstream_all, after(came_out, d_out), last=True), axis=1
    ).reshape(local_count, FE // net.nd, width)
    (d_expert_in,) = in_share(here, turned_rows, grad_pre, after(came_in, d_expert_out), last=True)
    activations = (hidden_state + after(mixture, d_expert_out).astype(F32)).astype(BF16)
    d_qkv = total(after(d_qkv_some, d_expert_out))
    return (
        activations,
        grad_tokens,
        d_qkv[:, :wide_qkv],
        d_out[:, :width],
        d_out[:, width : width + experts_all],
        d_qkv[:, wide_qkv],
        d_out[:, width + experts_all],
        d_expert_in,
        d_expert_out,
    )


def solution(mesh):
    rows = P(AXES, None)
    return jax.shard_map(
        on_device,
        mesh=mesh,
        in_specs=(rows,) * 7
        + (P(AXES), P(AXES), P("expert", None, None), P("expert", None, None)),
        out_specs=(rows,) * 5
        + (P(AXES), P(AXES), P("expert", "dp", None), P("expert", "dp", None)),
        check_vma=False,
    )
```

```python
import functools

import jax
import jax.numpy as jnp
from jax import lax
from jax.experimental import pallas as pl
from jax.experimental.pallas import tpu as pltpu
from jax.sharding import PartitionSpec as P

H = 24
KV = 8
HD = 64
FE = 512
TOP = 8

EPSILON = 1e-06
THETA = 10000.0
NEGATIVE = -1e30
AXES = ("dp", "expert")
CORE, WIDE = 1, 2
LANES = 128

F32 = jnp.float32
BF16 = jnp.bfloat16


def rope_tables(length):
    half_size = HD // 2
    frequency = THETA ** (-(jnp.arange(half_size, dtype=F32) * 2.0) / HD)
    angles = jnp.arange(length, dtype=F32)[:, None] * frequency[None, :]
    cos, sin = jnp.cos(angles), jnp.sin(angles)
    return (
        jnp.concatenate([cos] * (LANES // half_size), axis=1),
        jnp.concatenate([-sin, sin] * (LANES // HD), axis=1),
    )


def rotate_tile(tile, cos, sin):
    half_size = HD // 2
    lane = lax.broadcasted_iota(jnp.int32, tile.shape, 1)
    ahead = pltpu.roll(tile, LANES - half_size, 1)
    back = pltpu.roll(tile, half_size, 1)
    return tile * cos + jnp.where(lane % HD < half_size, ahead, back) * sin


def dot(left, right, dims=((1,), (0,))):
    return lax.dot_general(left, right, (dims, ((), ())), preferred_element_type=F32)


NT = ((1,), (1,))


def spread_row(row, lane, count):
    at = lax.broadcasted_iota(jnp.int32, (count, row.shape[1]), 0) == lane
    return jnp.where(at, jnp.broadcast_to(row, at.shape), 0.0).T


def call(kernel, out_shape, scratch=(), limit=40, name=None, specs=None, aliases=None):
    vmem = pl.BlockSpec(memory_space=pltpu.VMEM)
    return pl.pallas_call(
        kernel,
        out_shape=out_shape,
        in_specs=specs,
        out_specs=jax.tree.map(lambda _: vmem, out_shape),
        scratch_shapes=scratch,
        compiler_params=pltpu.CompilerParams(vmem_limit_bytes=limit * 2**20),
        cost_estimate=pl.CostEstimate(flops=1024, bytes_accessed=1024, transcendentals=0),
        name=name,
    )


VMEM_SPEC = pl.BlockSpec(memory_space=pltpu.VMEM)
SMEM_SPEC = pl.BlockSpec(memory_space=pltpu.SMEM)
ANY_SPEC = pl.BlockSpec(memory_space=pl.ANY)
HBM_SPEC = pl.BlockSpec(memory_space=pltpu.HBM)


def fetch(numbers, pieces, held, sems):
    columns = held.shape[1]
    copies = []
    for piece in pieces:
        places, wides, rows, wide = piece.shape
        for j in range(places):
            for w in range(wides):
                k = len(copies)
                source = piece.at[j, w]
                if columns < wide:
                    source = source.at[:, pl.ds(0, columns)]
                at = pl.ds(pl.multiple_of(numbers[k] * rows, 16), rows)
                copies.append(pltpu.make_async_copy(source, held.at[at], sems.at[k]))
    for copy in copies:
        copy.start()
    return copies


def wait_all(copies):
    for copy in copies:
        copy.wait()


def heads_of(array, group):
    size = H // KV
    first = group * size
    return jnp.concatenate(
        [array[:, h * HD : (h + 1) * HD] for h in range(first, first + size)], axis=0
    )


def group_softmax(queries, keys, bias):
    scores = dot(keys, queries, NT) * HD ** (-0.5)
    scores = jnp.where(bias > 0.0, scores, NEGATIVE)
    exponent = jnp.exp(scores - jnp.max(scores, axis=0, keepdims=True))
    return exponent * (1.0 / jnp.sum(exponent, axis=0, keepdims=True))


def attend_kernel(experts_all, count, numbers, tokens, bias, cos, sin, *refs):
    pieces = refs[:count]
    normed, turned_both, queries, key_rows, values, mixed, gains, small = refs[count : count + 8]
    project, held, sems = refs[count + 8 :]
    copies = fetch(numbers, pieces, held, sems)
    columns = held.shape[1]
    wide = columns - LANES
    x = tokens[...].astype(F32)
    plain = x * lax.rsqrt(jnp.mean(x * x, axis=-1, keepdims=True) + EPSILON)
    wait_all(copies)
    small[...] = held[:, wide:]
    turned = held[:, wide:].astype(F32).T
    gains[...] = turned[experts_all // 8 * 8 : experts_all // 8 * 8 + 16]
    row = experts_all
    low = (plain * turned[row : row + 1]).astype(BF16)
    normed[...] = low
    width = tokens.shape[1]
    turned_both[:width, :] = low.T
    tile = 4 * LANES
    for start in range(0, wide, tile):
        at = slice(start, min(start + tile, wide))
        project[:, at] = dot(low, held[:, at])
    c, s = cos[...], sin[...]
    for t in range(H * HD // LANES):
        at = slice(t * LANES, (t + 1) * LANES)
        queries[:, at] = rotate_tile(project[:, at], c, s).astype(BF16)
    for t in range(KV * HD // LANES):
        at = slice(t * LANES, (t + 1) * LANES)
        from_ = slice(H * HD + t * LANES, H * HD + (t + 1) * LANES)
        key_rows[:, at] = rotate_tile(project[:, from_], c, s).astype(BF16)
    values[...] = project[:, (H + KV) * HD : (H + 2 * KV) * HD].astype(BF16)
    size = H // KV
    length = tokens.shape[0]
    wide_bias = jnp.concatenate([bias[...]] * size, axis=1)
    for g in range(KV):
        at = slice(g * HD, (g + 1) * HD)
        probs = group_softmax(heads_of(queries, g), key_rows[:, at], wide_bias).astype(BF16)
        out = dot(values[:, at].T, probs)
        for j in range(size):
            h = g * size + j
            head = out[:, j * length : (j + 1) * length]
            mixed[:, h * HD : (h + 1) * HD] = head.T.astype(BF16)
            turned_both[width + h * HD : width + (h + 1) * HD, :] = head.astype(BF16)


def attend(experts_all, tokens, bias, cos, sin, weight):
    pieces, numbers = weight
    length, width = tokens.shape
    columns = pieces[0].shape[3]
    shape = lambda *dims, kind=BF16: jax.ShapeDtypeStruct(dims, kind)
    out_shape = [
        shape(length, width),
        shape(width + H * HD, length),
        shape(length, H * HD),
        shape(length, KV * HD),
        shape(length, KV * HD),
        shape(length, H * HD),
        shape(16, width, kind=F32),
        shape(width, LANES),
    ]
    scratch = [
        pltpu.VMEM((length, columns - LANES), F32),
        pltpu.VMEM((width, columns), BF16),
        pltpu.SemaphoreType.DMA(numbers.shape),
    ]
    return call(
        functools.partial(attend_kernel, experts_all, len(pieces)),
        out_shape,
        scratch,
        limit=58,
        name="attend",
        specs=[SMEM_SPEC] + [VMEM_SPEC] * 4 + [HBM_SPEC] * len(pieces),
    )(numbers, tokens, bias, cos, sin, *pieces)


def branch_kernel(gain_row, count, numbers, tokens, mixed, small, gains, routes, *refs):
    pieces = refs[:count]
    hidden, sent, gate_float = refs[count : count + 3]
    held, sems = refs[count + 3 :]
    copies = fetch(numbers, pieces, held, sems)
    width = tokens.shape[1]
    wait_all(copies)
    state = tokens[...].astype(F32) + dot(mixed[...], held[...])
    hidden[...] = state
    recip = lax.rsqrt(jnp.mean(state * state, axis=-1, keepdims=True) + EPSILON)
    low = (state * recip * gains[gain_row : gain_row + 1, :]).astype(BF16)
    sent[:, :width] = low
    logits = dot(low, small[...])
    lanes = lax.broadcasted_iota(jnp.int32, logits.shape, 1)
    chosen = lanes < 0
    for j in range(routes.shape[1]):
        chosen = chosen | (lanes == routes[:, j : j + 1])
    picked = jnp.where(chosen, logits, NEGATIVE)
    exponent = jnp.where(chosen, jnp.exp(picked - jnp.max(picked, axis=-1, keepdims=True)), 0.0)
    gate = exponent / jnp.sum(exponent, axis=-1, keepdims=True)
    gate_float[...] = gate
    sent[:, width:] = gate.astype(BF16)


def branch(gain_row, tokens, mixed, weight, small, gains, routes):
    pieces, numbers = weight
    length, width = tokens.shape
    shape = lambda *dims, kind=BF16: jax.ShapeDtypeStruct(dims, kind)
    return call(
        functools.partial(branch_kernel, gain_row, len(pieces)),
        [
            shape(length, width, kind=F32),
            shape(length, width + LANES),
            shape(length, LANES, kind=F32),
        ],
        [pltpu.VMEM((mixed.shape[1], width), BF16), pltpu.SemaphoreType.DMA(numbers.shape)],
        limit=58,
        name="branch",
        specs=[SMEM_SPEC] + [VMEM_SPEC] * 5 + [HBM_SPEC] * len(pieces),
    )(numbers, tokens, mixed, small, gains, routes, *pieces)


def owner_rows_kernel(extra_given, blocks, *refs):
    refs = refs[1:]
    left, weight = refs[:blocks], refs[blocks]
    extra = refs[blocks + 1 : 2 * blocks + 1] if extra_given else None
    out, total = refs[-2:]
    expert = pl.program_id(0)
    count = left[0].shape[1]
    width = total.shape[1]
    dims = NT if extra_given else ((1,), (0,))
    share = dot(jnp.concatenate([a[0] for a in left], axis=0), weight[0], dims)

    @pl.when(expert == 0)
    def _():
        total[...] = share

    @pl.when(expert > 0)
    def _():
        total[...] += share

    @pl.when(expert == pl.num_programs(0) - 1)
    def _():
        out[:, :width] = total[...].astype(BF16)
        if extra_given:
            for i in range(blocks):
                out[i * count : (i + 1) * count, width:] = extra[i][...].astype(BF16)


def owner_rows(devices, left, weight, extra=None):
    blocks = devices.shape[0]
    local, rows, inner = left.shape
    width = weight.shape[1] if extra is not None else weight.shape[2]
    columns = width if extra is None else width + LANES
    count = rows // 4
    out_shape = jax.ShapeDtypeStruct((blocks * count, columns), BF16)
    piece = lambda k: pl.BlockSpec((1, count, inner), lambda i, d: (i, d[k], 0))
    in_specs = [piece(k) for k in range(blocks)]
    in_specs.append(pl.BlockSpec((1,) + weight.shape[1:], lambda i, d: (i, 0, 0)))
    operands = [left] * blocks + [weight]
    if extra is not None:
        more = lambda k: pl.BlockSpec((count, LANES), lambda i, d: (d[k], 0))
        in_specs += [more(k) for k in range(blocks)]
        operands += [extra] * blocks
    return pl.pallas_call(
        functools.partial(owner_rows_kernel, extra is not None, blocks),
        out_shape=out_shape,
        grid_spec=pltpu.PrefetchScalarGridSpec(
            num_scalar_prefetch=1,
            grid=(local,),
            in_specs=in_specs,
            out_specs=pl.BlockSpec(out_shape.shape, lambda i, d: (0, 0)),
            scratch_shapes=[pltpu.VMEM((blocks * count, width), F32)],
        ),
        compiler_params=pltpu.CompilerParams(vmem_limit_bytes=58 * 2**20),
        cost_estimate=pl.CostEstimate(flops=1024, bytes_accessed=1024, transcendentals=0),
        name="owner_rows",
    )(devices.astype(jnp.int32), *operands)


def middle_kernel(
    experts_all,
    gain_row,
    parts,
    numbers,
    came,
    cotangent,
    hidden,
    gate_float,
    gains,
    small,
    *refs,
):
    pieces = refs[:parts]
    grad_hidden, pack, grad_mixed, held, sems = refs[parts:]
    copies = fetch(numbers, pieces, held, sems)
    count, width = cotangent.shape
    total = came[0].astype(F32) + came[1].astype(F32)
    gate = gate_float[...]
    gate_grad = total[:, width:].astype(BF16).astype(F32)
    centered = gate_grad - jnp.sum(gate * gate_grad, axis=-1, keepdims=True)
    logit_grad = (gate * centered).astype(BF16)
    grad_normed = total[:, :width] + dot(logit_grad, small[...], NT)
    state = hidden[...]
    recip = lax.rsqrt(jnp.mean(state * state, axis=-1, keepdims=True) + EPSILON)
    plain = state * recip
    scaled = grad_normed * gains[gain_row : gain_row + 1, :]
    gain_grad = jnp.sum(grad_normed * plain, axis=0, keepdims=True)
    back = recip * (scaled - plain * jnp.mean(scaled * plain, axis=-1, keepdims=True))
    grad = cotangent[...].astype(F32) + back
    grad_hidden[...] = grad
    low = grad.astype(BF16)
    first = lax.broadcasted_iota(jnp.int32, (16, width), 0) == 0
    high = gain_grad.astype(BF16).astype(F32)
    for k in range(2):
        pack[k, :count, :width] = low
        pack[k, :count, width:] = logit_grad
        pack[k, count:, :width] = jnp.where(first, high, gain_grad - high).astype(BF16)
        pack[k, count:, width:] = jnp.zeros((16, LANES), BF16)
    wait_all(copies)
    grad_mixed[...] = dot(low, held[...], NT).astype(BF16)


def attend_back_kernel(
    queries, key_rows, values, grad_mixed, bias, cos, sin, grad_project, project
):
    columns = grad_project.shape[2]
    size = H // KV
    length = queries.shape[0]
    scale = HD ** (-0.5)
    wide_bias = jnp.concatenate([bias[...]] * size, axis=1)
    for g in range(KV):
        at = slice(g * HD, (g + 1) * HD)
        q, k, v = heads_of(queries, g), key_rows[:, at], values[:, at]
        upstream = heads_of(grad_mixed, g)
        weights = group_softmax(q, k, wide_bias)
        grad_values = dot(weights.astype(BF16), upstream)
        grad_probs = dot(v, upstream, NT)
        delta = jnp.sum(weights * grad_probs, axis=0, keepdims=True)
        grad_scores = (weights * (grad_probs - delta)).astype(BF16)
        grad_keys = dot(grad_scores, q) * scale
        grad_queries = dot(k.T, grad_scores) * scale
        for j in range(size):
            h = g * size + j
            project[:, h * HD : (h + 1) * HD] = grad_queries[:, j * length : (j + 1) * length].T
        project[:, (H + g) * HD : (H + g + 1) * HD] = grad_keys
        project[:, (H + KV + g) * HD : (H + KV + g + 1) * HD] = grad_values
    c, s = cos[...], -sin[...]
    turns = (H + KV) * HD // LANES
    for t in range(turns):
        at = slice(t * LANES, (t + 1) * LANES)
        tile = rotate_tile(project[:, at], c, s).astype(BF16)
        grad_project[0, :, at] = tile
        grad_project[1, :, at] = tile
    rest = slice(turns * LANES, columns)
    tile = project[:, rest].astype(BF16)
    grad_project[0, :, rest] = tile
    grad_project[1, :, rest] = tile


def attend_back(*operands):
    length = operands[0].shape[0]
    columns = (H + 2 * KV) * HD
    return call(
        attend_back_kernel,
        jax.ShapeDtypeStruct((2, length, columns), BF16),
        [pltpu.VMEM((length, columns), F32)],
        limit=58,
        name="attend_back",
        specs=[VMEM_SPEC] * 7,
    )(*operands)


def input_back_kernel(
    gain_row, parts, numbers, tokens, grad_project, gains, grad_hidden, *refs
):
    pieces = refs[:parts]
    grad_tokens, held, sems = refs[parts:]
    copies = fetch(numbers, pieces, held, sems)
    wait_all(copies)
    grad_normed = dot(grad_project[0], held[...], NT)
    x = tokens[...].astype(F32)
    recip = lax.rsqrt(jnp.mean(x * x, axis=-1, keepdims=True) + EPSILON)
    plain = x * recip
    scaled = grad_normed * gains[gain_row : gain_row + 1, :]
    back = recip * (scaled - plain * jnp.mean(scaled * plain, axis=-1, keepdims=True))
    grad_tokens[...] = grad_hidden[...] + back


def middle(experts_all, gain_row, weight, *operands):
    pieces, numbers = weight
    count, width = operands[1].shape
    shape = lambda *dims, kind=BF16: jax.ShapeDtypeStruct(dims, kind)
    return call(
        functools.partial(middle_kernel, experts_all, gain_row, len(pieces)),
        [
            shape(count, width, kind=F32),
            shape(2, count + 16, width + LANES),
            shape(count, H * HD),
        ],
        [pltpu.VMEM((H * HD, width), BF16), pltpu.SemaphoreType.DMA(numbers.shape)],
        limit=58,
        name="middle",
        specs=[SMEM_SPEC] + [VMEM_SPEC] * 6 + [HBM_SPEC] * len(pieces),
    )(numbers, *operands, *pieces)


def input_back(gain_row, weight, *operands):
    pieces, numbers = weight
    length, width = operands[0].shape
    columns = operands[1].shape[2]
    return call(
        functools.partial(input_back_kernel, gain_row, len(pieces)),
        jax.ShapeDtypeStruct((length, width), F32),
        [pltpu.VMEM((width, columns), BF16), pltpu.SemaphoreType.DMA(numbers.shape)],
        limit=58,
        name="input_back",
        specs=[SMEM_SPEC] + [VMEM_SPEC] * 4 + [HBM_SPEC] * len(pieces),
    )(numbers, *operands, *pieces)


def after(value, *earlier):
    return lax.optimization_barrier((value, earlier))[0]


class Net:
    def __init__(self):
        self.nd = lax.axis_size("dp")
        self.ne = lax.axis_size("expert")
        self.p = lax.axis_index("dp")
        self.e = lax.axis_index("expert")
        self.r = self.place_of(self.p)
        order = list(range(0, self.nd, 2)) + list(range(1, self.nd, 2))[::-1]
        nd, ne = self.nd, self.ne
        self.ring = {
            way: [
                (order[i] * ne + e, order[(i + way) % nd] * ne + e)
                for i in range(nd)
                for e in range(ne)
            ]
            for way in (1, -1)
        }
        self.devices = nd * ne

    def place_of(self, p):
        return jnp.where(p % 2 == 0, p // 2, self.nd - 1 - p // 2)

    def dp_of(self, r):
        r = r % self.nd
        return jnp.where(r < self.nd // 2, 2 * r, 2 * (self.nd - 1 - r) + 1)

    def step(self, value, way):
        return lax.ppermute(value, AXES, self.ring[way])

    def exchange(self, value, bit):
        pairs = [[d, d | 1 << bit] for d in range(self.devices) if not d >> bit & 1]
        return lax.all_to_all(value, AXES, 0, 0, axis_index_groups=pairs, tiled=True)

    def swap(self, value, bit):
        return lax.ppermute(value, AXES, [(d, d ^ bit) for d in range(self.devices)])


def gather_weights(net, first, second, beside):
    half = net.nd // 2
    other_first = net.swap(first, WIDE)
    other_second = net.swap(after(second, other_first), WIDE)
    own = [jnp.stack([first, other_first]), jnp.stack([second, other_second])]
    offsets = [(0,)] + [(-s, s) for s in range(1, half)] + [(half,)]
    parts = [[], []]
    ahead, back = list(own), list(own)
    sent = None
    for s in range(half + 1):
        for k in (0, 1):
            if k == 0 and s == half - 2:
                ahead[k], back[k] = after((ahead[k], back[k]), beside)
            elif sent is not None:
                ahead[k], back[k] = after((ahead[k], back[k]), sent)
            sent = (ahead[k], back[k])
            if s in (0, half):
                parts[k].append((ahead[k] if s == 0 else jnp.stack([ahead[k], back[k]]))[None])
            else:
                parts[k].append(jnp.stack([ahead[k], back[k]]))
            if s + 1 < half:
                ahead[k] = net.step(ahead[k], 1)
                back[k] = net.step(back[k], -1)
            elif s + 1 == half:
                ahead[k] = net.step(ahead[k][0], 1)
                back[k] = net.step(back[k][1], -1)
    def numbers(groups):
        return [
            net.dp_of(net.r + offset) * net.ne + (net.e ^ bits)
            for group in groups
            for bits_of_core in (0, CORE)
            for offset in group
            for bits in (bits_of_core, bits_of_core ^ WIDE)
        ]

    first_pieces = [piece for mine in parts[0] for piece in (mine, net.swap(mine, CORE))]
    mine = jnp.concatenate(parts[1])
    second_pieces = [mine, net.swap(mine, CORE)]
    return (
        as_weight(first_pieces, numbers(offsets)),
        as_weight(second_pieces, numbers([[o for group in offsets for o in group]])),
    )


def as_weight(pieces, numbers):
    rows, columns = pieces[0].shape[2:]
    if rows % 16:
        blocks = jnp.concatenate([piece.reshape(-1, rows, columns) for piece in pieces])
        full = jnp.zeros_like(blocks).at[jnp.stack(numbers)].set(blocks)
        pieces, numbers = [full.reshape(1, 1, -1, columns)], [jnp.zeros((), jnp.int32)]
    return pieces, jnp.stack(numbers).astype(jnp.int32)


def weight_products_kernel(place, left, normed_two, gain, *refs):
    projects, packs, out = refs[:2], refs[2:4], refs[4]
    depth, count = out.shape[0], projects[0].shape[1]
    columns = projects[0].shape[2]
    width = packs[0].shape[2] - LANES
    core = place[0] % 2
    order = [2 * wide + c for c in (core, 1 - core) for wide in (0, 1)]

    def below(arrays, at):
        return jnp.concatenate([r[wide, :count, at] for r in arrays for wide in (0, 1)], axis=0)

    first = jnp.concatenate([left[i, :depth, :] for i in order], axis=1)
    second = jnp.concatenate([left[i, depth:, :] for i in order], axis=1)
    third = jnp.concatenate([normed_two[i] for i in order], axis=1)
    tile = 4 * LANES
    for start in range(0, columns, tile):
        at = slice(start, start + tile)
        out[:, at] = dot(first, below(projects, at)).astype(BF16)
    for start in range(0, width, tile):
        at = slice(start, start + tile)
        to = slice(columns + start, columns + start + tile)
        out[:, to] = dot(second, below(packs, at)).astype(BF16)
    rest = dot(third, below(packs, slice(width, width + LANES)))
    out[:, columns + width :] = (rest + gain[...]).astype(BF16)


def weight_products(place, left, normed_two, gain, projects, packs):
    depth = left.shape[1] // 2
    return call(
        weight_products_kernel,
        jax.ShapeDtypeStruct((depth, projects[0].shape[2] + packs[0].shape[2]), BF16),
        limit=58,
        name="weight_products",
        specs=[SMEM_SPEC] + [VMEM_SPEC] * 7,
    )(place, left, normed_two, gain, *projects, *packs)


def gain_column_kernel(lane, *refs):
    packs, out = refs[:2], refs[2]
    width = out.shape[0]
    count = packs[0].shape[1] - 16
    rows = sum(r[wide, count : count + 2, :width].astype(F32) for r in packs for wide in (0, 1))
    out[...] = spread_row(jnp.sum(rows, axis=0, keepdims=True), lane, LANES)


def gain_column(lane, packs):
    return call(
        functools.partial(gain_column_kernel, lane),
        jax.ShapeDtypeStruct((packs[0].shape[2] - LANES, LANES), F32),
        limit=58,
        name="gain_column",
        specs=[VMEM_SPEC] * 2,
    )(*packs)


def fold_kernel(came, out):
    for i in range(2):
        out[i, 0] = (came[0, 0, i].astype(F32) + came[1, 0, i].astype(F32)).astype(BF16)


def fold(came, rows):
    columns = came.shape[2]
    came = came.reshape(2, -1, 2, rows, columns)
    count = came.shape[1]
    return pl.pallas_call(
        fold_kernel,
        out_shape=jax.ShapeDtypeStruct((2, count, rows, columns), BF16),
        grid=(count,),
        in_specs=[pl.BlockSpec((2, 1, 2, rows, columns), lambda i: (0, i, 0, 0, 0))],
        out_specs=pl.BlockSpec((2, 1, rows, columns), lambda i: (0, i, 0, 0)),
        compiler_params=pltpu.CompilerParams(vmem_limit_bytes=58 * 2**20),
        cost_estimate=pl.CostEstimate(flops=1024, bytes_accessed=1024, transcendentals=0),
        name="fold",
    )(came).reshape(2, count * rows, columns)


class BlockSum:
    def __init__(self, net, halves, rows):
        self.net, self.halves, self.bit, self.rows = net, halves, 0, rows
        self.count = net.devices.bit_length() - 1

    def send(self, *earlier):
        halves = after(self.halves, *earlier) if earlier else self.halves
        self.came = self.net.exchange(halves, self.bit)
        self.bit += 1

    def add(self, *earlier):
        came = after(self.came, *earlier) if earlier else self.came
        if self.bit == self.count:
            return jnp.sum(came.astype(F32), axis=0)
        self.halves = fold(came, self.rows)
        return self.halves


def in_kernel(last, places, turned_rows, grad_pre, *refs):
    came, refs = (refs[:2], refs[2:]) if len(refs) > 10 - last else (None, refs)
    outs, (rows, grads, added, shares, rows_sems, grad_sems, came_sems, out_sems) = (
        refs[: 2 - last],
        refs[2 - last :],
    )
    local = grads.shape[0]
    depth = rows.shape[1]

    def rows_copy(i):
        at = pl.ds(pl.multiple_of(places[i] * depth, 16), depth)
        return pltpu.make_async_copy(turned_rows.at[at], rows.at[i], rows_sems.at[i])

    def grad_copy(e):
        return pltpu.make_async_copy(grad_pre.at[e], grads.at[e], grad_sems.at[e])

    def came_copy(i, e):
        return pltpu.make_async_copy(came[i].at[e], added.at[i, e], came_sems.at[i, e])

    def out_copy(i, e):
        if last:
            target = outs[0].at[e, :, pl.ds(i * FE, FE)]
        else:
            target = outs[i].at[e]
        return pltpu.make_async_copy(shares.at[i, e], target, out_sems.at[i, e])

    def begin(e):
        grad_copy(e).start()
        if came is not None:
            for i in range(2):
                came_copy(i, e).start()

    for i in range(2):
        rows_copy(i).start()
    begin(0)
    begin(1)
    for i in range(2):
        rows_copy(i).wait()

    @pl.loop(0, local)
    def _(e):
        @pl.when(e + 2 < local)
        def _():
            begin(e + 2)

        grad_copy(e).wait()
        if came is not None:
            for i in range(2):
                came_copy(i, e).wait()
        for i in range(2):
            share = dot(rows[i], grads[e, :, i * FE : (i + 1) * FE])
            if came is not None:
                share += added[i, e].astype(F32)
            shares[i, e] = share.astype(shares.dtype)
            out_copy(i, e).start()

    @pl.loop(0, local)
    def _(e):
        for i in range(2):
            out_copy(i, e).wait()


def in_share(places, turned_rows, grad_pre, came, cost, last=False):
    local, tokens_all, wide = grad_pre.shape
    depth = turned_rows.shape[0] // lax.axis_size("dp")
    kind = F32 if last else BF16
    if last:
        out_shape = [jax.ShapeDtypeStruct((local, depth, wide), kind)]
    else:
        out_shape = [jax.ShapeDtypeStruct((local, depth, FE), kind)] * 2
    return pl.pallas_call(
        functools.partial(in_kernel, int(last)),
        out_shape=out_shape,
        in_specs=[SMEM_SPEC] + [ANY_SPEC] * (2 + len(came)),
        out_specs=[ANY_SPEC] * len(out_shape),
        scratch_shapes=[
            pltpu.VMEM((2, depth, tokens_all), BF16),
            pltpu.VMEM((local, tokens_all, wide), BF16),
            pltpu.VMEM((2, local, depth, FE), BF16),
            pltpu.VMEM((2, local, depth, FE), kind),
            pltpu.SemaphoreType.DMA((2,)),
            pltpu.SemaphoreType.DMA((local,)),
            pltpu.SemaphoreType.DMA((2, local)),
            pltpu.SemaphoreType.DMA((2, local)),
        ],
        compiler_params=pltpu.CompilerParams(vmem_limit_bytes=58 * 2**20),
        cost_estimate=pl.CostEstimate(flops=cost, bytes_accessed=1024, transcendentals=0),
        name="in_share",
    )(places, turned_rows, grad_pre, *came)


def out_kernel(last, places, turned_act, upstream, *refs):
    came, refs = (refs[:2], refs[2:]) if len(refs) > 10 else (None, refs)
    outs, (rows, ups, added, shares, rows_sems, up_sems, came_sems, out_sems) = refs[:2], refs[2:]
    local, depth, tokens_all = rows.shape[1:]
    half = ups.shape[2]

    def copies(i):
        at = pl.ds(pl.multiple_of(places[i] * depth, 16), depth)
        some = [
            pltpu.make_async_copy(turned_act.at[:, at], rows.at[i], rows_sems.at[i]),
            pltpu.make_async_copy(upstream.at[:, pl.ds(i * half, half)], ups.at[i], up_sems.at[i]),
        ]
        if came is not None:
            some.append(pltpu.make_async_copy(came[i], added.at[i], came_sems.at[i]))
        return some

    def out_copy(i):
        return pltpu.make_async_copy(shares.at[i], outs[i], out_sems.at[i])

    for i in range(2):
        for copy in copies(i):
            copy.start()
    for i in range(2):
        for copy in copies(i):
            copy.wait()
        share = dot(rows[i].reshape(local * depth, tokens_all), ups[i])
        if came is not None:
            share += added[i].astype(F32)
        shares[i] = share.astype(shares.dtype)
        out_copy(i).start()
    for i in range(2):
        out_copy(i).wait()


def out_share(places, turned_act, upstream_all, came, cost, last=False):
    local, hidden, tokens_all = turned_act.shape
    half = upstream_all.shape[1] // 2
    depth = hidden // lax.axis_size("dp")
    kind = F32 if last else BF16
    return pl.pallas_call(
        functools.partial(out_kernel, int(last)),
        out_shape=[jax.ShapeDtypeStruct((local * depth, half), kind)] * 2,
        in_specs=[SMEM_SPEC] + [ANY_SPEC] * (2 + len(came)),
        out_specs=[ANY_SPEC] * 2,
        scratch_shapes=[
            pltpu.VMEM((2, local, depth, tokens_all), BF16),
            pltpu.VMEM((2, tokens_all, half), BF16),
            pltpu.VMEM((2, local * depth, half), BF16),
            pltpu.VMEM((2, local * depth, half), kind),
        ]
        + [pltpu.SemaphoreType.DMA((2,))] * 4,
        compiler_params=pltpu.CompilerParams(vmem_limit_bytes=58 * 2**20),
        cost_estimate=pl.CostEstimate(flops=cost, bytes_accessed=1024, transcendentals=0),
        name="out_share",
    )(places, turned_act, upstream_all, *came)


def owner_grads_kernel(upstream, weight, out):
    out[0] = dot(upstream[...], weight[0], NT).astype(BF16)


def owner_grads(upstream, weight):
    local, hidden, width = weight.shape
    rows = upstream.shape[0]
    return pl.pallas_call(
        owner_grads_kernel,
        out_shape=jax.ShapeDtypeStruct((local, rows, hidden), BF16),
        grid=(local,),
        in_specs=[
            pl.BlockSpec(upstream.shape, lambda i: (0, 0)),
            pl.BlockSpec((1, hidden, width), lambda i: (i, 0, 0)),
        ],
        out_specs=pl.BlockSpec((1, rows, hidden), lambda i: (i, 0, 0)),
        compiler_params=pltpu.CompilerParams(vmem_limit_bytes=58 * 2**20),
        cost_estimate=pl.CostEstimate(
            flops=2 * local * rows * hidden * width, bytes_accessed=16 * 2**20, transcendentals=0
        ),
        name="owner_grads",
    )(upstream, weight)


def expert_kernel(later, scalars, rows_a, rows_b, grad_plain, weight, *refs):
    refs = refs[5 if later else 0 :]
    outs, bufs, (weights, plains, weight_sems, plain_sems, out_sems) = refs[:5], refs[5:10], refs[10:]
    activated, turned_act, grad_pre, gate_grad, turned_rows = bufs
    local, width = weights.shape[:2]
    count = rows_a.shape[0]
    half = pl.ds(pl.multiple_of(scalars[1] * 2 * count, 2 * count), 2 * count)

    def weight_copy(e):
        return pltpu.make_async_copy(weight.at[e], weights.at[e], weight_sems.at[e])

    def plain_copy(e):
        return pltpu.make_async_copy(grad_plain.at[e, half], plains.at[e], plain_sems.at[e])

    def out_copies(e):
        return [
            pltpu.make_async_copy(activated.at[e], outs[0].at[e, half], out_sems.at[0, e]),
            pltpu.make_async_copy(turned_act.at[e], outs[1].at[e, :, half], out_sems.at[1, e]),
            pltpu.make_async_copy(grad_pre.at[e], outs[2].at[e, half], out_sems.at[2, e]),
        ]

    rows_copy = pltpu.make_async_copy(turned_rows, outs[4].at[:, half], out_sems.at[3, 0])
    gate_copy = pltpu.make_async_copy(gate_grad, outs[3].at[half], out_sems.at[3, 1])
    for e in range(2):
        weight_copy(e).start()
        plain_copy(e).start()
    both = (rows_a, rows_b)
    starts = [pl.multiple_of(scalars[2] * count, count), pl.multiple_of((1 - scalars[2]) * count, count)]
    gate_grad[...] = jnp.zeros_like(gate_grad)
    for start, rows in zip(starts, both):
        turned_rows[:, pl.ds(start, count)] = rows[:, :width].T
    rows_copy.start()
    lanes = lax.broadcasted_iota(jnp.int32, (count, LANES), 1)
    tile = 2 * LANES

    @pl.loop(0, local)
    def _(e):
        here = lanes == scalars[0] + e

        @pl.when(e + 2 < local)
        def _():
            weight_copy(e + 2).start()
            plain_copy(e + 2).start()

        weight_copy(e).wait()
        plain_copy(e).wait()
        gates = [
            jnp.sum(jnp.where(here, rows[:, width:].astype(F32), 0.0), axis=1, keepdims=True)
            for rows in both
        ]
        x = jnp.concatenate([rows[:, :width] for rows in both], axis=0)
        sums = [0.0, 0.0]
        for f in range(0, FE, tile):
            g_both = dot(x, weights[e, :, f : f + tile])
            u_both = dot(x, weights[e, :, FE + f : FE + f + tile])
            for i in range(2):
                at = pl.ds(starts[i], count)
                part = slice(i * count, (i + 1) * count)
                g, u, gate = g_both[part], u_both[part], gates[i]
                s = jax.nn.sigmoid(g)
                silu = g * s
                act = silu * u
                plain = plains[e, at, f : f + tile].astype(F32)
                sums[i] += jnp.sum(act * plain, axis=1, keepdims=True)
                low = (act * gate).astype(BF16)
                activated[e, at, f : f + tile] = low
                turned_act[e, f : f + tile, at] = low.T
                da = plain * gate
                grad_pre[e, at, f : f + tile] = (da * u * s * (1.0 + g * (1.0 - s))).astype(BF16)
                grad_pre[e, at, FE + f : FE + f + tile] = (da * silu).astype(BF16)
        for copy in out_copies(e):
            copy.start()
        for i in range(2):
            gate_grad[pl.ds(starts[i], count), :] += jnp.where(here, sums[i], 0.0)

    gate_copy.start()
    rows_copy.wait()
    gate_copy.wait()

    @pl.loop(0, local)
    def _(e):
        for copy in out_copies(e):
            copy.wait()


def expert_half(scalars, rows_a, rows_b, grad_plain, weight, earlier):
    count = 2 * rows_a.shape[0]
    local, width, wide = weight.shape
    total = 2 * count
    out_shape = [
        jax.ShapeDtypeStruct((local, total, FE), BF16),
        jax.ShapeDtypeStruct((local, FE, total), BF16),
        jax.ShapeDtypeStruct((local, total, wide), BF16),
        jax.ShapeDtypeStruct((total, LANES), F32),
        jax.ShapeDtypeStruct((width, total), BF16),
    ]
    return pl.pallas_call(
        functools.partial(expert_kernel, bool(earlier)),
        out_shape=out_shape,
        in_specs=[SMEM_SPEC, VMEM_SPEC, VMEM_SPEC, ANY_SPEC, ANY_SPEC] + [ANY_SPEC] * len(earlier),
        out_specs=[ANY_SPEC] * 5,
        scratch_shapes=[
            pltpu.VMEM((local, count, FE), BF16),
            pltpu.VMEM((local, FE, count), BF16),
            pltpu.VMEM((local, count, wide), BF16),
            pltpu.VMEM((count, LANES), F32),
            pltpu.VMEM((width, count), BF16),
            pltpu.VMEM(weight.shape, BF16),
            pltpu.VMEM((local, count, FE), BF16),
            pltpu.SemaphoreType.DMA((local,)),
            pltpu.SemaphoreType.DMA((local,)),
            pltpu.SemaphoreType.DMA((4, max(local, 2))),
        ],
        input_output_aliases={5 + k: k for k in range(len(earlier))},
        compiler_params=pltpu.CompilerParams(vmem_limit_bytes=58 * 2**20),
        cost_estimate=pl.CostEstimate(
            flops=2 * local * count * width * wide, bytes_accessed=30 * 2**20, transcendentals=0
        ),
        name="expert_half",
    )(scalars, rows_a, rows_b, grad_plain, weight, *earlier)


def on_device(
    tokens,
    cotangent,
    routes,
    segments,
    w_qkv,
    w_out,
    router,
    gain_attn,
    gain_mlp,
    expert_in,
    expert_out,
):
    net = Net()
    length, width = tokens.shape
    local_count = expert_in.shape[0]
    experts_all = local_count * net.ne
    wide_qkv = w_qkv.shape[1]

    small = jnp.concatenate([router, gain_attn[:, None], gain_mlp[:, None]], axis=1)
    small = jnp.pad(small, ((0, 0), (0, LANES - small.shape[1])))
    first_block = jnp.concatenate([w_qkv, small], axis=1)
    upstream_all = lax.all_gather(cotangent, "expert", axis=0, tiled=True)
    grad_act_plain = owner_grads(upstream_all, expert_out)
    qkv_weight, out_weight = gather_weights(net, first_block, w_out, grad_act_plain)
    gain_row = experts_all % 8

    cos, sin = rope_tables(length)
    places_row = jnp.arange(length)
    bias = (
        (places_row[:, None] <= places_row[None, :])
        & (segments[0][:, None] == segments[0][None, :])
    ).astype(F32)
    normed, turned_both, queries, key_rows, values, mixed_heads, gains, small_full = attend(
        experts_all, tokens, bias, cos, sin, qkv_weight
    )
    hidden_state, sent, gate_float = branch(
        gain_row + 1, tokens, mixed_heads, out_weight, small_full, gains, routes
    )
    across_rows = net.swap(sent, WIDE)
    own_rows, beside_rows = sent, net.swap(sent, CORE)
    core, wide = net.e % 2, net.e // 2
    scalars = lambda half: jnp.stack([net.e * local_count, half, core]).astype(jnp.int32)
    early = expert_half(scalars(wide), own_rows, beside_rows, grad_act_plain, expert_in, ())
    across_rows = after(across_rows, early)
    corner_rows = net.swap(across_rows, CORE)
    activated, turned_act, grad_pre, gate_grads, turned_rows = expert_half(
        scalars(1 - wide), across_rows, corner_rows, grad_act_plain, expert_in, early
    )

    def places(s):
        return jnp.stack([net.dp_of(net.r - 1 - s), net.dp_of(net.r + 1 + s)]).astype(jnp.int32)

    def cost(s):
        return 10**10 if s == 4 else 3 * 10**10

    def advance(shares):
        return [net.step(shares[0], 1), net.step(shares[1], -1)]

    came_in, came_out = (), ()

    def ring_in(s, *earlier, beside=None):
        nonlocal came_in
        if earlier:
            came_in = after(came_in, *earlier)
        shares = in_share(places(s), turned_rows, grad_pre, came_in, cost(s))
        if beside is not None:
            shares = after(shares, beside)
        came_in = advance(shares)
        return shares

    def ring_out(s, *earlier, beside=None):
        nonlocal came_out
        if earlier:
            came_out = after(came_out, *earlier)
        shares = out_share(places(s), turned_act, upstream_all, came_out, cost(s))
        if beside is not None:
            shares = after(shares, beside)
        came_out = advance(shares)
        return shares

    def devices(*bits):
        return jnp.stack([net.e ^ bit for bit in bits])

    sent_out = ring_out(0)
    sent_in = ring_in(0, sent_out)
    block = width // net.devices
    lefts = turned_both.reshape(2, net.nd, net.ne, block, length).transpose(2, 0, 1, 3, 4)
    lefts = lax.all_to_all(
        lefts.reshape(net.ne, -1, length), "expert", 0, 0, tiled=True
    )
    beside = owner_rows(devices(1, 3), after(grad_pre, sent_in, lefts), expert_in, gate_grads)
    beside_came = net.swap(beside, CORE)
    sent_out = ring_out(1, beside, beside=beside_came)
    kept = owner_rows(devices(0, 2), after(grad_pre, sent_out), expert_in, gate_grads)
    both = (kept.astype(F32) + beside_came.astype(F32)).astype(BF16)
    both = both.reshape(2, length, -1)
    came = net.exchange(jnp.where(wide == 0, both, both[::-1]), 1)
    sent_in = ring_in(1, both)
    mix = owner_rows(jnp.arange(4), after(activated, sent_in), expert_out)
    sent_out = ring_out(2, mix)
    grad_hidden, pack, grad_mixed = middle(
        experts_all,
        gain_row + 1,
        out_weight,
        after(came, sent_out),
        cotangent,
        hidden_state,
        gate_float,
        gains,
        small_full,
    )
    packs = net.exchange(pack, 1)
    sent_in = ring_in(2, grad_mixed)
    grad_project = attend_back(
        queries, key_rows, values, after(grad_mixed, sent_in), bias, cos, sin
    )
    projects = net.exchange(grad_project, 1)
    sent_out = ring_out(3, grad_project)
    sent_in = ring_in(3, sent_out)
    sent_out = ring_out(4, sent_in)
    projects, packs = after((projects, packs), sent_out, came_in)
    projects_beside, packs_beside = net.swap(projects, CORE), net.swap(packs, CORE)
    sent_in = ring_in(4, projects, packs, beside=(projects_beside, packs_beside))
    mine = lambda rows: lax.dynamic_index_in_dim(
        rows.reshape(net.nd, net.ne, block, -1), net.e, 1, keepdims=False
    ).reshape(net.nd * block, -1)
    normed_two = mine(turned_rows).reshape(-1, net.ne, length).transpose(1, 0, 2)
    packs = (packs, packs_beside)
    products = weight_products(
        net.e.astype(jnp.int32).reshape(1),
        after(lefts, sent_in),
        normed_two,
        mine(gain_column(experts_all, packs)),
        (projects, projects_beside),
        packs,
    )
    sent_out = ring_out(5, products)
    d_all = lax.psum_scatter(after(products, sent_out), "dp", scatter_dimension=0, tiled=True)
    sent_in = ring_in(5, sent_out)
    mix_all = lax.all_to_all(after(mix, sent_in), "expert", 0, 0, tiled=True)
    for s in range(6, net.nd - 1):
        sent_out = ring_out(s, sent_in)
        sent_in = ring_in(s, sent_out)
    grad_tokens = input_back(
        gain_row, qkv_weight, tokens, after(grad_project, sent_in), gains, grad_hidden
    )
    mixture = jnp.sum(mix_all.reshape(net.ne, length, width).astype(F32), axis=0)
    activations = (hidden_state + mixture).astype(BF16)
    here = jnp.stack([net.p, net.p]).astype(jnp.int32)
    d_expert_out = jnp.concatenate(
        out_share(
            here, turned_act, upstream_all, after(came_out, grad_tokens), cost(net.nd), last=True
        ),
        axis=1,
    ).reshape(local_count, FE // net.nd, width)
    d_all = after(d_all, d_expert_out).astype(F32)
    d_qkv = d_all[:, :wide_qkv]
    d_small = d_all[:, wide_qkv + width :]
    d_gain_first = jnp.sum(d_qkv * w_qkv.astype(F32), axis=1) / gain_attn.astype(F32)
    (d_expert_in,) = in_share(
        here, turned_rows, grad_pre, after(came_in, d_gain_first), cost(net.nd), last=True
    )
    return (
        activations,
        grad_tokens,
        d_qkv,
        d_all[:, wide_qkv : wide_qkv + width],
        d_small[:, :experts_all],
        d_gain_first,
        d_small[:, experts_all],
        d_expert_in,
        d_expert_out,
    )


def solution(mesh):
    rows = P(AXES, None)
    return jax.shard_map(
        on_device,
        mesh=mesh,
        in_specs=(rows,) * 7
        + (P(AXES), P(AXES), P("expert", None, None), P("expert", None, None)),
        out_specs=(rows,) * 5
        + (P(AXES), P(AXES), P("expert", "dp", None), P("expert", "dp", None)),
        check_vma=False,
    )
```

```python
import functools

import jax
import jax.numpy as jnp
from jax import lax
from jax.experimental import pallas as pl
from jax.experimental.pallas import tpu as pltpu
from jax.sharding import PartitionSpec as P

H = 24
KV = 8
HD = 64
FE = 512
TOP = 8

EPSILON = 1e-06
THETA = 10000.0
NEGATIVE = -1e30
AXES = ("dp", "expert")
CORE, WIDE = 1, 2
LANES = 128

F32 = jnp.float32
BF16 = jnp.bfloat16


def rope_tables(length):
    half_size = HD // 2
    frequency = THETA ** (-(jnp.arange(half_size, dtype=F32) * 2.0) / HD)
    angles = jnp.arange(length, dtype=F32)[:, None] * frequency[None, :]
    cos, sin = jnp.cos(angles), jnp.sin(angles)
    return (
        jnp.concatenate([cos] * (LANES // half_size), axis=1),
        jnp.concatenate([-sin, sin] * (LANES // HD), axis=1),
    )


def rotate_tile(tile, cos, sin):
    half_size = HD // 2
    lane = lax.broadcasted_iota(jnp.int32, tile.shape, 1)
    ahead = pltpu.roll(tile, LANES - half_size, 1)
    back = pltpu.roll(tile, half_size, 1)
    return tile * cos + jnp.where(lane % HD < half_size, ahead, back) * sin


def dot(left, right, dims=((1,), (0,))):
    return lax.dot_general(left, right, (dims, ((), ())), preferred_element_type=F32)


NT = ((1,), (1,))


def spread_row(row, lane, count):
    at = lax.broadcasted_iota(jnp.int32, (count, row.shape[1]), 0) == lane
    return jnp.where(at, jnp.broadcast_to(row, at.shape), 0.0).T


def call(kernel, out_shape, scratch=(), limit=40, name=None, specs=None, aliases=None):
    vmem = pl.BlockSpec(memory_space=pltpu.VMEM)
    return pl.pallas_call(
        kernel,
        out_shape=out_shape,
        in_specs=specs,
        out_specs=jax.tree.map(lambda _: vmem, out_shape),
        scratch_shapes=scratch,
        compiler_params=pltpu.CompilerParams(vmem_limit_bytes=limit * 2**20),
        cost_estimate=pl.CostEstimate(flops=1024, bytes_accessed=1024, transcendentals=0),
        name=name,
    )


VMEM_SPEC = pl.BlockSpec(memory_space=pltpu.VMEM)
SMEM_SPEC = pl.BlockSpec(memory_space=pltpu.SMEM)
ANY_SPEC = pl.BlockSpec(memory_space=pl.ANY)
HBM_SPEC = pl.BlockSpec(memory_space=pltpu.HBM)


def fetch(numbers, pieces, held, sems):
    columns = held.shape[1]
    copies = []
    for piece in pieces:
        places, wides, rows, wide = piece.shape
        for j in range(places):
            for w in range(wides):
                k = len(copies)
                source = piece.at[j, w]
                if columns < wide:
                    source = source.at[:, pl.ds(0, columns)]
                at = pl.ds(pl.multiple_of(numbers[k] * rows, 16), rows)
                copies.append(pltpu.make_async_copy(source, held.at[at], sems.at[k]))
    for copy in copies:
        copy.start()
    return copies


def wait_all(copies):
    for copy in copies:
        copy.wait()


def heads_of(array, group):
    size = H // KV
    first = group * size
    return jnp.concatenate(
        [array[:, h * HD : (h + 1) * HD] for h in range(first, first + size)], axis=0
    )


def group_softmax(queries, keys, bias):
    scores = dot(keys, queries, NT) * HD ** (-0.5)
    scores = jnp.where(bias > 0.0, scores, NEGATIVE)
    exponent = jnp.exp(scores - jnp.max(scores, axis=0, keepdims=True))
    return exponent * (1.0 / jnp.sum(exponent, axis=0, keepdims=True))


def attend_kernel(experts_all, count, numbers, tokens, bias, cos, sin, *refs):
    pieces = refs[:count]
    normed, turned_both, queries, key_rows, values, mixed, gains, small = refs[count : count + 8]
    project, held, sems = refs[count + 8 :]
    copies = fetch(numbers, pieces, held, sems)
    columns = held.shape[1]
    wide = columns - LANES
    x = tokens[...].astype(F32)
    plain = x * lax.rsqrt(jnp.mean(x * x, axis=-1, keepdims=True) + EPSILON)
    wait_all(copies)
    small[...] = held[:, wide:]
    turned = held[:, wide:].astype(F32).T
    gains[...] = turned[experts_all // 8 * 8 : experts_all // 8 * 8 + 16]
    row = experts_all
    low = (plain * turned[row : row + 1]).astype(BF16)
    normed[...] = low
    width = tokens.shape[1]
    turned_both[:width, :] = low.T
    tile = 4 * LANES
    for start in range(0, wide, tile):
        at = slice(start, min(start + tile, wide))
        project[:, at] = dot(low, held[:, at])
    c, s = cos[...], sin[...]
    for t in range(H * HD // LANES):
        at = slice(t * LANES, (t + 1) * LANES)
        queries[:, at] = rotate_tile(project[:, at], c, s).astype(BF16)
    for t in range(KV * HD // LANES):
        at = slice(t * LANES, (t + 1) * LANES)
        from_ = slice(H * HD + t * LANES, H * HD + (t + 1) * LANES)
        key_rows[:, at] = rotate_tile(project[:, from_], c, s).astype(BF16)
    values[...] = project[:, (H + KV) * HD : (H + 2 * KV) * HD].astype(BF16)
    size = H // KV
    length = tokens.shape[0]
    wide_bias = jnp.concatenate([bias[...]] * size, axis=1)
    for g in range(KV):
        at = slice(g * HD, (g + 1) * HD)
        probs = group_softmax(heads_of(queries, g), key_rows[:, at], wide_bias).astype(BF16)
        out = dot(values[:, at].T, probs)
        for j in range(size):
            h = g * size + j
            head = out[:, j * length : (j + 1) * length]
            mixed[:, h * HD : (h + 1) * HD] = head.T.astype(BF16)
            turned_both[width + h * HD : width + (h + 1) * HD, :] = head.astype(BF16)


def attend(experts_all, tokens, bias, cos, sin, weight):
    pieces, numbers = weight
    length, width = tokens.shape
    columns = pieces[0].shape[3]
    shape = lambda *dims, kind=BF16: jax.ShapeDtypeStruct(dims, kind)
    out_shape = [
        shape(length, width),
        shape(width + H * HD, length),
        shape(length, H * HD),
        shape(length, KV * HD),
        shape(length, KV * HD),
        shape(length, H * HD),
        shape(16, width, kind=F32),
        shape(width, LANES),
    ]
    scratch = [
        pltpu.VMEM((length, columns - LANES), F32),
        pltpu.VMEM((width, columns), BF16),
        pltpu.SemaphoreType.DMA(numbers.shape),
    ]
    return call(
        functools.partial(attend_kernel, experts_all, len(pieces)),
        out_shape,
        scratch,
        limit=58,
        name="attend",
        specs=[SMEM_SPEC] + [VMEM_SPEC] * 4 + [HBM_SPEC] * len(pieces),
    )(numbers, tokens, bias, cos, sin, *pieces)


def branch_kernel(gain_row, count, numbers, tokens, mixed, small, gains, routes, *refs):
    pieces = refs[:count]
    hidden, sent, gate_float = refs[count : count + 3]
    held, sems = refs[count + 3 :]
    copies = fetch(numbers, pieces, held, sems)
    width = tokens.shape[1]
    wait_all(copies)
    state = tokens[...].astype(F32) + dot(mixed[...], held[...])
    hidden[...] = state
    recip = lax.rsqrt(jnp.mean(state * state, axis=-1, keepdims=True) + EPSILON)
    low = (state * recip * gains[gain_row : gain_row + 1, :]).astype(BF16)
    sent[:, :width] = low
    logits = dot(low, small[...])
    lanes = lax.broadcasted_iota(jnp.int32, logits.shape, 1)
    chosen = lanes < 0
    for j in range(routes.shape[1]):
        chosen = chosen | (lanes == routes[:, j : j + 1])
    picked = jnp.where(chosen, logits, NEGATIVE)
    exponent = jnp.where(chosen, jnp.exp(picked - jnp.max(picked, axis=-1, keepdims=True)), 0.0)
    gate = exponent / jnp.sum(exponent, axis=-1, keepdims=True)
    gate_float[...] = gate
    sent[:, width:] = gate.astype(BF16)


def branch(gain_row, tokens, mixed, weight, small, gains, routes):
    pieces, numbers = weight
    length, width = tokens.shape
    shape = lambda *dims, kind=BF16: jax.ShapeDtypeStruct(dims, kind)
    return call(
        functools.partial(branch_kernel, gain_row, len(pieces)),
        [
            shape(length, width, kind=F32),
            shape(length, width + LANES),
            shape(length, LANES, kind=F32),
        ],
        [pltpu.VMEM((mixed.shape[1], width), BF16), pltpu.SemaphoreType.DMA(numbers.shape)],
        limit=58,
        name="branch",
        specs=[SMEM_SPEC] + [VMEM_SPEC] * 5 + [HBM_SPEC] * len(pieces),
    )(numbers, tokens, mixed, small, gains, routes, *pieces)


def owner_rows_kernel(extra_given, blocks, *refs):
    refs = refs[1:]
    left, weight = refs[:blocks], refs[blocks]
    extra = refs[blocks + 1 : 2 * blocks + 1] if extra_given else None
    out, total = refs[-2:]
    expert = pl.program_id(0)
    count = left[0].shape[1]
    width = total.shape[1]
    dims = NT if extra_given else ((1,), (0,))
    share = dot(jnp.concatenate([a[0] for a in left], axis=0), weight[0], dims)

    @pl.when(expert == 0)
    def _():
        total[...] = share

    @pl.when(expert > 0)
    def _():
        total[...] += share

    @pl.when(expert == pl.num_programs(0) - 1)
    def _():
        out[:, :width] = total[...].astype(BF16)
        if extra_given:
            for i in range(blocks):
                out[i * count : (i + 1) * count, width:] = extra[i][...].astype(BF16)


def owner_rows(devices, left, weight, extra=None):
    blocks = devices.shape[0]
    local, rows, inner = left.shape
    width = weight.shape[1] if extra is not None else weight.shape[2]
    columns = width if extra is None else width + LANES
    count = rows // 4
    out_shape = jax.ShapeDtypeStruct((blocks * count, columns), BF16)
    piece = lambda k: pl.BlockSpec((1, count, inner), lambda i, d: (i, d[k], 0))
    in_specs = [piece(k) for k in range(blocks)]
    in_specs.append(pl.BlockSpec((1,) + weight.shape[1:], lambda i, d: (i, 0, 0)))
    operands = [left] * blocks + [weight]
    if extra is not None:
        more = lambda k: pl.BlockSpec((count, LANES), lambda i, d: (d[k], 0))
        in_specs += [more(k) for k in range(blocks)]
        operands += [extra] * blocks
    return pl.pallas_call(
        functools.partial(owner_rows_kernel, extra is not None, blocks),
        out_shape=out_shape,
        grid_spec=pltpu.PrefetchScalarGridSpec(
            num_scalar_prefetch=1,
            grid=(local,),
            in_specs=in_specs,
            out_specs=pl.BlockSpec(out_shape.shape, lambda i, d: (0, 0)),
            scratch_shapes=[pltpu.VMEM((blocks * count, width), F32)],
        ),
        compiler_params=pltpu.CompilerParams(vmem_limit_bytes=58 * 2**20),
        cost_estimate=pl.CostEstimate(flops=1024, bytes_accessed=1024, transcendentals=0),
        name="owner_rows",
    )(devices.astype(jnp.int32), *operands)


def middle_kernel(
    experts_all,
    gain_row,
    parts,
    numbers,
    came,
    cotangent,
    hidden,
    gate_float,
    gains,
    small,
    *refs,
):
    pieces = refs[:parts]
    grad_hidden, pack, grad_mixed, held, sems = refs[parts:]
    copies = fetch(numbers, pieces, held, sems)
    count, width = cotangent.shape
    total = came[0].astype(F32) + came[1].astype(F32)
    gate = gate_float[...]
    gate_grad = total[:, width:].astype(BF16).astype(F32)
    centered = gate_grad - jnp.sum(gate * gate_grad, axis=-1, keepdims=True)
    logit_grad = (gate * centered).astype(BF16)
    grad_normed = total[:, :width] + dot(logit_grad, small[...], NT)
    state = hidden[...]
    recip = lax.rsqrt(jnp.mean(state * state, axis=-1, keepdims=True) + EPSILON)
    plain = state * recip
    scaled = grad_normed * gains[gain_row : gain_row + 1, :]
    gain_grad = jnp.sum(grad_normed * plain, axis=0, keepdims=True)
    back = recip * (scaled - plain * jnp.mean(scaled * plain, axis=-1, keepdims=True))
    grad = cotangent[...].astype(F32) + back
    grad_hidden[...] = grad
    low = grad.astype(BF16)
    first = lax.broadcasted_iota(jnp.int32, (16, width), 0) == 0
    high = gain_grad.astype(BF16).astype(F32)
    for k in range(2):
        pack[k, :count, :width] = low
        pack[k, :count, width:] = logit_grad
        pack[k, count:, :width] = jnp.where(first, high, gain_grad - high).astype(BF16)
        pack[k, count:, width:] = jnp.zeros((16, LANES), BF16)
    wait_all(copies)
    grad_mixed[...] = dot(low, held[...], NT).astype(BF16)


def attend_back_kernel(
    queries, key_rows, values, grad_mixed, bias, cos, sin, grad_project, project
):
    columns = grad_project.shape[2]
    size = H // KV
    length = queries.shape[0]
    scale = HD ** (-0.5)
    wide_bias = jnp.concatenate([bias[...]] * size, axis=1)
    for g in range(KV):
        at = slice(g * HD, (g + 1) * HD)
        q, k, v = heads_of(queries, g), key_rows[:, at], values[:, at]
        upstream = heads_of(grad_mixed, g)
        weights = group_softmax(q, k, wide_bias)
        grad_values = dot(weights.astype(BF16), upstream)
        grad_probs = dot(v, upstream, NT)
        delta = jnp.sum(weights * grad_probs, axis=0, keepdims=True)
        grad_scores = (weights * (grad_probs - delta)).astype(BF16)
        grad_keys = dot(grad_scores, q) * scale
        grad_queries = dot(k.T, grad_scores) * scale
        for j in range(size):
            h = g * size + j
            project[:, h * HD : (h + 1) * HD] = grad_queries[:, j * length : (j + 1) * length].T
        project[:, (H + g) * HD : (H + g + 1) * HD] = grad_keys
        project[:, (H + KV + g) * HD : (H + KV + g + 1) * HD] = grad_values
    c, s = cos[...], -sin[...]
    turns = (H + KV) * HD // LANES
    for t in range(turns):
        at = slice(t * LANES, (t + 1) * LANES)
        tile = rotate_tile(project[:, at], c, s).astype(BF16)
        grad_project[0, :, at] = tile
        grad_project[1, :, at] = tile
    rest = slice(turns * LANES, columns)
    tile = project[:, rest].astype(BF16)
    grad_project[0, :, rest] = tile
    grad_project[1, :, rest] = tile


def attend_back(*operands):
    length = operands[0].shape[0]
    columns = (H + 2 * KV) * HD
    return call(
        attend_back_kernel,
        jax.ShapeDtypeStruct((2, length, columns), BF16),
        [pltpu.VMEM((length, columns), F32)],
        limit=58,
        name="attend_back",
        specs=[VMEM_SPEC] * 7,
    )(*operands)


def input_back_kernel(
    gain_row, parts, numbers, tokens, grad_project, gains, grad_hidden, *refs
):
    pieces = refs[:parts]
    grad_tokens, held, sems = refs[parts:]
    copies = fetch(numbers, pieces, held, sems)
    wait_all(copies)
    grad_normed = dot(grad_project[0], held[...], NT)
    x = tokens[...].astype(F32)
    recip = lax.rsqrt(jnp.mean(x * x, axis=-1, keepdims=True) + EPSILON)
    plain = x * recip
    scaled = grad_normed * gains[gain_row : gain_row + 1, :]
    back = recip * (scaled - plain * jnp.mean(scaled * plain, axis=-1, keepdims=True))
    grad_tokens[...] = grad_hidden[...] + back


def middle(experts_all, gain_row, weight, *operands):
    pieces, numbers = weight
    count, width = operands[1].shape
    shape = lambda *dims, kind=BF16: jax.ShapeDtypeStruct(dims, kind)
    return call(
        functools.partial(middle_kernel, experts_all, gain_row, len(pieces)),
        [
            shape(count, width, kind=F32),
            shape(2, count + 16, width + LANES),
            shape(count, H * HD),
        ],
        [pltpu.VMEM((H * HD, width), BF16), pltpu.SemaphoreType.DMA(numbers.shape)],
        limit=58,
        name="middle",
        specs=[SMEM_SPEC] + [VMEM_SPEC] * 6 + [HBM_SPEC] * len(pieces),
    )(numbers, *operands, *pieces)


def input_back(gain_row, weight, *operands):
    pieces, numbers = weight
    length, width = operands[0].shape
    columns = operands[1].shape[2]
    return call(
        functools.partial(input_back_kernel, gain_row, len(pieces)),
        jax.ShapeDtypeStruct((length, width), F32),
        [pltpu.VMEM((width, columns), BF16), pltpu.SemaphoreType.DMA(numbers.shape)],
        limit=58,
        name="input_back",
        specs=[SMEM_SPEC] + [VMEM_SPEC] * 4 + [HBM_SPEC] * len(pieces),
    )(numbers, *operands, *pieces)


def after(value, *earlier):
    return lax.optimization_barrier((value, earlier))[0]


class Net:
    def __init__(self):
        self.nd = lax.axis_size("dp")
        self.ne = lax.axis_size("expert")
        self.p = lax.axis_index("dp")
        self.e = lax.axis_index("expert")
        self.r = self.place_of(self.p)
        order = list(range(0, self.nd, 2)) + list(range(1, self.nd, 2))[::-1]
        nd, ne = self.nd, self.ne
        self.ring = {
            way: [
                (order[i] * ne + e, order[(i + way) % nd] * ne + e)
                for i in range(nd)
                for e in range(ne)
            ]
            for way in (1, -1)
        }
        self.devices = nd * ne

    def place_of(self, p):
        return jnp.where(p % 2 == 0, p // 2, self.nd - 1 - p // 2)

    def dp_of(self, r):
        r = r % self.nd
        return jnp.where(r < self.nd // 2, 2 * r, 2 * (self.nd - 1 - r) + 1)

    def step(self, value, way):
        return lax.ppermute(value, AXES, self.ring[way])

    def exchange(self, value, bit):
        pairs = [[d, d | 1 << bit] for d in range(self.devices) if not d >> bit & 1]
        return lax.all_to_all(value, AXES, 0, 0, axis_index_groups=pairs, tiled=True)

    def swap(self, value, bit):
        return lax.ppermute(value, AXES, [(d, d ^ bit) for d in range(self.devices)])


def gather_weights(net, first, second, beside):
    half = net.nd // 2
    other_first = net.swap(first, WIDE)
    other_second = net.swap(after(second, other_first), WIDE)
    own = [jnp.stack([first, other_first]), jnp.stack([second, other_second])]
    offsets = [(0,)] + [(-s, s) for s in range(1, half)] + [(half,)]
    parts = [[], []]
    ahead, back = list(own), list(own)
    sent = None
    for s in range(half + 1):
        for k in (0, 1):
            if k == 0 and s == half - 2:
                ahead[k], back[k] = after((ahead[k], back[k]), beside)
            elif sent is not None:
                ahead[k], back[k] = after((ahead[k], back[k]), sent)
            sent = (ahead[k], back[k])
            if s in (0, half):
                parts[k].append((ahead[k] if s == 0 else jnp.stack([ahead[k], back[k]]))[None])
            else:
                parts[k].append(jnp.stack([ahead[k], back[k]]))
            if s + 1 < half:
                ahead[k] = net.step(ahead[k], 1)
                back[k] = net.step(back[k], -1)
            elif s + 1 == half:
                ahead[k] = net.step(ahead[k][0], 1)
                back[k] = net.step(back[k][1], -1)
    def numbers(groups):
        return [
            net.dp_of(net.r + offset) * net.ne + (net.e ^ bits)
            for group in groups
            for bits_of_core in (0, CORE)
            for offset in group
            for bits in (bits_of_core, bits_of_core ^ WIDE)
        ]

    first_pieces = [piece for mine in parts[0] for piece in (mine, net.swap(mine, CORE))]
    mine = jnp.concatenate(parts[1])
    second_pieces = [mine, net.swap(mine, CORE)]
    return (
        as_weight(first_pieces, numbers(offsets)),
        as_weight(second_pieces, numbers([[o for group in offsets for o in group]])),
    )


def as_weight(pieces, numbers):
    rows, columns = pieces[0].shape[2:]
    if rows % 16:
        blocks = jnp.concatenate([piece.reshape(-1, rows, columns) for piece in pieces])
        full = jnp.zeros_like(blocks).at[jnp.stack(numbers)].set(blocks)
        pieces, numbers = [full.reshape(1, 1, -1, columns)], [jnp.zeros((), jnp.int32)]
    return pieces, jnp.stack(numbers).astype(jnp.int32)


def below(arrays, rows, at):
    return jnp.concatenate([r[wide, :rows, at] for r in arrays for wide in (0, 1)], axis=0)


def beside_each_other(left, core, rows):
    order = [2 * wide + c for c in (core, 1 - core) for wide in (0, 1)]
    return jnp.concatenate([left[i, rows, :] for i in order], axis=1)


def project_products_kernel(place, left, earlier, own, other, out):
    depth = out.shape[0]
    first = beside_each_other(left, place[0] % 2, slice(0, depth))
    columns = own.shape[2]
    tile = 4 * LANES
    for start in range(0, columns, tile):
        at = slice(start, start + tile)
        out[:, at] = dot(first, below((own, other), own.shape[1], at)).astype(BF16)
    out[:, columns:] = earlier[...]


def pack_products_kernel(place, left, normed_two, gain, own, other, out):
    depth = out.shape[0]
    count, width = own.shape[1] - 16, own.shape[2] - LANES
    core = place[0] % 2
    second = beside_each_other(left, core, slice(depth, 2 * depth))
    third = beside_each_other(normed_two, core, slice(0, depth))
    tile = 4 * LANES
    for start in range(0, width, tile):
        at = slice(start, start + tile)
        out[:, at] = dot(second, below((own, other), count, at)).astype(BF16)
    rest = dot(third, below((own, other), count, slice(width, width + LANES)))
    out[:, width:] = (rest + gain[...]).astype(BF16)


def weight_products(place, left, pieces, *more):
    columns = pieces[0].shape[2] + (more[0].shape[1] if len(more) == 1 else 0)
    return call(
        pack_products_kernel if len(more) > 1 else project_products_kernel,
        jax.ShapeDtypeStruct((left.shape[1] // 2, columns), BF16),
        limit=58,
        name="weight_products",
        specs=[SMEM_SPEC] + [VMEM_SPEC] * (3 + len(more)),
    )(place, left, *more, *pieces)


def finish_kernel(total, weight, d_qkv, d_out, d_small):
    columns, width = d_qkv.shape[1], d_out.shape[1]
    first = total[:, :columns].astype(F32)
    d_qkv[...] = first
    d_out[...] = total[:, columns : columns + width].astype(F32)
    small = total[:, columns + width :].astype(F32)
    lanes = lax.broadcasted_iota(jnp.int32, small.shape, 1)
    row_sum = jnp.sum(first * weight[...].astype(F32), axis=1, keepdims=True)
    d_small[...] = jnp.where(lanes == LANES - 1, row_sum, small)


def finish(total, weight):
    rows, columns = weight.shape
    shape = lambda n: jax.ShapeDtypeStruct((rows, n), F32)
    return call(
        finish_kernel,
        [shape(columns), shape(total.shape[1] - columns - LANES), shape(LANES)],
        limit=40,
        name="finish",
        specs=[VMEM_SPEC] * 2,
    )(total, weight)


def gain_column_kernel(lane, *refs):
    packs, out = refs[:2], refs[2]
    width = out.shape[0]
    count = packs[0].shape[1] - 16
    rows = sum(r[wide, count : count + 2, :width].astype(F32) for r in packs for wide in (0, 1))
    out[...] = spread_row(jnp.sum(rows, axis=0, keepdims=True), lane, LANES)


def gain_column(lane, packs):
    return call(
        functools.partial(gain_column_kernel, lane),
        jax.ShapeDtypeStruct((packs[0].shape[2] - LANES, LANES), F32),
        limit=58,
        name="gain_column",
        specs=[VMEM_SPEC] * 2,
    )(*packs)


def fold_kernel(came, out):
    for i in range(2):
        out[i, 0] = (came[0, 0, i].astype(F32) + came[1, 0, i].astype(F32)).astype(BF16)


def fold(came, rows):
    columns = came.shape[2]
    came = came.reshape(2, -1, 2, rows, columns)
    count = came.shape[1]
    return pl.pallas_call(
        fold_kernel,
        out_shape=jax.ShapeDtypeStruct((2, count, rows, columns), BF16),
        grid=(count,),
        in_specs=[pl.BlockSpec((2, 1, 2, rows, columns), lambda i: (0, i, 0, 0, 0))],
        out_specs=pl.BlockSpec((2, 1, rows, columns), lambda i: (0, i, 0, 0)),
        compiler_params=pltpu.CompilerParams(vmem_limit_bytes=58 * 2**20),
        cost_estimate=pl.CostEstimate(flops=1024, bytes_accessed=1024, transcendentals=0),
        name="fold",
    )(came).reshape(2, count * rows, columns)


class BlockSum:
    def __init__(self, net, halves, rows):
        self.net, self.halves, self.bit, self.rows = net, halves, 0, rows
        self.count = net.devices.bit_length() - 1

    def send(self, *earlier):
        halves = after(self.halves, *earlier) if earlier else self.halves
        self.came = self.net.exchange(halves, self.bit)
        self.bit += 1

    def add(self, *earlier):
        came = after(self.came, *earlier) if earlier else self.came
        if self.bit == self.count:
            return jnp.sum(came.astype(F32), axis=0)
        self.halves = fold(came, self.rows)
        return self.halves


def in_kernel(last, step, places, turned_rows, grad_pre, *refs):
    came, refs = (refs[:2], refs[2:]) if len(refs) > 10 - last else (None, refs)
    outs, (rows, grads, added, shares, rows_sems, grad_sems, came_sems, out_sems) = (
        refs[: 2 - last],
        refs[2 - last :],
    )
    local = grads.shape[0]
    depth = rows.shape[1]

    def rows_copy(i):
        at = pl.ds(pl.multiple_of(places[step, i] * depth, 16), depth)
        return pltpu.make_async_copy(turned_rows.at[at], rows.at[i], rows_sems.at[i])

    def grad_copy(e):
        return pltpu.make_async_copy(grad_pre.at[e], grads.at[e], grad_sems.at[e])

    def came_copy(i, e):
        return pltpu.make_async_copy(came[i].at[e], added.at[i, e], came_sems.at[i, e])

    def out_copy(i, e):
        if last:
            target = outs[0].at[e, :, pl.ds(i * FE, FE)]
        else:
            target = outs[i].at[e]
        return pltpu.make_async_copy(shares.at[i, e], target, out_sems.at[i, e])

    def begin(e):
        grad_copy(e).start()
        if came is not None:
            for i in range(2):
                came_copy(i, e).start()

    for i in range(2):
        rows_copy(i).start()
    begin(0)
    begin(1)
    for i in range(2):
        rows_copy(i).wait()

    @pl.loop(0, local)
    def _(e):
        @pl.when(e + 2 < local)
        def _():
            begin(e + 2)

        grad_copy(e).wait()
        if came is not None:
            for i in range(2):
                came_copy(i, e).wait()
        for i in range(2):
            share = dot(rows[i], grads[e, :, i * FE : (i + 1) * FE])
            if came is not None:
                share += added[i, e].astype(F32)
            shares[i, e] = share.astype(shares.dtype)
            out_copy(i, e).start()

    @pl.loop(0, local)
    def _(e):
        for i in range(2):
            out_copy(i, e).wait()


def in_share(step, places, turned_rows, grad_pre, came, cost, last=False):
    local, tokens_all, wide = grad_pre.shape
    depth = turned_rows.shape[0] // lax.axis_size("dp")
    kind = F32 if last else BF16
    if last:
        out_shape = [jax.ShapeDtypeStruct((local, depth, wide), kind)]
    else:
        out_shape = [jax.ShapeDtypeStruct((local, depth, FE), kind)] * 2
    return pl.pallas_call(
        functools.partial(in_kernel, int(last), step),
        out_shape=out_shape,
        in_specs=[SMEM_SPEC] + [ANY_SPEC] * (2 + len(came)),
        out_specs=[ANY_SPEC] * len(out_shape),
        scratch_shapes=[
            pltpu.VMEM((2, depth, tokens_all), BF16),
            pltpu.VMEM((local, tokens_all, wide), BF16),
            pltpu.VMEM((2, local, depth, FE), BF16),
            pltpu.VMEM((2, local, depth, FE), kind),
            pltpu.SemaphoreType.DMA((2,)),
            pltpu.SemaphoreType.DMA((local,)),
            pltpu.SemaphoreType.DMA((2, local)),
            pltpu.SemaphoreType.DMA((2, local)),
        ],
        compiler_params=pltpu.CompilerParams(vmem_limit_bytes=58 * 2**20),
        cost_estimate=pl.CostEstimate(flops=cost, bytes_accessed=1024, transcendentals=0),
        name="in_share",
    )(places, turned_rows, grad_pre, *came)


def out_kernel(step, places, turned_act, upstream, *refs):
    came, refs = (refs[:2], refs[2:]) if len(refs) > 10 else (None, refs)
    outs, (rows, ups, added, shares, rows_sems, up_sems, came_sems, out_sems) = refs[:2], refs[2:]
    local, depth, tokens_all = rows.shape[1:]
    half = ups.shape[2]

    def copies(i):
        at = pl.ds(pl.multiple_of(places[step, i] * depth, 16), depth)
        some = [
            pltpu.make_async_copy(turned_act.at[:, at], rows.at[i], rows_sems.at[i]),
            pltpu.make_async_copy(upstream.at[:, pl.ds(i * half, half)], ups.at[i], up_sems.at[i]),
        ]
        if came is not None:
            some.append(pltpu.make_async_copy(came[i], added.at[i], came_sems.at[i]))
        return some

    def out_copy(i):
        return pltpu.make_async_copy(shares.at[i], outs[i], out_sems.at[i])

    for i in range(2):
        for copy in copies(i):
            copy.start()
    for i in range(2):
        for copy in copies(i):
            copy.wait()
        share = dot(rows[i].reshape(local * depth, tokens_all), ups[i])
        if came is not None:
            share += added[i].astype(F32)
        shares[i] = share.astype(shares.dtype)
        out_copy(i).start()
    for i in range(2):
        out_copy(i).wait()


def out_share(step, places, turned_act, upstream_all, came, cost, last=False):
    local, hidden, tokens_all = turned_act.shape
    half = upstream_all.shape[1] // 2
    depth = hidden // lax.axis_size("dp")
    kind = F32 if last else BF16
    return pl.pallas_call(
        functools.partial(out_kernel, step),
        out_shape=[jax.ShapeDtypeStruct((local * depth, half), kind)] * 2,
        in_specs=[SMEM_SPEC] + [ANY_SPEC] * (2 + len(came)),
        out_specs=[ANY_SPEC] * 2,
        scratch_shapes=[
            pltpu.VMEM((2, local, depth, tokens_all), BF16),
            pltpu.VMEM((2, tokens_all, half), BF16),
            pltpu.VMEM((2, local * depth, half), BF16),
            pltpu.VMEM((2, local * depth, half), kind),
        ]
        + [pltpu.SemaphoreType.DMA((2,))] * 4,
        compiler_params=pltpu.CompilerParams(vmem_limit_bytes=58 * 2**20),
        cost_estimate=pl.CostEstimate(flops=cost, bytes_accessed=1024, transcendentals=0),
        name="out_share",
    )(places, turned_act, upstream_all, *came)


def owner_grads_kernel(upstream, weight, out):
    out[0] = dot(upstream[...], weight[0], NT).astype(BF16)


def owner_grads(upstream, weight):
    local, hidden, width = weight.shape
    rows = upstream.shape[0]
    return pl.pallas_call(
        owner_grads_kernel,
        out_shape=jax.ShapeDtypeStruct((local, rows, hidden), BF16),
        grid=(local,),
        in_specs=[
            pl.BlockSpec(upstream.shape, lambda i: (0, 0)),
            pl.BlockSpec((1, hidden, width), lambda i: (i, 0, 0)),
        ],
        out_specs=pl.BlockSpec((1, rows, hidden), lambda i: (i, 0, 0)),
        compiler_params=pltpu.CompilerParams(vmem_limit_bytes=58 * 2**20),
        cost_estimate=pl.CostEstimate(
            flops=2 * local * rows * hidden * width, bytes_accessed=16 * 2**20, transcendentals=0
        ),
        name="owner_grads",
    )(upstream, weight)


def expert_kernel(later, both_scalars, rows_a, rows_b, grad_plain, weight, *refs):
    scalars = [both_scalars[int(later), i] for i in range(3)]
    refs = refs[5 if later else 0 :]
    outs, bufs, (weights, plains, weight_sems, plain_sems, out_sems) = refs[:5], refs[5:10], refs[10:]
    activated, turned_act, grad_pre, gate_grad, turned_rows = bufs
    local, width = weights.shape[:2]
    count = rows_a.shape[0]
    half = pl.ds(pl.multiple_of(scalars[1] * 2 * count, 2 * count), 2 * count)

    def weight_copy(e):
        return pltpu.make_async_copy(weight.at[e], weights.at[e], weight_sems.at[e])

    def plain_copy(e):
        return pltpu.make_async_copy(grad_plain.at[e, half], plains.at[e], plain_sems.at[e])

    def out_copies(e):
        return [
            pltpu.make_async_copy(activated.at[e], outs[0].at[e, half], out_sems.at[0, e]),
            pltpu.make_async_copy(turned_act.at[e], outs[1].at[e, :, half], out_sems.at[1, e]),
            pltpu.make_async_copy(grad_pre.at[e], outs[2].at[e, half], out_sems.at[2, e]),
        ]

    rows_copy = pltpu.make_async_copy(turned_rows, outs[4].at[:, half], out_sems.at[3, 0])
    gate_copy = pltpu.make_async_copy(gate_grad, outs[3].at[half], out_sems.at[3, 1])
    for e in range(2):
        weight_copy(e).start()
        plain_copy(e).start()
    both = (rows_a, rows_b)
    starts = [pl.multiple_of(scalars[2] * count, count), pl.multiple_of((1 - scalars[2]) * count, count)]
    gate_grad[...] = jnp.zeros_like(gate_grad)
    for start, rows in zip(starts, both):
        turned_rows[:, pl.ds(start, count)] = rows[:, :width].T
    rows_copy.start()
    lanes = lax.broadcasted_iota(jnp.int32, (count, LANES), 1)
    tile = 2 * LANES

    @pl.loop(0, local)
    def _(e):
        here = lanes == scalars[0] + e

        @pl.when(e + 2 < local)
        def _():
            weight_copy(e + 2).start()
            plain_copy(e + 2).start()

        weight_copy(e).wait()
        plain_copy(e).wait()
        gates = [
            jnp.sum(jnp.where(here, rows[:, width:].astype(F32), 0.0), axis=1, keepdims=True)
            for rows in both
        ]
        x = jnp.concatenate([rows[:, :width] for rows in both], axis=0)
        sums = [0.0, 0.0]
        for f in range(0, FE, tile):
            g_both = dot(x, weights[e, :, f : f + tile])
            u_both = dot(x, weights[e, :, FE + f : FE + f + tile])
            for i in range(2):
                at = pl.ds(starts[i], count)
                part = slice(i * count, (i + 1) * count)
                g, u, gate = g_both[part], u_both[part], gates[i]
                s = jax.nn.sigmoid(g)
                silu = g * s
                act = silu * u
                plain = plains[e, at, f : f + tile].astype(F32)
                sums[i] += jnp.sum(act * plain, axis=1, keepdims=True)
                low = (act * gate).astype(BF16)
                activated[e, at, f : f + tile] = low
                turned_act[e, f : f + tile, at] = low.T
                da = plain * gate
                grad_pre[e, at, f : f + tile] = (da * u * s * (1.0 + g * (1.0 - s))).astype(BF16)
                grad_pre[e, at, FE + f : FE + f + tile] = (da * silu).astype(BF16)
        for copy in out_copies(e):
            copy.start()
        for i in range(2):
            gate_grad[pl.ds(starts[i], count), :] += jnp.where(here, sums[i], 0.0)

    gate_copy.start()
    rows_copy.wait()
    gate_copy.wait()

    @pl.loop(0, local)
    def _(e):
        for copy in out_copies(e):
            copy.wait()


def expert_half(scalars, rows_a, rows_b, grad_plain, weight, earlier):
    count = 2 * rows_a.shape[0]
    local, width, wide = weight.shape
    total = 2 * count
    out_shape = [
        jax.ShapeDtypeStruct((local, total, FE), BF16),
        jax.ShapeDtypeStruct((local, FE, total), BF16),
        jax.ShapeDtypeStruct((local, total, wide), BF16),
        jax.ShapeDtypeStruct((total, LANES), F32),
        jax.ShapeDtypeStruct((width, total), BF16),
    ]
    return pl.pallas_call(
        functools.partial(expert_kernel, bool(earlier)),
        out_shape=out_shape,
        in_specs=[SMEM_SPEC, VMEM_SPEC, VMEM_SPEC, ANY_SPEC, ANY_SPEC] + [ANY_SPEC] * len(earlier),
        out_specs=[ANY_SPEC] * 5,
        scratch_shapes=[
            pltpu.VMEM((local, count, FE), BF16),
            pltpu.VMEM((local, FE, count), BF16),
            pltpu.VMEM((local, count, wide), BF16),
            pltpu.VMEM((count, LANES), F32),
            pltpu.VMEM((width, count), BF16),
            pltpu.VMEM(weight.shape, BF16),
            pltpu.VMEM((local, count, FE), BF16),
            pltpu.SemaphoreType.DMA((local,)),
            pltpu.SemaphoreType.DMA((local,)),
            pltpu.SemaphoreType.DMA((4, max(local, 2))),
        ],
        input_output_aliases={5 + k: k for k in range(len(earlier))},
        compiler_params=pltpu.CompilerParams(vmem_limit_bytes=58 * 2**20),
        cost_estimate=pl.CostEstimate(
            flops=2 * local * count * width * wide, bytes_accessed=30 * 2**20, transcendentals=0
        ),
        name="expert_half",
    )(scalars, rows_a, rows_b, grad_plain, weight, *earlier)


def on_device(
    tokens,
    cotangent,
    routes,
    segments,
    w_qkv,
    w_out,
    router,
    gain_attn,
    gain_mlp,
    expert_in,
    expert_out,
):
    net = Net()
    length, width = tokens.shape
    local_count = expert_in.shape[0]
    experts_all = local_count * net.ne
    wide_qkv = w_qkv.shape[1]

    small = jnp.concatenate([router, gain_attn[:, None], gain_mlp[:, None]], axis=1)
    small = jnp.pad(small, ((0, 0), (0, LANES - small.shape[1])))
    first_block = jnp.concatenate([w_qkv, small], axis=1)
    upstream_all = lax.all_gather(cotangent, "expert", axis=0, tiled=True)
    grad_act_plain = owner_grads(upstream_all, expert_out)
    qkv_weight, out_weight = gather_weights(net, first_block, w_out, grad_act_plain)
    gain_row = experts_all % 8

    cos, sin = rope_tables(length)
    places_row = jnp.arange(length)
    bias = (
        (places_row[:, None] <= places_row[None, :])
        & (segments[0][:, None] == segments[0][None, :])
    ).astype(F32)
    normed, turned_both, queries, key_rows, values, mixed_heads, gains, small_full = attend(
        experts_all, tokens, bias, cos, sin, qkv_weight
    )
    hidden_state, sent, gate_float = branch(
        gain_row + 1, tokens, mixed_heads, out_weight, small_full, gains, routes
    )
    across_rows = net.swap(sent, WIDE)
    own_rows, beside_rows = sent, net.swap(sent, CORE)
    core, wide = net.e % 2, net.e // 2
    first_expert = net.e * local_count
    scalars = jnp.stack([first_expert, wide, core, first_expert, 1 - wide, core])
    scalars = scalars.reshape(2, 3).astype(jnp.int32)
    early = expert_half(scalars, own_rows, beside_rows, grad_act_plain, expert_in, ())
    across_rows = after(across_rows, early)
    corner_rows = net.swap(across_rows, CORE)
    activated, turned_act, grad_pre, gate_grads, turned_rows = expert_half(
        scalars, across_rows, corner_rows, grad_act_plain, expert_in, early
    )

    steps = jnp.arange(net.nd, dtype=jnp.int32)
    ways = jnp.stack([net.r - 1 - steps, net.r + 1 + steps], axis=1)
    places = jnp.where(steps[:, None] < net.nd - 1, net.dp_of(ways), net.p).astype(jnp.int32)

    def cost(s):
        return 10**10 if s == 4 else 3 * 10**10

    def advance(shares):
        return [net.step(shares[0], 1), net.step(shares[1], -1)]

    came_in, came_out = (), ()

    def ring_in(s, *earlier, beside=None):
        nonlocal came_in
        if earlier:
            came_in = after(came_in, *earlier)
        shares = in_share(s, places, turned_rows, grad_pre, came_in, cost(s))
        if beside is not None:
            shares = after(shares, beside)
        came_in = advance(shares)
        return shares

    def ring_out(s, *earlier, beside=None):
        nonlocal came_out
        if earlier:
            came_out = after(came_out, *earlier)
        shares = out_share(s, places, turned_act, upstream_all, came_out, cost(s))
        if beside is not None:
            shares = after(shares, beside)
        came_out = advance(shares)
        return shares

    def devices(*bits):
        return jnp.stack([net.e ^ bit for bit in bits])

    sent_out = ring_out(0)
    sent_in = ring_in(0, sent_out)
    block = width // net.devices
    lefts = turned_both.reshape(2, net.nd, net.ne, block, length).transpose(2, 0, 1, 3, 4)
    lefts = lax.all_to_all(
        lefts.reshape(net.ne, -1, length), "expert", 0, 0, tiled=True
    )
    beside = owner_rows(devices(1, 3), after(grad_pre, sent_in, lefts), expert_in, gate_grads)
    beside_came = net.swap(beside, CORE)
    sent_out = ring_out(1, beside, beside=beside_came)
    kept = owner_rows(devices(0, 2), after(grad_pre, sent_out), expert_in, gate_grads)
    both = (kept.astype(F32) + beside_came.astype(F32)).astype(BF16)
    both = both.reshape(2, length, -1)
    came = net.exchange(jnp.where(wide == 0, both, both[::-1]), 1)
    sent_in = ring_in(1, both)
    mix = owner_rows(jnp.arange(4), after(activated, sent_in), expert_out)
    sent_out = ring_out(2, mix)
    grad_hidden, pack, grad_mixed = middle(
        experts_all,
        gain_row + 1,
        out_weight,
        after(came, sent_out),
        cotangent,
        hidden_state,
        gate_float,
        gains,
        small_full,
    )
    packs = net.exchange(pack, 1)
    sent_in = ring_in(2, grad_mixed)
    grad_project = attend_back(
        queries, key_rows, values, after(grad_mixed, sent_in), bias, cos, sin
    )
    projects = net.exchange(grad_project, 1)
    sent_out = ring_out(3, grad_project)
    packs = after(packs, sent_out, came_in)
    packs = (packs, net.swap(packs, CORE))
    sent_in = ring_in(3, sent_out, packs[0], beside=packs[1])
    mine = lambda rows: lax.dynamic_index_in_dim(
        rows.reshape(net.nd, net.ne, block, -1), net.e, 1, keepdims=False
    ).reshape(net.nd * block, -1)
    normed_two = mine(turned_rows).reshape(-1, net.ne, length).transpose(1, 0, 2)
    place = net.e.astype(jnp.int32).reshape(1)
    out_products = weight_products(
        place,
        after(lefts, sent_in),
        packs,
        normed_two,
        mine(gain_column(experts_all, packs)),
    )
    sent_out = ring_out(4, out_products)
    projects = after(projects, sent_out, came_in)
    projects = (projects, net.swap(projects, CORE))
    sent_in = ring_in(4, projects[0], beside=projects[1])
    products = weight_products(place, after(lefts, sent_in), projects, out_products)
    sent_out = ring_out(5, products)
    d_all = lax.psum_scatter(after(products, sent_out), "dp", scatter_dimension=0, tiled=True)
    sent_in = ring_in(5, sent_out)
    mix_all = lax.all_to_all(after(mix, sent_in), "expert", 0, 0, tiled=True)
    for s in range(6, net.nd - 1):
        sent_out = ring_out(s, sent_in)
        sent_in = ring_in(s, sent_out)
    grad_tokens = input_back(
        gain_row, qkv_weight, tokens, after(grad_project, sent_in), gains, grad_hidden
    )
    mixture = jnp.sum(mix_all.reshape(net.ne, length, width).astype(F32), axis=0)
    activations = (hidden_state + mixture).astype(BF16)
    d_expert_out = jnp.concatenate(
        out_share(
            net.nd - 1, places, turned_act, upstream_all, after(came_out, grad_tokens), cost(net.nd), last=True
        ),
        axis=1,
    ).reshape(local_count, FE // net.nd, width)
    (d_expert_in,) = in_share(
        net.nd - 1, places, turned_rows, grad_pre, after(came_in, d_expert_out, activations), cost(net.nd), last=True
    )
    d_qkv, d_out, d_small = finish(after(d_all, d_expert_in), w_qkv)
    d_gain_first = d_small[:, LANES - 1] / gain_attn.astype(F32)
    return (
        activations,
        grad_tokens,
        d_qkv,
        d_out,
        d_small[:, :experts_all],
        d_gain_first,
        d_small[:, experts_all],
        d_expert_in,
        d_expert_out,
    )


def solution(mesh):
    rows = P(AXES, None)
    return jax.shard_map(
        on_device,
        mesh=mesh,
        in_specs=(rows,) * 7
        + (P(AXES), P(AXES), P("expert", None, None), P("expert", None, None)),
        out_specs=(rows,) * 5
        + (P(AXES), P(AXES), P("expert", "dp", None), P("expert", "dp", None)),
        check_vma=False,
    )
```

```python
import functools

import jax
import jax.numpy as jnp
from jax import lax
from jax.experimental import pallas as pl
from jax.experimental.pallas import tpu as pltpu
from jax.sharding import PartitionSpec as P

H = 24
KV = 8
HD = 64
FE = 512
TOP = 8

EPSILON = 1e-06
THETA = 10000.0
NEGATIVE = -1e30
AXES = ("dp", "expert")
CORE, WIDE = 1, 2
LANES = 128

F32 = jnp.float32
BF16 = jnp.bfloat16


def rope_tables(length):
    half_size = HD // 2
    frequency = THETA ** (-(jnp.arange(half_size, dtype=F32) * 2.0) / HD)
    angles = jnp.arange(length, dtype=F32)[:, None] * frequency[None, :]
    cos, sin = jnp.cos(angles), jnp.sin(angles)
    return (
        jnp.concatenate([cos] * (LANES // half_size), axis=1),
        jnp.concatenate([-sin, sin] * (LANES // HD), axis=1),
    )


def rotate_tile(tile, cos, sin):
    half_size = HD // 2
    lane = lax.broadcasted_iota(jnp.int32, tile.shape, 1)
    ahead = pltpu.roll(tile, LANES - half_size, 1)
    back = pltpu.roll(tile, half_size, 1)
    return tile * cos + jnp.where(lane % HD < half_size, ahead, back) * sin


def dot(left, right, dims=((1,), (0,))):
    return lax.dot_general(left, right, (dims, ((), ())), preferred_element_type=F32)


NT = ((1,), (1,))


def spread_row(row, lane, count):
    at = lax.broadcasted_iota(jnp.int32, (count, row.shape[1]), 0) == lane
    return jnp.where(at, jnp.broadcast_to(row, at.shape), 0.0).T


def call(kernel, out_shape, scratch=(), limit=40, name=None, specs=None, aliases=None):
    vmem = pl.BlockSpec(memory_space=pltpu.VMEM)
    return pl.pallas_call(
        kernel,
        out_shape=out_shape,
        in_specs=specs,
        out_specs=jax.tree.map(lambda _: vmem, out_shape),
        scratch_shapes=scratch,
        compiler_params=pltpu.CompilerParams(vmem_limit_bytes=limit * 2**20),
        cost_estimate=pl.CostEstimate(flops=1024, bytes_accessed=1024, transcendentals=0),
        name=name,
    )


VMEM_SPEC = pl.BlockSpec(memory_space=pltpu.VMEM)
SMEM_SPEC = pl.BlockSpec(memory_space=pltpu.SMEM)
ANY_SPEC = pl.BlockSpec(memory_space=pl.ANY)
HBM_SPEC = pl.BlockSpec(memory_space=pltpu.HBM)


def fetch(numbers, pieces, held, sems):
    columns = held.shape[1]
    copies = []
    for piece in pieces:
        places, wides, rows, wide = piece.shape
        for j in range(places):
            for w in range(wides):
                k = len(copies)
                source = piece.at[j, w]
                if columns < wide:
                    source = source.at[:, pl.ds(0, columns)]
                at = pl.ds(pl.multiple_of(numbers[k] * rows, 16), rows)
                copies.append(pltpu.make_async_copy(source, held.at[at], sems.at[k]))
    for copy in copies:
        copy.start()
    return copies


def wait_all(copies):
    for copy in copies:
        copy.wait()


def heads_of(array, group):
    size = H // KV
    first = group * size
    return jnp.concatenate(
        [array[:, h * HD : (h + 1) * HD] for h in range(first, first + size)], axis=0
    )


def group_softmax(queries, keys, bias):
    scores = dot(keys, queries, NT) * HD ** (-0.5)
    scores = jnp.where(bias > 0.0, scores, NEGATIVE)
    exponent = jnp.exp(scores - jnp.max(scores, axis=0, keepdims=True))
    return exponent * (1.0 / jnp.sum(exponent, axis=0, keepdims=True))


def attend_kernel(experts_all, count, numbers, tokens, bias, cos, sin, *refs):
    pieces = refs[:count]
    normed, turned_both, queries, key_rows, values, mixed, gains, small = refs[count : count + 8]
    project, held, sems = refs[count + 8 :]
    copies = fetch(numbers, pieces, held, sems)
    columns = held.shape[1]
    wide = columns - LANES
    x = tokens[...].astype(F32)
    plain = x * lax.rsqrt(jnp.mean(x * x, axis=-1, keepdims=True) + EPSILON)
    wait_all(copies)
    small[...] = held[:, wide:]
    turned = held[:, wide:].astype(F32).T
    gains[...] = turned[experts_all // 8 * 8 : experts_all // 8 * 8 + 16]
    row = experts_all
    low = (plain * turned[row : row + 1]).astype(BF16)
    normed[...] = low
    width = tokens.shape[1]
    turned_both[:width, :] = low.T
    tile = 4 * LANES
    for start in range(0, wide, tile):
        at = slice(start, min(start + tile, wide))
        project[:, at] = dot(low, held[:, at])
    c, s = cos[...], sin[...]
    for t in range(H * HD // LANES):
        at = slice(t * LANES, (t + 1) * LANES)
        queries[:, at] = rotate_tile(project[:, at], c, s).astype(BF16)
    for t in range(KV * HD // LANES):
        at = slice(t * LANES, (t + 1) * LANES)
        from_ = slice(H * HD + t * LANES, H * HD + (t + 1) * LANES)
        key_rows[:, at] = rotate_tile(project[:, from_], c, s).astype(BF16)
    values[...] = project[:, (H + KV) * HD : (H + 2 * KV) * HD].astype(BF16)
    size = H // KV
    length = tokens.shape[0]
    wide_bias = jnp.concatenate([bias[...]] * size, axis=1)
    for g in range(KV):
        at = slice(g * HD, (g + 1) * HD)
        probs = group_softmax(heads_of(queries, g), key_rows[:, at], wide_bias).astype(BF16)
        out = dot(values[:, at].T, probs)
        for j in range(size):
            h = g * size + j
            head = out[:, j * length : (j + 1) * length]
            mixed[:, h * HD : (h + 1) * HD] = head.T.astype(BF16)
            turned_both[width + h * HD : width + (h + 1) * HD, :] = head.astype(BF16)


def attend(experts_all, tokens, bias, cos, sin, weight):
    pieces, numbers = weight
    length, width = tokens.shape
    columns = pieces[0].shape[3]
    shape = lambda *dims, kind=BF16: jax.ShapeDtypeStruct(dims, kind)
    out_shape = [
        shape(length, width),
        shape(width + H * HD, length),
        shape(length, H * HD),
        shape(length, KV * HD),
        shape(length, KV * HD),
        shape(length, H * HD),
        shape(16, width, kind=F32),
        shape(width, LANES),
    ]
    scratch = [
        pltpu.VMEM((length, columns - LANES), F32),
        pltpu.VMEM((width, columns), BF16),
        pltpu.SemaphoreType.DMA(numbers.shape),
    ]
    return call(
        functools.partial(attend_kernel, experts_all, len(pieces)),
        out_shape,
        scratch,
        limit=58,
        name="attend",
        specs=[SMEM_SPEC] + [VMEM_SPEC] * 4 + [HBM_SPEC] * len(pieces),
    )(numbers, tokens, bias, cos, sin, *pieces)


def branch_kernel(gain_row, count, numbers, tokens, mixed, small, gains, routes, *refs):
    pieces = refs[:count]
    hidden, sent, gate_float = refs[count : count + 3]
    held, sems = refs[count + 3 :]
    copies = fetch(numbers, pieces, held, sems)
    width = tokens.shape[1]
    wait_all(copies)
    state = tokens[...].astype(F32) + dot(mixed[...], held[...])
    hidden[...] = state
    recip = lax.rsqrt(jnp.mean(state * state, axis=-1, keepdims=True) + EPSILON)
    low = (state * recip * gains[gain_row : gain_row + 1, :]).astype(BF16)
    sent[:, :width] = low
    logits = dot(low, small[...])
    lanes = lax.broadcasted_iota(jnp.int32, logits.shape, 1)
    chosen = lanes < 0
    for j in range(routes.shape[1]):
        chosen = chosen | (lanes == routes[:, j : j + 1])
    picked = jnp.where(chosen, logits, NEGATIVE)
    exponent = jnp.where(chosen, jnp.exp(picked - jnp.max(picked, axis=-1, keepdims=True)), 0.0)
    gate = exponent / jnp.sum(exponent, axis=-1, keepdims=True)
    gate_float[...] = gate
    sent[:, width:] = gate.astype(BF16)


def branch(gain_row, tokens, mixed, weight, small, gains, routes):
    pieces, numbers = weight
    length, width = tokens.shape
    shape = lambda *dims, kind=BF16: jax.ShapeDtypeStruct(dims, kind)
    return call(
        functools.partial(branch_kernel, gain_row, len(pieces)),
        [
            shape(length, width, kind=F32),
            shape(length, width + LANES),
            shape(length, LANES, kind=F32),
        ],
        [pltpu.VMEM((mixed.shape[1], width), BF16), pltpu.SemaphoreType.DMA(numbers.shape)],
        limit=58,
        name="branch",
        specs=[SMEM_SPEC] + [VMEM_SPEC] * 5 + [HBM_SPEC] * len(pieces),
    )(numbers, tokens, mixed, small, gains, routes, *pieces)


def owner_rows_kernel(extra_given, blocks, *refs):
    refs = refs[1:]
    left, weight = refs[:blocks], refs[blocks]
    extra = refs[blocks + 1 : 2 * blocks + 1] if extra_given else None
    outs, total = refs[-1 - (2 if extra_given else 1) : -1], refs[-1]
    expert = pl.program_id(0)
    count = left[0].shape[1]
    width = total.shape[1]
    dims = NT if extra_given else ((1,), (0,))
    share = dot(jnp.concatenate([a[0] for a in left], axis=0), weight[0], dims)

    @pl.when(expert == 0)
    def _():
        total[...] = share

    @pl.when(expert > 0)
    def _():
        total[...] += share

    @pl.when(expert == pl.num_programs(0) - 1)
    def _():
        each = blocks // len(outs)
        for i in range(blocks):
            out, at = outs[i // each], slice(i % each * count, (i % each + 1) * count)
            out[at, :width] = total[i * count : (i + 1) * count].astype(BF16)
            if extra_given:
                out[at, width:] = extra[i][...].astype(BF16)


def owner_rows(devices, left, weight, extra=None):
    blocks = devices.shape[0]
    local, rows, inner = left.shape
    width = weight.shape[1] if extra is not None else weight.shape[2]
    columns = width if extra is None else width + LANES
    count = rows // 4
    parts = 1 if extra is None else 2
    out_shape = [jax.ShapeDtypeStruct((blocks // parts * count, columns), BF16)] * parts
    piece = lambda k: pl.BlockSpec((1, count, inner), lambda i, d: (i, d[k], 0))
    in_specs = [piece(k) for k in range(blocks)]
    in_specs.append(pl.BlockSpec((1,) + weight.shape[1:], lambda i, d: (i, 0, 0)))
    operands = [left] * blocks + [weight]
    if extra is not None:
        more = lambda k: pl.BlockSpec((count, LANES), lambda i, d: (d[k], 0))
        in_specs += [more(k) for k in range(blocks)]
        operands += [extra] * blocks
    return pl.pallas_call(
        functools.partial(owner_rows_kernel, extra is not None, blocks),
        out_shape=out_shape,
        grid_spec=pltpu.PrefetchScalarGridSpec(
            num_scalar_prefetch=1,
            grid=(local,),
            in_specs=in_specs,
            out_specs=[pl.BlockSpec(o.shape, lambda i, d: (0, 0)) for o in out_shape],
            scratch_shapes=[pltpu.VMEM((blocks * count, width), F32)],
        ),
        compiler_params=pltpu.CompilerParams(vmem_limit_bytes=58 * 2**20),
        cost_estimate=pl.CostEstimate(flops=1024, bytes_accessed=1024, transcendentals=0),
        name="owner_rows",
    )(devices.astype(jnp.int32), *operands)


def middle_kernel(
    experts_all,
    gain_row,
    parts,
    numbers,
    came,
    cotangent,
    hidden,
    gate_float,
    gains,
    small,
    *refs,
):
    pieces = refs[:parts]
    grad_hidden, pack, grad_mixed, held, sems = refs[parts:]
    copies = fetch(numbers, pieces, held, sems)
    count, width = cotangent.shape
    total = came[0].astype(F32) + came[1].astype(F32)
    gate = gate_float[...]
    gate_grad = total[:, width:].astype(BF16).astype(F32)
    centered = gate_grad - jnp.sum(gate * gate_grad, axis=-1, keepdims=True)
    logit_grad = (gate * centered).astype(BF16)
    grad_normed = total[:, :width] + dot(logit_grad, small[...], NT)
    state = hidden[...]
    recip = lax.rsqrt(jnp.mean(state * state, axis=-1, keepdims=True) + EPSILON)
    plain = state * recip
    scaled = grad_normed * gains[gain_row : gain_row + 1, :]
    gain_grad = jnp.sum(grad_normed * plain, axis=0, keepdims=True)
    back = recip * (scaled - plain * jnp.mean(scaled * plain, axis=-1, keepdims=True))
    grad = cotangent[...].astype(F32) + back
    grad_hidden[...] = grad
    low = grad.astype(BF16)
    first = lax.broadcasted_iota(jnp.int32, (16, width), 0) == 0
    high = gain_grad.astype(BF16).astype(F32)
    for k in range(2):
        pack[k, :count, :width] = low
        pack[k, :count, width:] = logit_grad
        pack[k, count:, :width] = jnp.where(first, high, gain_grad - high).astype(BF16)
        pack[k, count:, width:] = jnp.zeros((16, LANES), BF16)
    wait_all(copies)
    grad_mixed[...] = dot(low, held[...], NT).astype(BF16)


def attend_back_kernel(
    queries, key_rows, values, grad_mixed, bias, cos, sin, grad_project, project
):
    columns = grad_project.shape[2]
    size = H // KV
    length = queries.shape[0]
    scale = HD ** (-0.5)
    wide_bias = jnp.concatenate([bias[...]] * size, axis=1)
    for g in range(KV):
        at = slice(g * HD, (g + 1) * HD)
        q, k, v = heads_of(queries, g), key_rows[:, at], values[:, at]
        upstream = heads_of(grad_mixed, g)
        weights = group_softmax(q, k, wide_bias)
        grad_values = dot(weights.astype(BF16), upstream)
        grad_probs = dot(v, upstream, NT)
        delta = jnp.sum(weights * grad_probs, axis=0, keepdims=True)
        grad_scores = (weights * (grad_probs - delta)).astype(BF16)
        grad_keys = dot(grad_scores, q) * scale
        grad_queries = dot(k.T, grad_scores) * scale
        for j in range(size):
            h = g * size + j
            project[:, h * HD : (h + 1) * HD] = grad_queries[:, j * length : (j + 1) * length].T
        project[:, (H + g) * HD : (H + g + 1) * HD] = grad_keys
        project[:, (H + KV + g) * HD : (H + KV + g + 1) * HD] = grad_values
    c, s = cos[...], -sin[...]
    turns = (H + KV) * HD // LANES
    for t in range(turns):
        at = slice(t * LANES, (t + 1) * LANES)
        tile = rotate_tile(project[:, at], c, s).astype(BF16)
        grad_project[0, :, at] = tile
        grad_project[1, :, at] = tile
    rest = slice(turns * LANES, columns)
    tile = project[:, rest].astype(BF16)
    grad_project[0, :, rest] = tile
    grad_project[1, :, rest] = tile


def attend_back(*operands):
    length = operands[0].shape[0]
    columns = (H + 2 * KV) * HD
    return call(
        attend_back_kernel,
        jax.ShapeDtypeStruct((2, length, columns), BF16),
        [pltpu.VMEM((length, columns), F32)],
        limit=58,
        name="attend_back",
        specs=[VMEM_SPEC] * 7,
    )(*operands)


def input_back_kernel(
    gain_row, parts, numbers, tokens, grad_project, gains, grad_hidden, *refs
):
    pieces = refs[:parts]
    grad_tokens, held, sems = refs[parts:]
    copies = fetch(numbers, pieces, held, sems)
    wait_all(copies)
    grad_normed = dot(grad_project[0], held[...], NT)
    x = tokens[...].astype(F32)
    recip = lax.rsqrt(jnp.mean(x * x, axis=-1, keepdims=True) + EPSILON)
    plain = x * recip
    scaled = grad_normed * gains[gain_row : gain_row + 1, :]
    back = recip * (scaled - plain * jnp.mean(scaled * plain, axis=-1, keepdims=True))
    grad_tokens[...] = grad_hidden[...] + back


def middle(experts_all, gain_row, weight, *operands):
    pieces, numbers = weight
    count, width = operands[1].shape
    shape = lambda *dims, kind=BF16: jax.ShapeDtypeStruct(dims, kind)
    return call(
        functools.partial(middle_kernel, experts_all, gain_row, len(pieces)),
        [
            shape(count, width, kind=F32),
            shape(2, count + 16, width + LANES),
            shape(count, H * HD),
        ],
        [pltpu.VMEM((H * HD, width), BF16), pltpu.SemaphoreType.DMA(numbers.shape)],
        limit=58,
        name="middle",
        specs=[SMEM_SPEC] + [VMEM_SPEC] * 6 + [HBM_SPEC] * len(pieces),
    )(numbers, *operands, *pieces)


def input_back(gain_row, weight, *operands):
    pieces, numbers = weight
    length, width = operands[0].shape
    columns = operands[1].shape[2]
    return call(
        functools.partial(input_back_kernel, gain_row, len(pieces)),
        jax.ShapeDtypeStruct((length, width), F32),
        [pltpu.VMEM((width, columns), BF16), pltpu.SemaphoreType.DMA(numbers.shape)],
        limit=58,
        name="input_back",
        specs=[SMEM_SPEC] + [VMEM_SPEC] * 4 + [HBM_SPEC] * len(pieces),
    )(numbers, *operands, *pieces)


def after(value, *earlier):
    return lax.optimization_barrier((value, earlier))[0]


class Net:
    def __init__(self):
        self.nd = lax.axis_size("dp")
        self.ne = lax.axis_size("expert")
        self.p = lax.axis_index("dp")
        self.e = lax.axis_index("expert")
        self.r = self.place_of(self.p)
        order = list(range(0, self.nd, 2)) + list(range(1, self.nd, 2))[::-1]
        nd, ne = self.nd, self.ne
        self.ring = {
            way: [
                (order[i] * ne + e, order[(i + way) % nd] * ne + e)
                for i in range(nd)
                for e in range(ne)
            ]
            for way in (1, -1)
        }
        self.devices = nd * ne

    def place_of(self, p):
        return jnp.where(p % 2 == 0, p // 2, self.nd - 1 - p // 2)

    def dp_of(self, r):
        r = r % self.nd
        return jnp.where(r < self.nd // 2, 2 * r, 2 * (self.nd - 1 - r) + 1)

    def step(self, value, way):
        return lax.ppermute(value, AXES, self.ring[way])

    def exchange(self, value, bit):
        pairs = [[d, d | 1 << bit] for d in range(self.devices) if not d >> bit & 1]
        return lax.all_to_all(value, AXES, 0, 0, axis_index_groups=pairs, tiled=True)

    def swap(self, value, bit):
        return lax.ppermute(value, AXES, [(d, d ^ bit) for d in range(self.devices)])


def gather_weights(net, first, second, beside):
    half = net.nd // 2
    other_first = net.swap(first, WIDE)
    other_second = net.swap(after(second, other_first), WIDE)
    own = [jnp.stack([first, other_first]), jnp.stack([second, other_second])]
    offsets = [(0,)] + [(-s, s) for s in range(1, half)] + [(half,)]
    parts = [[], []]
    ahead, back = list(own), list(own)
    sent = None
    for s in range(half + 1):
        for k in (0, 1):
            if k == 0 and s == half - 2:
                ahead[k], back[k] = after((ahead[k], back[k]), beside)
            elif sent is not None:
                ahead[k], back[k] = after((ahead[k], back[k]), sent)
            sent = (ahead[k], back[k])
            if s in (0, half):
                parts[k].append((ahead[k] if s == 0 else jnp.stack([ahead[k], back[k]]))[None])
            else:
                parts[k].append(jnp.stack([ahead[k], back[k]]))
            if s + 1 < half:
                ahead[k] = net.step(ahead[k], 1)
                back[k] = net.step(back[k], -1)
            elif s + 1 == half:
                ahead[k] = net.step(ahead[k][0], 1)
                back[k] = net.step(back[k][1], -1)
    def numbers(groups):
        return [
            net.dp_of(net.r + offset) * net.ne + (net.e ^ bits)
            for group in groups
            for bits_of_core in (0, CORE)
            for offset in group
            for bits in (bits_of_core, bits_of_core ^ WIDE)
        ]

    first_pieces = [piece for mine in parts[0] for piece in (mine, net.swap(mine, CORE))]
    mine = jnp.concatenate(parts[1])
    second_pieces = [mine, net.swap(mine, CORE)]
    return (
        as_weight(first_pieces, numbers(offsets)),
        as_weight(second_pieces, numbers([[o for group in offsets for o in group]])),
    )


def as_weight(pieces, numbers):
    rows, columns = pieces[0].shape[2:]
    if rows % 16:
        blocks = jnp.concatenate([piece.reshape(-1, rows, columns) for piece in pieces])
        full = jnp.zeros_like(blocks).at[jnp.stack(numbers)].set(blocks)
        pieces, numbers = [full.reshape(1, 1, -1, columns)], [jnp.zeros((), jnp.int32)]
    return pieces, jnp.stack(numbers).astype(jnp.int32)


def below(arrays, rows, at):
    return jnp.concatenate([r[wide, :rows, at] for r in arrays for wide in (0, 1)], axis=0)


def beside_each_other(left, core, rows):
    order = [2 * wide + c for c in (core, 1 - core) for wide in (0, 1)]
    return jnp.concatenate([left[i, rows, :] for i in order], axis=1)


def project_products_kernel(place, left, earlier, own, other, out):
    depth = out.shape[0]
    first = beside_each_other(left, place[0] % 2, slice(0, depth))
    columns = own.shape[2]
    tile = 4 * LANES
    for start in range(0, columns, tile):
        at = slice(start, start + tile)
        out[:, at] = dot(first, below((own, other), own.shape[1], at)).astype(BF16)
    out[:, columns:] = earlier[...]


def pack_products_kernel(place, left, normed_two, gain, own, other, out):
    depth = out.shape[0]
    count, width = own.shape[1] - 16, own.shape[2] - LANES
    core = place[0] % 2
    second = beside_each_other(left, core, slice(depth, 2 * depth))
    third = beside_each_other(normed_two, core, slice(0, depth))
    tile = 4 * LANES
    for start in range(0, width, tile):
        at = slice(start, start + tile)
        out[:, at] = dot(second, below((own, other), count, at)).astype(BF16)
    rest = dot(third, below((own, other), count, slice(width, width + LANES)))
    out[:, width:] = (rest + gain[...]).astype(BF16)


def weight_products(place, left, pieces, *more):
    columns = pieces[0].shape[2] + (more[0].shape[1] if len(more) == 1 else 0)
    return call(
        pack_products_kernel if len(more) > 1 else project_products_kernel,
        jax.ShapeDtypeStruct((left.shape[1] // 2, columns), BF16),
        limit=58,
        name="weight_products",
        specs=[SMEM_SPEC] + [VMEM_SPEC] * (3 + len(more)),
    )(place, left, *more, *pieces)


def finish_kernel(total, weight, d_qkv, d_out, d_small):
    columns, width = d_qkv.shape[1], d_out.shape[1]
    first = total[:, :columns].astype(F32)
    d_qkv[...] = first
    d_out[...] = total[:, columns : columns + width].astype(F32)
    small = total[:, columns + width :].astype(F32)
    lanes = lax.broadcasted_iota(jnp.int32, small.shape, 1)
    row_sum = jnp.sum(first * weight[...].astype(F32), axis=1, keepdims=True)
    d_small[...] = jnp.where(lanes == LANES - 1, row_sum, small)


def finish(total, weight):
    rows, columns = weight.shape
    shape = lambda n: jax.ShapeDtypeStruct((rows, n), F32)
    return call(
        finish_kernel,
        [shape(columns), shape(total.shape[1] - columns - LANES), shape(LANES)],
        limit=40,
        name="finish",
        specs=[VMEM_SPEC] * 2,
    )(total, weight)


def gain_column_kernel(lane, *refs):
    packs, out = refs[:2], refs[2]
    width = out.shape[0]
    count = packs[0].shape[1] - 16
    rows = sum(r[wide, count : count + 2, :width].astype(F32) for r in packs for wide in (0, 1))
    out[...] = spread_row(jnp.sum(rows, axis=0, keepdims=True), lane, LANES)


def gain_column(lane, packs):
    return call(
        functools.partial(gain_column_kernel, lane),
        jax.ShapeDtypeStruct((packs[0].shape[2] - LANES, LANES), F32),
        limit=58,
        name="gain_column",
        specs=[VMEM_SPEC] * 2,
    )(*packs)


def fold_kernel(came, out):
    for i in range(2):
        out[i, 0] = (came[0, 0, i].astype(F32) + came[1, 0, i].astype(F32)).astype(BF16)


def fold(came, rows):
    columns = came.shape[2]
    came = came.reshape(2, -1, 2, rows, columns)
    count = came.shape[1]
    return pl.pallas_call(
        fold_kernel,
        out_shape=jax.ShapeDtypeStruct((2, count, rows, columns), BF16),
        grid=(count,),
        in_specs=[pl.BlockSpec((2, 1, 2, rows, columns), lambda i: (0, i, 0, 0, 0))],
        out_specs=pl.BlockSpec((2, 1, rows, columns), lambda i: (0, i, 0, 0)),
        compiler_params=pltpu.CompilerParams(vmem_limit_bytes=58 * 2**20),
        cost_estimate=pl.CostEstimate(flops=1024, bytes_accessed=1024, transcendentals=0),
        name="fold",
    )(came).reshape(2, count * rows, columns)


class BlockSum:
    def __init__(self, net, halves, rows):
        self.net, self.halves, self.bit, self.rows = net, halves, 0, rows
        self.count = net.devices.bit_length() - 1

    def send(self, *earlier):
        halves = after(self.halves, *earlier) if earlier else self.halves
        self.came = self.net.exchange(halves, self.bit)
        self.bit += 1

    def add(self, *earlier):
        came = after(self.came, *earlier) if earlier else self.came
        if self.bit == self.count:
            return jnp.sum(came.astype(F32), axis=0)
        self.halves = fold(came, self.rows)
        return self.halves


def in_kernel(last, step, places, turned_rows, grad_pre, *refs):
    came, refs = (refs[:2], refs[2:]) if len(refs) > 10 - last else (None, refs)
    outs, (rows, grads, added, shares, rows_sems, grad_sems, came_sems, out_sems) = (
        refs[: 2 - last],
        refs[2 - last :],
    )
    local = grads.shape[0]
    depth = rows.shape[1]

    def rows_copy(i):
        at = pl.ds(pl.multiple_of(places[step, i] * depth, 16), depth)
        return pltpu.make_async_copy(turned_rows.at[at], rows.at[i], rows_sems.at[i])

    def grad_copy(e):
        return pltpu.make_async_copy(grad_pre.at[e], grads.at[e], grad_sems.at[e])

    def came_copy(i, e):
        return pltpu.make_async_copy(came[i].at[e], added.at[i, e], came_sems.at[i, e])

    def out_copy(i, e):
        if last:
            target = outs[0].at[e, :, pl.ds(i * FE, FE)]
        else:
            target = outs[i].at[e]
        return pltpu.make_async_copy(shares.at[i, e], target, out_sems.at[i, e])

    def begin(e):
        grad_copy(e).start()
        if came is not None:
            for i in range(2):
                came_copy(i, e).start()

    for i in range(2):
        rows_copy(i).start()
    begin(0)
    begin(1)
    for i in range(2):
        rows_copy(i).wait()

    @pl.loop(0, local)
    def _(e):
        @pl.when(e + 2 < local)
        def _():
            begin(e + 2)

        grad_copy(e).wait()
        if came is not None:
            for i in range(2):
                came_copy(i, e).wait()
        for i in range(2):
            share = dot(rows[i], grads[e, :, i * FE : (i + 1) * FE])
            if came is not None:
                share += added[i, e].astype(F32)
            shares[i, e] = share.astype(shares.dtype)
            out_copy(i, e).start()

    @pl.loop(0, local)
    def _(e):
        for i in range(2):
            out_copy(i, e).wait()


def in_share(step, places, turned_rows, grad_pre, came, cost, last=False):
    local, tokens_all, wide = grad_pre.shape
    depth = turned_rows.shape[0] // lax.axis_size("dp")
    kind = F32 if last else BF16
    if last:
        out_shape = [jax.ShapeDtypeStruct((local, depth, wide), kind)]
    else:
        out_shape = [jax.ShapeDtypeStruct((local, depth, FE), kind)] * 2
    return pl.pallas_call(
        functools.partial(in_kernel, int(last), step),
        out_shape=out_shape,
        in_specs=[SMEM_SPEC] + [ANY_SPEC] * (2 + len(came)),
        out_specs=[ANY_SPEC] * len(out_shape),
        scratch_shapes=[
            pltpu.VMEM((2, depth, tokens_all), BF16),
            pltpu.VMEM((local, tokens_all, wide), BF16),
            pltpu.VMEM((2, local, depth, FE), BF16),
            pltpu.VMEM((2, local, depth, FE), kind),
            pltpu.SemaphoreType.DMA((2,)),
            pltpu.SemaphoreType.DMA((local,)),
            pltpu.SemaphoreType.DMA((2, local)),
            pltpu.SemaphoreType.DMA((2, local)),
        ],
        compiler_params=pltpu.CompilerParams(vmem_limit_bytes=58 * 2**20),
        cost_estimate=pl.CostEstimate(flops=cost, bytes_accessed=1024, transcendentals=0),
        name="in_share",
    )(places, turned_rows, grad_pre, *came)


def out_kernel(step, places, turned_act, upstream, *refs):
    came, refs = (refs[:2], refs[2:]) if len(refs) > 10 else (None, refs)
    outs, (rows, ups, added, shares, rows_sems, up_sems, came_sems, out_sems) = refs[:2], refs[2:]
    local, depth, tokens_all = rows.shape[1:]
    half = ups.shape[2]

    def copies(i):
        at = pl.ds(pl.multiple_of(places[step, i] * depth, 16), depth)
        some = [
            pltpu.make_async_copy(turned_act.at[:, at], rows.at[i], rows_sems.at[i]),
            pltpu.make_async_copy(upstream.at[:, pl.ds(i * half, half)], ups.at[i], up_sems.at[i]),
        ]
        if came is not None:
            some.append(pltpu.make_async_copy(came[i], added.at[i], came_sems.at[i]))
        return some

    def out_copy(i):
        return pltpu.make_async_copy(shares.at[i], outs[i], out_sems.at[i])

    for i in range(2):
        for copy in copies(i):
            copy.start()
    for i in range(2):
        for copy in copies(i):
            copy.wait()
        share = dot(rows[i].reshape(local * depth, tokens_all), ups[i])
        if came is not None:
            share += added[i].astype(F32)
        shares[i] = share.astype(shares.dtype)
        out_copy(i).start()
    for i in range(2):
        out_copy(i).wait()


def out_share(step, places, turned_act, upstream_all, came, cost, last=False):
    local, hidden, tokens_all = turned_act.shape
    half = upstream_all.shape[1] // 2
    depth = hidden // lax.axis_size("dp")
    kind = F32 if last else BF16
    return pl.pallas_call(
        functools.partial(out_kernel, step),
        out_shape=[jax.ShapeDtypeStruct((local * depth, half), kind)] * 2,
        in_specs=[SMEM_SPEC] + [ANY_SPEC] * (2 + len(came)),
        out_specs=[ANY_SPEC] * 2,
        scratch_shapes=[
            pltpu.VMEM((2, local, depth, tokens_all), BF16),
            pltpu.VMEM((2, tokens_all, half), BF16),
            pltpu.VMEM((2, local * depth, half), BF16),
            pltpu.VMEM((2, local * depth, half), kind),
        ]
        + [pltpu.SemaphoreType.DMA((2,))] * 4,
        compiler_params=pltpu.CompilerParams(vmem_limit_bytes=58 * 2**20),
        cost_estimate=pl.CostEstimate(flops=cost, bytes_accessed=1024, transcendentals=0),
        name="out_share",
    )(places, turned_act, upstream_all, *came)


def owner_grads_kernel(upstream, weight, out):
    out[0] = dot(upstream[...], weight[0], NT).astype(BF16)


def owner_grads(upstream, weight):
    local, hidden, width = weight.shape
    rows = upstream.shape[0]
    return pl.pallas_call(
        owner_grads_kernel,
        out_shape=jax.ShapeDtypeStruct((local, rows, hidden), BF16),
        grid=(local,),
        in_specs=[
            pl.BlockSpec(upstream.shape, lambda i: (0, 0)),
            pl.BlockSpec((1, hidden, width), lambda i: (i, 0, 0)),
        ],
        out_specs=pl.BlockSpec((1, rows, hidden), lambda i: (i, 0, 0)),
        compiler_params=pltpu.CompilerParams(vmem_limit_bytes=58 * 2**20),
        cost_estimate=pl.CostEstimate(
            flops=2 * local * rows * hidden * width, bytes_accessed=16 * 2**20, transcendentals=0
        ),
        name="owner_grads",
    )(upstream, weight)


def expert_kernel(later, both_scalars, rows_a, rows_b, grad_plain, weight, *refs):
    scalars = [both_scalars[int(later), i] for i in range(3)]
    refs = refs[5 if later else 0 :]
    outs, bufs, (weights, plains, weight_sems, plain_sems, out_sems) = refs[:5], refs[5:10], refs[10:]
    activated, turned_act, grad_pre, gate_grad, turned_rows = bufs
    local, width = weights.shape[:2]
    count = rows_a.shape[0]
    half = pl.ds(pl.multiple_of(scalars[1] * 2 * count, 2 * count), 2 * count)

    def weight_copy(e):
        return pltpu.make_async_copy(weight.at[e], weights.at[e], weight_sems.at[e])

    def plain_copy(e):
        return pltpu.make_async_copy(grad_plain.at[e, half], plains.at[e], plain_sems.at[e])

    def out_copies(e):
        return [
            pltpu.make_async_copy(activated.at[e], outs[0].at[e, half], out_sems.at[0, e]),
            pltpu.make_async_copy(turned_act.at[e], outs[1].at[e, :, half], out_sems.at[1, e]),
            pltpu.make_async_copy(grad_pre.at[e], outs[2].at[e, half], out_sems.at[2, e]),
        ]

    rows_copy = pltpu.make_async_copy(turned_rows, outs[4].at[:, half], out_sems.at[3, 0])
    gate_copy = pltpu.make_async_copy(gate_grad, outs[3].at[half], out_sems.at[3, 1])
    for e in range(2):
        weight_copy(e).start()
        plain_copy(e).start()
    both = (rows_a, rows_b)
    starts = [pl.multiple_of(scalars[2] * count, count), pl.multiple_of((1 - scalars[2]) * count, count)]
    gate_grad[...] = jnp.zeros_like(gate_grad)
    for start, rows in zip(starts, both):
        turned_rows[:, pl.ds(start, count)] = rows[:, :width].T
    rows_copy.start()
    lanes = lax.broadcasted_iota(jnp.int32, (count, LANES), 1)
    tile = 2 * LANES

    @pl.loop(0, local)
    def _(e):
        here = lanes == scalars[0] + e

        @pl.when(e + 2 < local)
        def _():
            weight_copy(e + 2).start()
            plain_copy(e + 2).start()

        weight_copy(e).wait()
        plain_copy(e).wait()
        gates = [
            jnp.sum(jnp.where(here, rows[:, width:].astype(F32), 0.0), axis=1, keepdims=True)
            for rows in both
        ]
        x = jnp.concatenate([rows[:, :width] for rows in both], axis=0)
        sums = [0.0, 0.0]
        for f in range(0, FE, tile):
            g_both = dot(x, weights[e, :, f : f + tile])
            u_both = dot(x, weights[e, :, FE + f : FE + f + tile])
            for i in range(2):
                at = pl.ds(starts[i], count)
                part = slice(i * count, (i + 1) * count)
                g, u, gate = g_both[part], u_both[part], gates[i]
                s = jax.nn.sigmoid(g)
                silu = g * s
                act = silu * u
                plain = plains[e, at, f : f + tile].astype(F32)
                sums[i] += jnp.sum(act * plain, axis=1, keepdims=True)
                low = (act * gate).astype(BF16)
                activated[e, at, f : f + tile] = low
                turned_act[e, f : f + tile, at] = low.T
                da = plain * gate
                grad_pre[e, at, f : f + tile] = (da * u * s * (1.0 + g * (1.0 - s))).astype(BF16)
                grad_pre[e, at, FE + f : FE + f + tile] = (da * silu).astype(BF16)
        for copy in out_copies(e):
            copy.start()
        for i in range(2):
            gate_grad[pl.ds(starts[i], count), :] += jnp.where(here, sums[i], 0.0)

    gate_copy.start()
    rows_copy.wait()
    gate_copy.wait()

    @pl.loop(0, local)
    def _(e):
        for copy in out_copies(e):
            copy.wait()


def expert_half(scalars, rows_a, rows_b, grad_plain, weight, earlier):
    count = 2 * rows_a.shape[0]
    local, width, wide = weight.shape
    total = 2 * count
    out_shape = [
        jax.ShapeDtypeStruct((local, total, FE), BF16),
        jax.ShapeDtypeStruct((local, FE, total), BF16),
        jax.ShapeDtypeStruct((local, total, wide), BF16),
        jax.ShapeDtypeStruct((total, LANES), F32),
        jax.ShapeDtypeStruct((width, total), BF16),
    ]
    return pl.pallas_call(
        functools.partial(expert_kernel, bool(earlier)),
        out_shape=out_shape,
        in_specs=[SMEM_SPEC, VMEM_SPEC, VMEM_SPEC, ANY_SPEC, ANY_SPEC] + [ANY_SPEC] * len(earlier),
        out_specs=[ANY_SPEC] * 5,
        scratch_shapes=[
            pltpu.VMEM((local, count, FE), BF16),
            pltpu.VMEM((local, FE, count), BF16),
            pltpu.VMEM((local, count, wide), BF16),
            pltpu.VMEM((count, LANES), F32),
            pltpu.VMEM((width, count), BF16),
            pltpu.VMEM(weight.shape, BF16),
            pltpu.VMEM((local, count, FE), BF16),
            pltpu.SemaphoreType.DMA((local,)),
            pltpu.SemaphoreType.DMA((local,)),
            pltpu.SemaphoreType.DMA((4, max(local, 2))),
        ],
        input_output_aliases={5 + k: k for k in range(len(earlier))},
        compiler_params=pltpu.CompilerParams(vmem_limit_bytes=58 * 2**20),
        cost_estimate=pl.CostEstimate(
            flops=2 * local * count * width * wide, bytes_accessed=30 * 2**20, transcendentals=0
        ),
        name="expert_half",
    )(scalars, rows_a, rows_b, grad_plain, weight, *earlier)


def on_device(
    tokens,
    cotangent,
    routes,
    segments,
    w_qkv,
    w_out,
    router,
    gain_attn,
    gain_mlp,
    expert_in,
    expert_out,
):
    net = Net()
    length, width = tokens.shape
    local_count = expert_in.shape[0]
    experts_all = local_count * net.ne
    wide_qkv = w_qkv.shape[1]

    small = jnp.concatenate([router, gain_attn[:, None], gain_mlp[:, None]], axis=1)
    small = jnp.pad(small, ((0, 0), (0, LANES - small.shape[1])))
    first_block = jnp.concatenate([w_qkv, small], axis=1)
    upstream_all = lax.all_gather(cotangent, "expert", axis=0, tiled=True)
    grad_act_plain = owner_grads(upstream_all, expert_out)
    qkv_weight, out_weight = gather_weights(net, first_block, w_out, grad_act_plain)
    gain_row = experts_all % 8

    cos, sin = rope_tables(length)
    places_row = jnp.arange(length)
    bias = (
        (places_row[:, None] <= places_row[None, :])
        & (segments[0][:, None] == segments[0][None, :])
    ).astype(F32)
    normed, turned_both, queries, key_rows, values, mixed_heads, gains, small_full = attend(
        experts_all, tokens, bias, cos, sin, qkv_weight
    )
    hidden_state, sent, gate_float = branch(
        gain_row + 1, tokens, mixed_heads, out_weight, small_full, gains, routes
    )
    across_rows = net.swap(sent, WIDE)
    own_rows, beside_rows = sent, net.swap(sent, CORE)
    core, wide = net.e % 2, net.e // 2
    first_expert = net.e * local_count
    scalars = jnp.stack([first_expert, wide, core, first_expert, 1 - wide, core])
    scalars = scalars.reshape(2, 3).astype(jnp.int32)
    early = expert_half(scalars, own_rows, beside_rows, grad_act_plain, expert_in, ())
    across_rows = after(across_rows, early)
    corner_rows = net.swap(across_rows, CORE)
    activated, turned_act, grad_pre, gate_grads, turned_rows = expert_half(
        scalars, across_rows, corner_rows, grad_act_plain, expert_in, early
    )

    steps = jnp.arange(net.nd, dtype=jnp.int32)
    ways = jnp.stack([net.r - 1 - steps, net.r + 1 + steps], axis=1)
    places = jnp.where(steps[:, None] < net.nd - 1, net.dp_of(ways), net.p).astype(jnp.int32)

    def cost(s):
        return 10**10 if s == 4 else 3 * 10**10

    def advance(shares):
        return [net.step(shares[0], 1), net.step(shares[1], -1)]

    came_in, came_out = (), ()

    def ring_in(s, *earlier, beside=None):
        nonlocal came_in
        if earlier:
            came_in = after(came_in, *earlier)
        shares = in_share(s, places, turned_rows, grad_pre, came_in, cost(s))
        if beside is not None:
            shares = after(shares, beside)
        came_in = advance(shares)
        return shares

    def ring_out(s, *earlier, beside=None):
        nonlocal came_out
        if earlier:
            came_out = after(came_out, *earlier)
        shares = out_share(s, places, turned_act, upstream_all, came_out, cost(s))
        if beside is not None:
            shares = after(shares, beside)
        came_out = advance(shares)
        return shares

    def devices(*bits):
        return jnp.stack([net.e ^ bit for bit in bits])

    sent_in = ring_in(0)
    sent_out = ring_out(0, sent_in)
    block = width // net.devices
    lefts = turned_both.reshape(2, net.nd, net.ne, block, length).transpose(2, 0, 1, 3, 4)
    lefts = lax.all_to_all(
        lefts.reshape(net.ne, -1, length), "expert", 0, 0, tiled=True
    )
    beside, kept = owner_rows(
        devices(1, 3, 0, 2), after(grad_pre, sent_out, lefts), expert_in, gate_grads
    )
    beside_came = net.swap(beside, CORE)
    sent_in = ring_in(1, kept, beside=beside_came)
    both = (kept.astype(F32) + after(beside_came, sent_in).astype(F32)).astype(BF16)
    both = both.reshape(2, length, -1)
    both = jnp.where(wide == 0, both, both[::-1])
    came = net.exchange(both, 1)
    sent_out = ring_out(1, both)
    (mix,) = owner_rows(jnp.arange(4), after(activated, sent_out), expert_out)
    sent_out = mix
    grad_hidden, pack, grad_mixed = middle(
        experts_all,
        gain_row + 1,
        out_weight,
        after(came, sent_out),
        cotangent,
        hidden_state,
        gate_float,
        gains,
        small_full,
    )
    packs = net.exchange(pack, 1)
    sent_in = ring_in(2, grad_mixed)
    sent_out = ring_out(2, sent_in)
    grad_project = attend_back(
        queries, key_rows, values, after(grad_mixed, sent_out), bias, cos, sin
    )
    projects = net.exchange(grad_project, 1)
    sent_out = ring_out(3, grad_project)
    packs = after(packs, sent_out, came_in)
    packs = (packs, net.swap(packs, CORE))
    sent_in = ring_in(3, sent_out, packs[0], beside=packs[1])
    mine = lambda rows: lax.dynamic_index_in_dim(
        rows.reshape(net.nd, net.ne, block, -1), net.e, 1, keepdims=False
    ).reshape(net.nd * block, -1)
    normed_two = mine(turned_rows).reshape(-1, net.ne, length).transpose(1, 0, 2)
    place = net.e.astype(jnp.int32).reshape(1)
    out_products = weight_products(
        place,
        after(lefts, sent_in),
        packs,
        normed_two,
        mine(gain_column(experts_all, packs)),
    )
    sent_out = ring_out(4, out_products)
    projects = after(projects, sent_out, came_in)
    projects = (projects, net.swap(projects, CORE))
    sent_in = ring_in(4, projects[0], beside=projects[1])
    products = weight_products(place, after(lefts, sent_in), projects, out_products)
    sent_out = ring_out(5, products)
    d_all = lax.psum_scatter(after(products, sent_out), "dp", scatter_dimension=0, tiled=True)
    sent_in = ring_in(5, sent_out)
    mix_all = lax.all_to_all(after(mix, sent_in), "expert", 0, 0, tiled=True)
    for s in range(6, net.nd - 1):
        sent_out = ring_out(s, sent_in)
        sent_in = ring_in(s, sent_out)
    grad_tokens = input_back(
        gain_row, qkv_weight, tokens, after(grad_project, sent_in), gains, grad_hidden
    )
    mixture = jnp.sum(mix_all.reshape(net.ne, length, width).astype(F32), axis=0)
    activations = (hidden_state + mixture).astype(BF16)
    d_expert_out = jnp.concatenate(
        out_share(
            net.nd - 1, places, turned_act, upstream_all, after(came_out, grad_tokens), cost(net.nd), last=True
        ),
        axis=1,
    ).reshape(local_count, FE // net.nd, width)
    (d_expert_in,) = in_share(
        net.nd - 1, places, turned_rows, grad_pre, after(came_in, d_expert_out, activations), cost(net.nd), last=True
    )
    d_qkv, d_out, d_small = finish(after(d_all, d_expert_in), w_qkv)
    d_gain_first = d_small[:, LANES - 1] / gain_attn.astype(F32)
    return (
        activations,
        grad_tokens,
        d_qkv,
        d_out,
        d_small[:, :experts_all],
        d_gain_first,
        d_small[:, experts_all],
        d_expert_in,
        d_expert_out,
    )


def solution(mesh):
    rows = P(AXES, None)
    return jax.shard_map(
        on_device,
        mesh=mesh,
        in_specs=(rows,) * 7
        + (P(AXES), P(AXES), P("expert", None, None), P("expert", None, None)),
        out_specs=(rows,) * 5
        + (P(AXES), P(AXES), P("expert", "dp", None), P("expert", "dp", None)),
        check_vma=False,
    )
```
